512 devices in a mesh: blk: 128 (over z, y, core), pair: 4 (over x).
Axes of the slice: x: 4, y: 8, z: 8, core: 2. Of those that a mesh axis runs over, the one named last changes fastest.
Arguments:
- features: bfloat16 [557, 786432], P(None, ('blk', 'pair')), may hold values from -6 to 6
- daylit_list: int32 [786432], P(('blk', 'pair')), may hold values from 0 to 1535, as said below
- daylit_count: int32 [512], P(('blk', 'pair')), may hold values from 0 to 1536
- in_weight: bfloat16 [557, 512], replicated, may hold values from -0.25 to 0.25
- in_bias: float32 [512], replicated, may hold values from -3 to 3
- mid_weight: bfloat16 [2, 512, 512], replicated, may hold values from -0.25 to 0.25
- mid_bias: float32 [2, 512], replicated, may hold values from -3 to 3
- out_weight: bfloat16 [368, 512], replicated, may hold values from -0.25 to 0.25
- out_bias: float32 [368], replicated, may hold values from -3 to 3
Outputs:
- heating: bfloat16 [368, 786432], P(None, ('blk', 'pair'))
The draws below stay inside these ranges and needn't reach their ends.
Inputs may be any that keep to these rules, and one draw needn't show every extreme that they name: `daylit_list`: the first daylit_count[d] of block d's 1536 entries are the local indices of its daylit columns in increasing order; the remaining entries are 0. The column with local index j of block (blk, pair) and the one with the same j of block (blk, (pair + 2) mod 4) lie half a globe apart, and exactly one of the two is daylit.
All inputs are finite; a program needn't handle non-finite values.
Results may differ from the reference program's by a relative error of at most 0.0052.
Values may be sent and summed in bfloat16 or wider, within the bound.
A program may use at most 64 MiB of HBM per device.

```python
import jax
import jax.numpy as jnp
from jax import lax

FEAT = 557
HID = 512
OUT = 368
MID = 2
COLS_DEV = 1536
NCOL = 786432
N_BLK = 128
N_PAIR = 4


def daylight_table(key):
    level_key, bit_key = jax.random.split(key)
    levels = jax.random.randint(level_key, (N_BLK, N_PAIR // 2), 2, 7)
    strong = jax.random.randint(jax.random.fold_in(level_key, 1), (N_BLK,), 6, 9)
    levels = levels.at[:, 0].set(strong)
    levels = levels.at[0, 0].set(8)
    samples = jax.random.randint(bit_key, (N_BLK, N_PAIR // 2, COLS_DEV), 0, 8)
    daylit_near = (samples < levels[:, :, None]).astype(jnp.int32)
    daylight = jnp.concatenate([daylit_near, 1 - daylit_near], axis=1)
    return daylight.reshape(N_BLK * N_PAIR, COLS_DEV)


def draw_daylit_list(key, part):
    daylight = daylight_table(key)
    ranking = jnp.argsort(1 - daylight, axis=1, stable=True).astype(jnp.int32)
    counts = jnp.sum(daylight, axis=1).astype(jnp.int32)
    positions = jnp.arange(COLS_DEV, dtype=jnp.int32)[None, :]
    listed = jnp.where(positions < counts[:, None], ranking, 0)
    return listed.reshape(-1).astype(jnp.int32)


def draw_daylit_count(key, part):
    daylight = daylight_table(key)
    return jnp.sum(daylight, axis=1).astype(jnp.int32)


def shard_levels(key, shape, shards, smallest, largest):
    loudness, own = 1.0, jax.random.fold_in(key, 6)
    for position, blocks in shards:
        heights = jnp.exp(jax.random.uniform(jax.random.fold_in(own, position), (blocks,), jnp.float32, smallest / len(shards), largest / len(shards)))
        loudness = loudness * jnp.repeat(heights, shape[position] // blocks).reshape([-1 if axis == position else 1 for axis in range(len(shape))])
    return loudness


def centred(stream_key, extent, spread, limit, pieces=(), held_as=jnp.bfloat16):
    loudness = shard_levels(stream_key, extent, pieces, -0.22, 0.18) if pieces else 1.0
    values = jax.random.normal(stream_key, extent, jnp.float32) * spread * loudness
    return jnp.minimum(jnp.maximum(values, -limit), limit).astype(held_as)


def setup_inputs(seed: int = 0) -> dict:
    arg_keys = jax.random.split(jax.random.key(seed), 10)
    features = centred(arg_keys[0], (FEAT, NCOL), 1.0, 6.0, ((1, 512),))
    daylit_list = draw_daylit_list(jax.random.fold_in(arg_keys[9], 71), 0)
    daylit_count = draw_daylit_count(jax.random.fold_in(arg_keys[9], 71), 0)
    in_weight = centred(arg_keys[3], (FEAT, HID), FEAT ** -0.5, 0.25)
    in_bias = centred(arg_keys[4], (HID,), 0.5, 3.0, (), jnp.float32)
    mid_weight = centred(arg_keys[5], (MID, HID, HID), HID ** -0.5, 0.25)
    mid_bias = centred(arg_keys[6], (MID, HID), 0.5, 3.0, (), jnp.float32)
    out_weight = centred(arg_keys[7], (OUT, HID), HID ** -0.5, 0.25)
    out_bias = centred(arg_keys[8], (OUT,), 0.5, 3.0, (), jnp.float32)
    return dict(features=features, daylit_list=daylit_list, daylit_count=daylit_count, in_weight=in_weight, in_bias=in_bias, mid_weight=mid_weight, mid_bias=mid_bias, out_weight=out_weight, out_bias=out_bias)


def leaky_unit(values):
    return jnp.where(values > 0, values, 0.15 * values)


def network(columns, in_weight, in_bias, mid_weight, mid_bias, out_weight, out_bias):
    hidden = lax.dot_general(in_weight, columns, (((0,), (0,)), ((), ())), preferred_element_type=jnp.float32)
    hidden = leaky_unit(hidden + in_bias[:, None]).astype(jnp.bfloat16)
    for layer_index in range(mid_weight.shape[0]):
        hidden = jnp.dot(mid_weight[layer_index], hidden, preferred_element_type=jnp.float32)
        hidden = leaky_unit(hidden + mid_bias[layer_index][:, None]).astype(jnp.bfloat16)
    return jnp.dot(out_weight, hidden, preferred_element_type=jnp.float32) + out_bias[:, None]


def reference(features, daylit_list, daylit_count, in_weight, in_bias, mid_weight, mid_bias, out_weight, out_bias):
    devices = N_BLK * N_PAIR
    entries = daylit_list.reshape(devices, COLS_DEV)
    positions = jnp.arange(COLS_DEV, dtype=jnp.int32)[None, :]
    owners = jnp.arange(devices, dtype=jnp.int32)[:, None] * COLS_DEV
    targets = jnp.where(positions < daylit_count[:, None], entries + owners, devices * COLS_DEV).astype(jnp.int32)
    daylit = jnp.zeros((devices * COLS_DEV,), jnp.int32).at[targets.reshape(-1)].set(1, mode="drop")
    daylit = daylit.reshape(N_BLK, N_PAIR, COLS_DEV)
    half_pair = N_PAIR // 2

    def one_block(block_index):
        block_cols = lax.dynamic_slice_in_dim(features, block_index * (N_PAIR * COLS_DEV), N_PAIR * COLS_DEV, 1)
        block_cols = block_cols.reshape(FEAT, N_PAIR, COLS_DEV)
        day_flags = lax.dynamic_index_in_dim(daylit, block_index, 0, keepdims=False)[:half_pair]
        chosen = jnp.where(day_flags[None] > 0, block_cols[:, :half_pair], block_cols[:, half_pair:])
        result = network(chosen.reshape(FEAT, half_pair * COLS_DEV), in_weight, in_bias, mid_weight, mid_bias, out_weight, out_bias)
        result = result.reshape(OUT, half_pair, COLS_DEV)
        weights = day_flags.astype(jnp.float32)[None]
        return jnp.concatenate([result * weights, result * (1.0 - weights)], axis=1).astype(jnp.bfloat16)

    blocks = lax.map(one_block, jnp.arange(N_BLK, dtype=jnp.int32))
    peer_cols = COLS_DEV // (N_PAIR * N_BLK)
    blocks = blocks.reshape(N_BLK, OUT, N_PAIR, N_PAIR, N_BLK, peer_cols)
    return jnp.transpose(blocks, (1, 4, 3, 2, 0, 5)).reshape(OUT, N_BLK * N_PAIR * COLS_DEV)
```

```python
import jax
import jax.numpy as jnp
from jax import lax
from jax.experimental import pallas as pl
from jax.experimental.pallas import tpu as pltpu
from jax.sharding import PartitionSpec as P

FEAT, HID, OUT = 557, 512, 368
LANES = 384
NX, NZ, NY, NC, NK = 4, 8, 8, 2, 3
BLOCK = NZ * NY * NC * NK
ROWS = NZ * NY
COLS = NX * BLOCK
OFFSETS = (1, 3, 2, 0)
RING = (4, 3, 5, 2, 6, 1, 7)
BF16, F32 = jnp.bfloat16, jnp.float32
MESH = pl.DeviceIdType.MESH


def nt(a, b):
    return lax.dot_general(a, b, (((1,), (1,)), ((), ())), preferred_element_type=F32)


def leaky(t):
    return jnp.maximum(t, 0.15 * t)


def selector(rows, cols, column_of_row):
    r = lax.broadcasted_iota(jnp.int32, (rows, cols), 0)
    c = lax.broadcasted_iota(jnp.int32, (rows, cols), 1)
    return jnp.where(c == column_of_row(r), 1.0, 0.0).astype(BF16)


def kernel(
    count_ref, list_ref, bias_ref, feat_ref, w0_ref, wm_ref, wo_ref, out_ref,
    f_v, w0_v, wm_v, wo_v, day_v, sx, rx, zs, zr, ys, yr, o_v,
    load_sem, sx_sem, rx_sem, zs_sem, zr_sem, ys_sem, yr_sem, o_sem,
):
    x = lax.axis_index("pair")
    blk = lax.axis_index("blk")
    z, y, c = blk // (NY * NC), (blk // NC) % NY, blk % NC

    def blk_of(zz, yy, cc):
        return (zz * NY + yy) * NC + cc

    sectors = [lax.rem(x + off, NX) for off in OFFSETS]

    loads = [
        pltpu.make_async_copy(
            feat_ref.at[:, pl.ds(pl.multiple_of(a * BLOCK, 128), BLOCK)], f_v.at[i], load_sem.at[i]
        )
        for i, a in enumerate(sectors)
    ]
    load_w0 = pltpu.make_async_copy(w0_ref, w0_v, load_sem.at[4])
    load_wm = pltpu.make_async_copy(wm_ref, wm_v, load_sem.at[5])
    load_wo = pltpu.make_async_copy(wo_ref, wo_v.at[pl.ds(0, OUT)], load_sem.at[6])
    for load in (loads[0], load_w0, load_wm, load_wo, *loads[1:]):
        load.start()

    barrier = pltpu.get_barrier_semaphore()
    peers = []
    for a in sectors:
        peers.append((blk_of(z, y, 1 - c), a))
    for a in sectors[:3]:
        peers.append((blk, a))
    for d in RING:
        peers.append((blk_of(lax.rem(z + d, NZ), y, c), x))
    for d in RING:
        peers.append((blk_of(z, lax.rem(y + d, NY), c), x))
    for peer in peers:
        pl.semaphore_signal(barrier, inc=1, device_id=peer, device_id_type=MESH)

    group = selector(BLOCK, BLOCK, lambda r: (r & (ROWS - 1)) * (NC * NK) + (r >> 6))
    turn = selector(128, 128, lambda r: (r & 15) * 8 + (r >> 4))
    place = selector(
        BLOCK,
        BLOCK,
        lambda r: (((r >> 1) & 7) * 16 + ((r >> 4) & 7) * 2 + (r & 1)) * NK + (r >> 7),
    )
    eye = selector(LANES, LANES, lambda r: r)

    entries = list_ref[...]
    usable = lax.broadcasted_iota(jnp.int32, (1, COLS), 1) < count_ref[0]
    high = jnp.where(usable, entries >> 7, -1)
    high = jnp.broadcast_to(high, (16, COLS)) == lax.broadcasted_iota(jnp.int32, (16, COLS), 0)
    low = jnp.broadcast_to(entries & 127, (128, COLS)) == lax.broadcasted_iota(
        jnp.int32, (128, COLS), 0
    )
    day_v[...] = nt(
        jnp.where(high, 1.0, 0.0).astype(BF16), jnp.where(low, 1.0, 0.0).astype(BF16)
    )
    wo_v[pl.ds(OUT, LANES - OUT), :] = jnp.zeros((LANES - OUT, HID), BF16)
    first_half = jnp.where(x < NX // 2, 1.0, 0.0)
    lane = lax.broadcasted_iota(jnp.int32, (BLOCK, LANES), 1)

    def compute(i):
        day = jnp.concatenate(
            [day_v[pl.ds(sectors[i] * 3 + t, 1), :] for t in range(3)], axis=1
        )
        day = jnp.where(day > 0.5, 1.0, 0.0)
        day = nt(group, jnp.broadcast_to(day, (128, BLOCK)).astype(BF16))
        day = jnp.concatenate([day, day, day], axis=1)
        cols = nt(group, f_v[i]).astype(BF16)
        if i == 0:
            load_w0.wait()
        h = jnp.dot(cols, w0_v[...], preferred_element_type=F32)
        h = leaky(h + bias_ref[pl.ds(0, 1), :]).astype(BF16)
        if i == 0:
            load_wm.wait()
        for layer in range(2):
            h = leaky(nt(h, wm_v[layer]) + bias_ref[pl.ds(1 + layer, 1), :]).astype(BF16)
        if i == 0:
            load_wo.wait()
        v = nt(h, wo_v[...]) + bias_ref[pl.ds(3, 1), pl.ds(0, LANES)]
        v = jnp.where(lane == OUT, first_half, v) * day
        sx[i] = v.astype(BF16)

    def send_x(i):
        half = i // 2
        for k in range(NK):
            for cc in range(NC) if i < 3 else (1 - c,):
                pltpu.make_async_remote_copy(
                    src_ref=sx.at[i, pl.ds(pl.multiple_of((cc * NK + k) * ROWS, ROWS), ROWS)],
                    dst_ref=rx.at[half, k, 2 * (i % 2) + c],
                    send_sem=sx_sem.at[0],
                    recv_sem=rx_sem.at[half, k],
                    device_id=(blk_of(z, y, cc), sectors[i]),
                    device_id_type=MESH,
                ).start()

    def wait_for(view, sem):
        pltpu.make_async_copy(view, view, sem).wait()

    for i in range(4):
        loads[i].wait()
        compute(i)
        if i == 0:
            pl.semaphore_wait(barrier, len(peers))
        send_x(i)
    for k in range(NK):
        rx[1, k, pl.ds(2 + c, 1)] = sx[
            3, pl.ds(pl.multiple_of((c * NK + k) * ROWS, ROWS), ROWS)
        ][None]

    def stage_x(half, k):
        wait_for(rx.at[half, k, pl.ds(0, 4 - half)], rx_sem.at[half, k])
        parts = [
            (rx[half, k, cc].astype(F32) + rx[half, k, 2 + cc].astype(F32)).reshape(NZ, NY, LANES)
            for cc in range(NC)
        ]
        zs[half, k] = jnp.concatenate(parts, axis=1).astype(BF16)
        for d in RING:
            zz = lax.rem(z + d, NZ)
            pltpu.make_async_remote_copy(
                src_ref=zs.at[half, k, zz],
                dst_ref=zr.at[half, k, z],
                send_sem=zs_sem.at[0],
                recv_sem=zr_sem.at[half, k],
                device_id=(blk_of(zz, y, c), x),
                device_id_type=MESH,
            ).start()
        zr[half, k, pl.ds(z, 1)] = zs[half, k, pl.ds(z, 1)]

    def stage_z(half, k):
        wait_for(zr.at[half, k, pl.ds(0, NZ - 1)], zr_sem.at[half, k])
        turned = jnp.dot(turn, zr[half, k].reshape(128, LANES), preferred_element_type=F32)
        ys[half, k] = turned.astype(BF16).reshape(NY, 16, LANES)
        for d in RING:
            yy = lax.rem(y + d, NY)
            pltpu.make_async_remote_copy(
                src_ref=ys.at[half, k, yy],
                dst_ref=yr.at[half, k, y],
                send_sem=ys_sem.at[0],
                recv_sem=yr_sem.at[half, k],
                device_id=(blk_of(z, yy, c), x),
                device_id_type=MESH,
            ).start()
        yr[half, k, pl.ds(y, 1)] = ys[half, k, pl.ds(y, 1)]

    outs = []

    def stage_y(half):
        for k in range(NK):
            wait_for(yr.at[half, k, pl.ds(0, NY - 1)], yr_sem.at[half, k])
        rows = yr[half].reshape(BLOCK, LANES)
        turned = nt(eye, rows).astype(BF16)
        result = jnp.dot(turned, place, preferred_element_type=F32)
        flag = result[OUT : OUT + 1, :]
        near = lax.rem(x + 1 + half, 2)
        for far, weight in enumerate((flag, 1.0 - flag)):
            slot = 2 * half + far
            o_v[slot] = (result[:OUT] * weight).astype(BF16)
            start = pl.multiple_of((near + 2 * far) * BLOCK, 128)
            copy = pltpu.make_async_copy(
                o_v.at[slot], out_ref.at[:, pl.ds(start, BLOCK)], o_sem.at[slot]
            )
            copy.start()
            outs.append(copy)

    chunks = [(half, k) for half in range(2) for k in range(NK)]
    for t in range(len(chunks) + 1):
        if t < len(chunks):
            stage_x(*chunks[t])
        if t >= 1:
            stage_z(*chunks[t - 1])
        if t == 5:
            stage_y(0)
    stage_y(1)

    wait_for(sx.at[pl.ds(0, 3)], sx_sem.at[0])
    wait_for(sx.at[3, pl.ds(0, BLOCK // 2)], sx_sem.at[0])
    wait_for(zs.at[:, :, pl.ds(0, NZ - 1)], zs_sem.at[0])
    wait_for(ys.at[:, :, pl.ds(0, NY - 1)], ys_sem.at[0])
    for copy in outs:
        copy.wait()


def shards(
    features, daylit_list, daylit_count, in_weight, in_bias, mid_weight, mid_bias, out_weight, out_bias
):
    biases = jnp.concatenate(
        [in_bias[None], mid_bias, jnp.pad(out_bias, (0, HID - OUT))[None], jnp.zeros((4, HID), F32)]
    )
    vmem, hbm = pl.BlockSpec(memory_space=pltpu.VMEM), pl.BlockSpec(memory_space=pl.ANY)
    dma = pltpu.SemaphoreType.DMA
    return pl.pallas_call(
        kernel,
        out_shape=jax.ShapeDtypeStruct((OUT, COLS), BF16),
        in_specs=[pl.BlockSpec(memory_space=pltpu.SMEM), vmem, vmem, hbm, hbm, hbm, hbm],
        out_specs=hbm,
        scratch_shapes=[
            pltpu.VMEM((4, FEAT, BLOCK), BF16),
            pltpu.VMEM((FEAT, HID), BF16),
            pltpu.VMEM((2, HID, HID), BF16),
            pltpu.VMEM((LANES, HID), BF16),
            pltpu.VMEM((16, 128), F32),
            pltpu.VMEM((4, BLOCK, LANES), BF16),
            pltpu.VMEM((2, NK, 4, ROWS, LANES), BF16),
            pltpu.VMEM((2, NK, NZ, 16, LANES), BF16),
            pltpu.VMEM((2, NK, NZ, 16, LANES), BF16),
            pltpu.VMEM((2, NK, NY, 16, LANES), BF16),
            pltpu.VMEM((2, NK, NY, 16, LANES), BF16),
            pltpu.VMEM((4, OUT, BLOCK), BF16),
            dma((7,)),
            dma((1,)),
            dma((2, NK)),
            dma((1,)),
            dma((2, NK)),
            dma((1,)),
            dma((2, NK)),
            dma((4,)),
        ],
        compiler_params=pltpu.CompilerParams(
            collective_id=0, has_side_effects=True, vmem_limit_bytes=40 * 1024 * 1024
        ),
        cost_estimate=pl.CostEstimate(
            flops=4_000_000_000, bytes_accessed=5_000_000, transcendentals=0
        ),
    )(
        daylit_count,
        daylit_list.reshape(1, COLS),
        biases,
        features,
        in_weight,
        mid_weight,
        out_weight,
    )


def solution(mesh):
    in_specs = (
        P(None, ("blk", "pair")),
        P(("blk", "pair")),
        P(("blk", "pair")),
        P(),
        P(),
        P(),
        P(),
        P(),
        P(),
    )
    out_specs = P(None, ("blk", "pair"))
    return jax.shard_map(shards, mesh=mesh, in_specs=in_specs, out_specs=out_specs, check_vma=False)
```

```python
import jax
import jax.numpy as jnp
from jax import lax
from jax.experimental import pallas as pl
from jax.experimental.pallas import tpu as pltpu
from jax.sharding import PartitionSpec as P

FEAT, HID, OUT = 557, 512, 368
LANES = 384
NX, NZ, NY, NC, NK = 4, 8, 8, 2, 3
BLOCK = NZ * NY * NC * NK
ROWS = NZ * NY
COLS = NX * BLOCK
OFFSETS = (1, 3, 2, 0)
RING = (4, 3, 5, 2, 6, 1, 7)
BF16, F32 = jnp.bfloat16, jnp.float32
MESH = pl.DeviceIdType.MESH


def nt(a, b):
    return lax.dot_general(a, b, (((1,), (1,)), ((), ())), preferred_element_type=F32)


def leaky(t):
    return jnp.maximum(t, 0.15 * t)


def selector(rows, cols, column_of_row):
    r = lax.broadcasted_iota(jnp.int32, (rows, cols), 0)
    c = lax.broadcasted_iota(jnp.int32, (rows, cols), 1)
    return jnp.where(c == column_of_row(r), 1.0, 0.0).astype(BF16)


def kernel(
    count_ref, list_ref, feat_ref, w0_ref, b0_ref, wm_ref, bm_ref, wo_ref, bo_ref, out_ref,
    list_v, f_v, w0_v, b0_v, wm_v, bm_v, wo_v, bo_v, day_v, sx, fx, rx, zs, zr, ys, yr, o_v,
    load_sem, sx_sem, fr_sem, fs_sem, rx_sem, zs_sem, zr_sem, ys_sem, yr_sem, o_sem,
):
    x = lax.axis_index("pair")
    blk = lax.axis_index("blk")
    z, y, c = blk // (NY * NC), (blk // NC) % NY, blk % NC

    def blk_of(zz, yy, cc):
        return (zz * NY + yy) * NC + cc

    sectors = [lax.rem(x + off, NX) for off in OFFSETS]

    loads = [
        pltpu.make_async_copy(
            feat_ref.at[:, pl.ds(pl.multiple_of(a * BLOCK, 128), BLOCK)], f_v.at[i], load_sem.at[i]
        )
        for i, a in enumerate(sectors)
    ]
    load_w0 = pltpu.make_async_copy(w0_ref, w0_v, load_sem.at[4])
    load_wm = pltpu.make_async_copy(wm_ref, wm_v, load_sem.at[5])
    load_wo = pltpu.make_async_copy(wo_ref, wo_v.at[pl.ds(0, OUT)], load_sem.at[6])
    small = [
        pltpu.make_async_copy(src, dst, load_sem.at[7 + n])
        for n, (src, dst) in enumerate(
            ((list_ref, list_v), (b0_ref, b0_v), (bm_ref, bm_v), (bo_ref, bo_v))
        )
    ]
    for load in (*small, loads[0], load_w0, load_wm, load_wo, *loads[1:]):
        load.start()

    barrier = pltpu.get_barrier_semaphore()
    peers = []
    for a in (sectors[0], sectors[1], x):
        peers.append((blk_of(z, y, 1 - c), a))
    for a in sectors[:2]:
        peers.append((blk, a))
    for d in RING:
        peers.append((blk_of(lax.rem(z + d, NZ), y, c), x))
    for d in RING:
        peers.append((blk_of(z, lax.rem(y + d, NY), c), x))
    for peer in peers:
        pl.semaphore_signal(barrier, inc=1, device_id=peer, device_id_type=MESH)

    group = selector(BLOCK, BLOCK, lambda r: (r & (ROWS - 1)) * (NC * NK) + (r >> 6))
    turn = selector(128, 128, lambda r: (r & 15) * 8 + (r >> 4))
    place = selector(
        BLOCK,
        BLOCK,
        lambda r: (((r >> 1) & 7) * 16 + ((r >> 4) & 7) * 2 + (r & 1)) * NK + (r >> 7),
    )
    eye = selector(LANES, LANES, lambda r: r)

    for load in small:
        load.wait()
    entries = list_v[...].reshape(1, COLS)
    usable = lax.broadcasted_iota(jnp.int32, (1, COLS), 1) < count_ref[0]
    high = jnp.where(usable, entries >> 7, -1)
    high = jnp.broadcast_to(high, (16, COLS)) == lax.broadcasted_iota(jnp.int32, (16, COLS), 0)
    low = jnp.broadcast_to(entries & 127, (128, COLS)) == lax.broadcasted_iota(
        jnp.int32, (128, COLS), 0
    )
    day_v[...] = nt(
        jnp.where(high, 1.0, 0.0).astype(BF16), jnp.where(low, 1.0, 0.0).astype(BF16)
    )
    wo_v[pl.ds(OUT, LANES - OUT), :] = jnp.zeros((LANES - OUT, HID), BF16)
    bias_0 = b0_v[...].reshape(1, HID)
    bias_out = jnp.concatenate([bo_v[...].reshape(1, OUT), jnp.zeros((1, LANES - OUT), F32)], axis=1)
    first_half = jnp.where(x < NX // 2, 1.0, 0.0)
    lane = lax.broadcasted_iota(jnp.int32, (BLOCK, LANES), 1)

    def compute(i):
        day = jnp.concatenate(
            [day_v[pl.ds(sectors[i] * 3 + t, 1), :] for t in range(3)], axis=1
        )
        day = jnp.where(day > 0.5, 1.0, 0.0)
        day = nt(group, jnp.broadcast_to(day, (128, BLOCK)).astype(BF16))
        day = jnp.concatenate([day, day, day], axis=1)
        cols = nt(group, f_v[i]).astype(BF16)
        if i == 0:
            load_w0.wait()
        h = jnp.dot(cols, w0_v[...], preferred_element_type=F32)
        h = leaky(h + bias_0).astype(BF16)
        if i == 0:
            load_wm.wait()
        for layer in range(2):
            h = leaky(nt(h, wm_v[layer]) + bm_v[pl.ds(layer, 1), :]).astype(BF16)
        if i == 0:
            load_wo.wait()
        v = nt(h, wo_v[...]) + bias_out
        v = jnp.where(lane == OUT, first_half, v) * day
        sx[i] = v.astype(BF16)

    def send_x(i):
        half = i // 2
        for k in range(NK):
            for cc in range(NC) if i < 3 else (1 - c,):
                if i == 2:
                    pltpu.make_async_remote_copy(
                        src_ref=sx.at[i, pl.ds((cc * NK + k) * ROWS, ROWS)],
                        dst_ref=fx.at[k, cc],
                        send_sem=sx_sem.at[0],
                        recv_sem=fr_sem.at[k, cc],
                        device_id=(blk, sectors[cc]),
                        device_id_type=MESH,
                    ).start()
                    continue
                pltpu.make_async_remote_copy(
                    src_ref=sx.at[i, pl.ds(pl.multiple_of((cc * NK + k) * ROWS, ROWS), ROWS)],
                    dst_ref=rx.at[half, k, 2 * (i % 2) + c],
                    send_sem=sx_sem.at[0],
                    recv_sem=rx_sem.at[half, k],
                    device_id=(blk_of(z, y, cc), sectors[i]),
                    device_id_type=MESH,
                ).start()

    def wait_for(view, sem):
        pltpu.make_async_copy(view, view, sem).wait()

    def forward(k):
        for cc in range(NC):
            wait_for(fx.at[k, cc], fr_sem.at[k, cc])
            pltpu.make_async_remote_copy(
                src_ref=fx.at[k, cc],
                dst_ref=rx.at[1, k, c],
                send_sem=fs_sem.at[0],
                recv_sem=rx_sem.at[1, k],
                device_id=(blk_of(z, y, cc), sectors[cc]),
                device_id_type=MESH,
            ).start()

    for i in range(4):
        loads[i].wait()
        compute(i)
        if i == 0:
            pl.semaphore_wait(barrier, len(peers))
        send_x(i)
    for k in range(NK):
        rx[1, k, pl.ds(2 + c, 1)] = sx[
            3, pl.ds(pl.multiple_of((c * NK + k) * ROWS, ROWS), ROWS)
        ][None]

    def stage_x(half, k):
        wait_for(rx.at[half, k, pl.ds(0, 4 - half)], rx_sem.at[half, k])
        parts = [
            (rx[half, k, cc].astype(F32) + rx[half, k, 2 + cc].astype(F32)).reshape(NZ, NY, LANES)
            for cc in range(NC)
        ]
        zs[half, k] = jnp.concatenate(parts, axis=1).astype(BF16)
        for d in RING:
            zz = lax.rem(z + d, NZ)
            pltpu.make_async_remote_copy(
                src_ref=zs.at[half, k, zz],
                dst_ref=zr.at[half, k, z],
                send_sem=zs_sem.at[0],
                recv_sem=zr_sem.at[half, k],
                device_id=(blk_of(zz, y, c), x),
                device_id_type=MESH,
            ).start()
        zr[half, k, pl.ds(z, 1)] = zs[half, k, pl.ds(z, 1)]

    def stage_z(half, k):
        wait_for(zr.at[half, k, pl.ds(0, NZ - 1)], zr_sem.at[half, k])
        turned = jnp.dot(turn, zr[half, k].reshape(128, LANES), preferred_element_type=F32)
        ys[half, k] = turned.astype(BF16).reshape(NY, 16, LANES)
        for d in RING:
            yy = lax.rem(y + d, NY)
            pltpu.make_async_remote_copy(
                src_ref=ys.at[half, k, yy],
                dst_ref=yr.at[half, k, y],
                send_sem=ys_sem.at[0],
                recv_sem=yr_sem.at[half, k],
                device_id=(blk_of(z, yy, c), x),
                device_id_type=MESH,
            ).start()
        yr[half, k, pl.ds(y, 1)] = ys[half, k, pl.ds(y, 1)]

    outs = []

    def stage_y(half):
        for k in range(NK):
            wait_for(yr.at[half, k, pl.ds(0, NY - 1)], yr_sem.at[half, k])
        rows = yr[half].reshape(BLOCK, LANES)
        turned = nt(eye, rows).astype(BF16)
        result = jnp.dot(turned, place, preferred_element_type=F32)
        flag = result[OUT : OUT + 1, :]
        near = lax.rem(x + 1 + half, 2)
        for far, weight in enumerate((flag, 1.0 - flag)):
            slot = 2 * half + far
            o_v[slot] = (result[:OUT] * weight).astype(BF16)
            start = pl.multiple_of((near + 2 * far) * BLOCK, 128)
            copy = pltpu.make_async_copy(
                o_v.at[slot], out_ref.at[:, pl.ds(start, BLOCK)], o_sem.at[slot]
            )
            copy.start()
            outs.append(copy)

    chunks = [(half, k) for half in range(2) for k in range(NK)]
    for t in range(len(chunks) + 1):
        if t < len(chunks):
            stage_x(*chunks[t])
        if t < NK:
            forward(t)
        if t >= 1:
            stage_z(*chunks[t - 1])
        if t == 5:
            stage_y(0)
    stage_y(1)

    wait_for(sx.at[pl.ds(0, 3)], sx_sem.at[0])
    wait_for(sx.at[3, pl.ds(0, BLOCK // 2)], sx_sem.at[0])
    wait_for(fx, fs_sem.at[0])
    wait_for(zs.at[:, :, pl.ds(0, NZ - 1)], zs_sem.at[0])
    wait_for(ys.at[:, :, pl.ds(0, NY - 1)], ys_sem.at[0])
    for copy in outs:
        copy.wait()


def shards(
    features, daylit_list, daylit_count, in_weight, in_bias, mid_weight, mid_bias, out_weight, out_bias
):
    hbm = pl.BlockSpec(memory_space=pltpu.HBM)
    dma = pltpu.SemaphoreType.DMA
    return pl.pallas_call(
        kernel,
        out_shape=jax.ShapeDtypeStruct((OUT, COLS), BF16),
        in_specs=[pl.BlockSpec(memory_space=pltpu.SMEM)] + [hbm] * 8,
        out_specs=hbm,
        scratch_shapes=[
            pltpu.VMEM((COLS,), jnp.int32),
            pltpu.VMEM((4, FEAT, BLOCK), BF16),
            pltpu.VMEM((FEAT, HID), BF16),
            pltpu.VMEM((HID,), F32),
            pltpu.VMEM((2, HID, HID), BF16),
            pltpu.VMEM((2, HID), F32),
            pltpu.VMEM((LANES, HID), BF16),
            pltpu.VMEM((OUT,), F32),
            pltpu.VMEM((16, 128), F32),
            pltpu.VMEM((4, BLOCK, LANES), BF16),
            pltpu.VMEM((NK, NC, ROWS, LANES), BF16),
            pltpu.VMEM((2, NK, 4, ROWS, LANES), BF16),
            pltpu.VMEM((2, NK, NZ, 16, LANES), BF16),
            pltpu.VMEM((2, NK, NZ, 16, LANES), BF16),
            pltpu.VMEM((2, NK, NY, 16, LANES), BF16),
            pltpu.VMEM((2, NK, NY, 16, LANES), BF16),
            pltpu.VMEM((4, OUT, BLOCK), BF16),
            dma((11,)),
            dma((1,)),
            dma((NK, NC)),
            dma((1,)),
            dma((2, NK)),
            dma((1,)),
            dma((2, NK)),
            dma((1,)),
            dma((2, NK)),
            dma((4,)),
        ],
        compiler_params=pltpu.CompilerParams(
            collective_id=0, has_side_effects=True, vmem_limit_bytes=64 * 1024 * 1024 - 65536
        ),
        cost_estimate=pl.CostEstimate(
            flops=4_000_000_000, bytes_accessed=5_000_000, transcendentals=0
        ),
    )(
        daylit_count,
        daylit_list,
        features,
        in_weight,
        in_bias,
        mid_weight,
        mid_bias,
        out_weight,
        out_bias,
    )


def solution(mesh):
    in_specs = (
        P(None, ("blk", "pair")),
        P(("blk", "pair")),
        P(("blk", "pair")),
        P(),
        P(),
        P(),
        P(),
        P(),
        P(),
    )
    out_specs = P(None, ("blk", "pair"))
    return jax.shard_map(shards, mesh=mesh, in_specs=in_specs, out_specs=out_specs, check_vma=False)
```

```python
import jax
import jax.numpy as jnp
from jax import lax
from jax.experimental import pallas as pl
from jax.experimental.pallas import tpu as pltpu
from jax.sharding import PartitionSpec as P

FEAT, HID, OUT = 557, 512, 368
LANES = 384
NX, NZ, NY, NC, NK = 4, 8, 8, 2, 3
BLOCK = NZ * NY * NC * NK
ROWS = NZ * NY
COLS = NX * BLOCK
OFFSETS = (1, 3, 2, 0)
RING = (4, 3, 5, 2, 6, 1, 7)
VMEM = 62 * 1024 * 1024
BF16, F32 = jnp.bfloat16, jnp.float32
MESH = pl.DeviceIdType.MESH


def nt(a, b):
    return lax.dot_general(a, b, (((1,), (1,)), ((), ())), preferred_element_type=F32)


def leaky(t):
    return jnp.maximum(t, 0.15 * t)


def selector(rows, cols, column_of_row):
    r = lax.broadcasted_iota(jnp.int32, (rows, cols), 0)
    c = lax.broadcasted_iota(jnp.int32, (rows, cols), 1)
    return jnp.where(c == column_of_row(r), 1.0, 0.0).astype(BF16)


def kernel(
    count_ref, list_ref, feat_ref, w0_ref, b0_ref, wm_ref, bm_ref, wo_ref, bo_ref, out_ref,
    list_v, f_v, w0_v, b0_v, wm_v, bm_v, wo_v, bo_v, day_v, sx, rx, zs, zr, ys, yr, t_v,
    load_sem, sx_sem, rx_sem, zs_sem, zr_sem, ys_sem, yr_sem, t_sem,
):
    x = lax.axis_index("pair")
    blk = lax.axis_index("blk")
    z, y, c = blk // (NY * NC), (blk // NC) % NY, blk % NC

    def blk_of(zz, yy, cc):
        return (zz * NY + yy) * NC + cc

    sectors = [lax.rem(x + off, NX) for off in OFFSETS]

    loads = [
        pltpu.make_async_copy(
            feat_ref.at[:, pl.ds(pl.multiple_of(a * BLOCK, 128), BLOCK)], f_v.at[i], load_sem.at[i]
        )
        for i, a in enumerate(sectors)
    ]
    load_w0 = pltpu.make_async_copy(w0_ref, w0_v, load_sem.at[4])
    load_wm = pltpu.make_async_copy(wm_ref, wm_v, load_sem.at[5])
    load_wo = pltpu.make_async_copy(wo_ref, wo_v.at[pl.ds(0, OUT)], load_sem.at[6])
    small = [
        pltpu.make_async_copy(src, dst, load_sem.at[7 + n])
        for n, (src, dst) in enumerate(
            ((list_ref, list_v), (b0_ref, b0_v), (bm_ref, bm_v), (bo_ref, bo_v))
        )
    ]
    for load in (*small, loads[0], load_w0, load_wm, load_wo, *loads[1:]):
        load.start()

    barrier = pltpu.get_barrier_semaphore()
    peers = []
    for a in sectors:
        peers.append((blk_of(z, y, 1 - c), a))
    for a in sectors[:3]:
        peers.append((blk, a))
    for d in RING:
        peers.append((blk_of(lax.rem(z + d, NZ), y, c), x))
    for d in RING:
        peers.append((blk_of(z, lax.rem(y + d, NY), c), x))
    for peer in peers:
        pl.semaphore_signal(barrier, inc=1, device_id=peer, device_id_type=MESH)

    group = selector(BLOCK, BLOCK, lambda r: (r & (ROWS - 1)) * (NC * NK) + (r >> 6))
    turn = selector(128, 128, lambda r: (r & 15) * 8 + (r >> 4))
    place = selector(
        BLOCK,
        BLOCK,
        lambda r: (((r >> 1) & 7) * 16 + ((r >> 4) & 7) * 2 + (r & 1)) * NK + (r >> 7),
    )
    eye = selector(LANES, LANES, lambda r: r)

    for load in small:
        load.wait()
    entries = list_v[...].reshape(1, COLS)
    usable = lax.broadcasted_iota(jnp.int32, (1, COLS), 1) < count_ref[0]
    high = jnp.where(usable, entries >> 7, -1)
    high = jnp.broadcast_to(high, (16, COLS)) == lax.broadcasted_iota(jnp.int32, (16, COLS), 0)
    low = jnp.broadcast_to(entries & 127, (128, COLS)) == lax.broadcasted_iota(
        jnp.int32, (128, COLS), 0
    )
    day_v[...] = nt(
        jnp.where(high, 1.0, 0.0).astype(BF16), jnp.where(low, 1.0, 0.0).astype(BF16)
    )
    wo_v[pl.ds(OUT, LANES - OUT), :] = jnp.zeros((LANES - OUT, HID), BF16)
    bias_0 = b0_v[...].reshape(1, HID)
    bias_out = jnp.concatenate([bo_v[...].reshape(1, OUT), jnp.zeros((1, LANES - OUT), F32)], axis=1)
    first_half = jnp.where(x < NX // 2, 1.0, 0.0)
    lane = lax.broadcasted_iota(jnp.int32, (BLOCK, LANES), 1)

    def compute(i):
        day = jnp.concatenate(
            [day_v[pl.ds(sectors[i] * 3 + t, 1), :] for t in range(3)], axis=1
        )
        day = jnp.where(day > 0.5, 1.0, 0.0)
        day = nt(group, jnp.broadcast_to(day, (128, BLOCK)).astype(BF16))
        day = jnp.concatenate([day, day, day], axis=1)
        cols = nt(group, f_v[i]).astype(BF16)
        if i == 0:
            load_w0.wait()
        h = jnp.dot(cols, w0_v[...], preferred_element_type=F32)
        h = leaky(h + bias_0).astype(BF16)
        if i == 0:
            load_wm.wait()
        for layer in range(2):
            h = leaky(nt(h, wm_v[layer]) + bm_v[pl.ds(layer, 1), :]).astype(BF16)
        if i == 0:
            load_wo.wait()
        v = nt(h, wo_v[...]) + bias_out
        v = jnp.where(lane == OUT, first_half, v) * day
        sx[i] = v.astype(BF16)

    def send_x(i):
        half = i // 2
        for k in range(NK):
            for cc in range(NC) if i < 3 else (1 - c,):
                pltpu.make_async_remote_copy(
                    src_ref=sx.at[i, pl.ds(pl.multiple_of((cc * NK + k) * ROWS, ROWS), ROWS)],
                    dst_ref=rx.at[half, k, 2 * (i % 2) + c],
                    send_sem=sx_sem.at[0],
                    recv_sem=rx_sem.at[half, k],
                    device_id=(blk_of(z, y, cc), sectors[i]),
                    device_id_type=MESH,
                ).start()

    def wait_for(view, sem):
        pltpu.make_async_copy(view, view, sem).wait()

    def block(i):
        loads[i].wait()
        compute(i)
        if i == 0:
            pl.semaphore_wait(barrier, len(peers))
        send_x(i)
        if i == 3:
            for k in range(NK):
                rx[1, k, pl.ds(2 + c, 1)] = sx[
                    3, pl.ds(pl.multiple_of((c * NK + k) * ROWS, ROWS), ROWS)
                ][None]

    def stage_x(half, k):
        wait_for(rx.at[half, k, pl.ds(0, 4 - half)], rx_sem.at[half, k])
        parts = [
            (rx[half, k, cc].astype(F32) + rx[half, k, 2 + cc].astype(F32)).reshape(NZ, NY, LANES)
            for cc in range(NC)
        ]
        zs[half, k] = jnp.concatenate(parts, axis=1).astype(BF16)
        for d in RING:
            zz = lax.rem(z + d, NZ)
            pltpu.make_async_remote_copy(
                src_ref=zs.at[half, k, zz],
                dst_ref=zr.at[half, k, z],
                send_sem=zs_sem.at[0],
                recv_sem=zr_sem.at[half, k],
                device_id=(blk_of(zz, y, c), x),
                device_id_type=MESH,
            ).start()
        zr[half, k, pl.ds(z, 1)] = zs[half, k, pl.ds(z, 1)]

    def stage_z(half, k):
        wait_for(zr.at[half, k, pl.ds(0, NZ - 1)], zr_sem.at[half, k])
        turned = jnp.dot(turn, zr[half, k].reshape(128, LANES), preferred_element_type=F32)
        ys[half, k] = turned.astype(BF16).reshape(NY, 16, LANES)
        for d in RING:
            yy = lax.rem(y + d, NY)
            pltpu.make_async_remote_copy(
                src_ref=ys.at[half, k, yy],
                dst_ref=yr.at[half, k, y],
                send_sem=ys_sem.at[0],
                recv_sem=yr_sem.at[half, k],
                device_id=(blk_of(z, yy, c), x),
                device_id_type=MESH,
            ).start()
        yr[half, k, pl.ds(y, 1)] = ys[half, k, pl.ds(y, 1)]

    def stage_y(half, k, total):
        wait_for(yr.at[half, k, pl.ds(0, NY - 1)], yr_sem.at[half, k])
        turned = nt(eye, yr[half, k].reshape(128, LANES)).astype(BF16)
        part = jnp.dot(turned, place[k * 128 : (k + 1) * 128], preferred_element_type=F32)
        return part if total is None else total + part

    def put(half, total):
        t_v[half] = total.astype(BF16)
        near = lax.rem(x + 1 + half, 2)
        pltpu.make_async_copy(t_v.at[half], out_ref.at[near], t_sem.at[half]).start()

    for i in range(3):
        block(i)
    stage_x(0, 0)
    block(3)
    chunks = [(half, k) for half in range(2) for k in range(NK)]
    for t in range(1, len(chunks) + 1):
        if t < len(chunks):
            stage_x(*chunks[t])
        stage_z(*chunks[t - 1])
    for half in range(2):
        total = None
        for k in range(NK):
            total = stage_y(half, k, total)
        put(half, total)

    wait_for(sx.at[pl.ds(0, 3)], sx_sem.at[0])
    wait_for(sx.at[3, pl.ds(0, BLOCK // 2)], sx_sem.at[0])
    wait_for(zs.at[:, :, pl.ds(0, NZ - 1)], zs_sem.at[0])
    wait_for(ys.at[:, :, pl.ds(0, NY - 1)], ys_sem.at[0])
    for half in range(2):
        wait_for(t_v.at[half], t_sem.at[half])


def spread(t_ref, out_ref, t_v, o_v, t_sem, o_sem):
    loads = [pltpu.make_async_copy(t_ref.at[n], t_v.at[n], t_sem.at[n]) for n in range(2)]
    for load in loads:
        load.start()
    stores = []
    for n in range(2):
        loads[n].wait()
        values = t_v[n].astype(F32)
        flag = values[OUT : OUT + 1]
        for far, weight in enumerate((flag, 1.0 - flag)):
            slot = n + 2 * far
            o_v[slot] = (values[:OUT] * weight).astype(BF16)
            store = pltpu.make_async_copy(
                o_v.at[slot], out_ref.at[:, pl.ds(slot * BLOCK, BLOCK)], o_sem.at[slot]
            )
            store.start()
            stores.append(store)
    for store in stores:
        store.wait()


def shards(
    features, daylit_list, daylit_count, in_weight, in_bias, mid_weight, mid_bias, out_weight, out_bias
):
    hbm = pl.BlockSpec(memory_space=pltpu.HBM)
    dma = pltpu.SemaphoreType.DMA
    halves = pl.pallas_call(
        kernel,
        out_shape=jax.ShapeDtypeStruct((2, LANES, BLOCK), BF16),
        in_specs=[pl.BlockSpec(memory_space=pltpu.SMEM)] + [hbm] * 8,
        out_specs=hbm,
        scratch_shapes=[
            pltpu.VMEM((COLS,), jnp.int32),
            pltpu.VMEM((4, FEAT, BLOCK), BF16),
            pltpu.VMEM((FEAT, HID), BF16),
            pltpu.VMEM((HID,), F32),
            pltpu.VMEM((2, HID, HID), BF16),
            pltpu.VMEM((2, HID), F32),
            pltpu.VMEM((LANES, HID), BF16),
            pltpu.VMEM((OUT,), F32),
            pltpu.VMEM((16, 128), F32),
            pltpu.VMEM((4, BLOCK, LANES), BF16),
            pltpu.VMEM((2, NK, 4, ROWS, LANES), BF16),
            pltpu.VMEM((2, NK, NZ, 16, LANES), BF16),
            pltpu.VMEM((2, NK, NZ, 16, LANES), BF16),
            pltpu.VMEM((2, NK, NY, 16, LANES), BF16),
            pltpu.VMEM((2, NK, NY, 16, LANES), BF16),
            pltpu.VMEM((2, LANES, BLOCK), BF16),
            dma((11,)),
            dma((1,)),
            dma((2, NK)),
            dma((1,)),
            dma((2, NK)),
            dma((1,)),
            dma((2, NK)),
            dma((2,)),
        ],
        compiler_params=pltpu.CompilerParams(
            collective_id=0, has_side_effects=True, vmem_limit_bytes=VMEM
        ),
        cost_estimate=pl.CostEstimate(
            flops=4_000_000_000, bytes_accessed=5_000_000, transcendentals=0
        ),
    )(
        daylit_count,
        daylit_list,
        features,
        in_weight,
        in_bias,
        mid_weight,
        mid_bias,
        out_weight,
        out_bias,
    )
    return pl.pallas_call(
        spread,
        out_shape=jax.ShapeDtypeStruct((OUT, COLS), BF16),
        in_specs=[hbm],
        out_specs=hbm,
        scratch_shapes=[
            pltpu.VMEM((2, LANES, BLOCK), BF16),
            pltpu.VMEM((4, OUT, BLOCK), BF16),
            dma((2,)),
            dma((4,)),
        ],
        compiler_params=pltpu.CompilerParams(vmem_limit_bytes=VMEM),
    )(halves)


def solution(mesh):
    in_specs = (
        P(None, ("blk", "pair")),
        P(("blk", "pair")),
        P(("blk", "pair")),
        P(),
        P(),
        P(),
        P(),
        P(),
        P(),
    )
    out_specs = P(None, ("blk", "pair"))
    return jax.shard_map(shards, mesh=mesh, in_specs=in_specs, out_specs=out_specs, check_vma=False)
```

```python
import jax
import jax.numpy as jnp
from jax import lax
from jax.experimental import pallas as pl
from jax.experimental.pallas import tpu as pltpu
from jax.sharding import PartitionSpec as P

FEAT, HID, OUT = 557, 512, 368
LANES = 384
NX, NZ, NY, NC, NK = 4, 8, 8, 2, 3
BLOCK = NZ * NY * NC * NK
ROWS = NZ * NY
COLS = NX * BLOCK
OFFSETS = (1, 3, 2, 0)
RING = (4, 3, 5, 2, 6, 1, 7)
VMEM = 62 * 1024 * 1024
BF16, F32 = jnp.bfloat16, jnp.float32
MESH = pl.DeviceIdType.MESH


def nt(a, b):
    return lax.dot_general(a, b, (((1,), (1,)), ((), ())), preferred_element_type=F32)


def leaky(t):
    return jnp.maximum(t, 0.15 * t)


def selector(rows, cols, column_of_row):
    r = lax.broadcasted_iota(jnp.int32, (rows, cols), 0)
    c = lax.broadcasted_iota(jnp.int32, (rows, cols), 1)
    return jnp.where(c == column_of_row(r), 1.0, 0.0).astype(BF16)


def column(row):
    return jnp.transpose(jnp.broadcast_to(row, (128, row.shape[1])))


def network(
    count_ref, list_ref, feat_ref, w0_ref, b0_ref, wm_ref, bm_ref, wo_ref, bo_ref, out_ref,
    list_v, f_v, w0_v, b0_v, wm_v, bm_v, wo_v, bo_v, day_v, w0t_v, o_v, load_sem, o_sem,
):
    x = lax.axis_index("pair")
    width = 2 * BLOCK
    loads = [
        pltpu.make_async_copy(src, dst, load_sem.at[n])
        for n, (src, dst) in enumerate(
            (
                (list_ref, list_v),
                (b0_ref, b0_v),
                (bm_ref, bm_v),
                (bo_ref, bo_v),
                (w0_ref, w0_v),
                (feat_ref.at[:, pl.ds(0, width)], f_v.at[0]),
                (wm_ref, wm_v),
                (wo_ref, wo_v.at[pl.ds(0, OUT)]),
                (feat_ref.at[:, pl.ds(width, width)], f_v.at[1]),
            )
        )
    ]
    for load in loads:
        load.start()

    group = selector(BLOCK, BLOCK, lambda r: (r & (ROWS - 1)) * (NC * NK) + (r >> 6))
    wo_v[pl.ds(OUT, LANES - OUT), :] = jnp.zeros((LANES - OUT, HID), BF16)

    for load in loads[:4]:
        load.wait()
    entries = list_v[...].reshape(1, COLS)
    usable = lax.broadcasted_iota(jnp.int32, (1, COLS), 1) < count_ref[0]
    high = jnp.where(usable, entries >> 7, -1)
    high = jnp.broadcast_to(high, (16, COLS)) == lax.broadcasted_iota(jnp.int32, (16, COLS), 0)
    low = jnp.broadcast_to(entries & 127, (128, COLS)) == lax.broadcasted_iota(
        jnp.int32, (128, COLS), 0
    )
    day_v[...] = nt(
        jnp.where(high, 1.0, 0.0).astype(BF16), jnp.where(low, 1.0, 0.0).astype(BF16)
    )
    biases = [column(b0_v[...].reshape(1, HID))]
    biases += [column(bm_v[pl.ds(n, 1), :]) for n in range(2)]
    bias_out = jnp.concatenate([bo_v[...].reshape(1, OUT), jnp.zeros((1, LANES - OUT), F32)], axis=1)
    biases.append(column(bias_out))
    biases = [jnp.concatenate([b] * (width // 128), axis=1) for b in biases]
    first_half = jnp.where(x < NX // 2, 1.0, 0.0)
    feat = lax.broadcasted_iota(jnp.int32, (LANES, width), 0)

    loads[4].wait()
    w0t_v[...] = nt(selector(HID, HID, lambda r: r), w0_v[...]).astype(BF16)
    stores = []
    for n in range(2):
        loads[5 if n == 0 else 8].wait()
        h = jnp.dot(w0t_v[...], f_v[n], preferred_element_type=F32)
        h = leaky(h + biases[0]).astype(BF16)
        if n == 0:
            loads[6].wait()
        for layer in range(2):
            h = jnp.dot(wm_v[layer], h, preferred_element_type=F32)
            h = leaky(h + biases[1 + layer]).astype(BF16)
        if n == 0:
            loads[7].wait()
        v = jnp.dot(wo_v[...], h, preferred_element_type=F32) + biases[3]
        day = jnp.concatenate([day_v[pl.ds(n * 6 + t, 1), :] for t in range(6)], axis=1)
        v = jnp.where(feat == OUT, first_half, v) * jnp.where(day > 0.5, 1.0, 0.0)
        v = v.astype(BF16)
        for t in range(2):
            a = 2 * n + t
            o_v[a] = nt(group, v[:, t * BLOCK : (t + 1) * BLOCK]).astype(BF16)
            stores.append(pltpu.make_async_copy(o_v.at[a], out_ref.at[a], o_sem.at[a]))
            stores[-1].start()
    for store in stores:
        store.wait()


def regroup(
    sx, out_ref, rx, zs, zr, ys, yr, t_v,
    own_sem, sx_sem, rx_sem, zs_sem, zr_sem, ys_sem, yr_sem, t_sem,
):
    x = lax.axis_index("pair")
    blk = lax.axis_index("blk")
    z, y, c = blk // (NY * NC), (blk // NC) % NY, blk % NC

    def blk_of(zz, yy, cc):
        return (zz * NY + yy) * NC + cc

    sectors = [lax.rem(x + off, NX) for off in OFFSETS]

    barrier = pltpu.get_barrier_semaphore()
    peers = []
    for a in sectors:
        peers.append((blk_of(z, y, 1 - c), a))
    for a in sectors[:3]:
        peers.append((blk, a))
    for d in RING:
        peers.append((blk_of(lax.rem(z + d, NZ), y, c), x))
    for d in RING:
        peers.append((blk_of(z, lax.rem(y + d, NY), c), x))
    for peer in peers:
        pl.semaphore_signal(barrier, inc=1, device_id=peer, device_id_type=MESH)

    own = [
        pltpu.make_async_copy(
            sx.at[x, pl.ds(pl.multiple_of((c * NK + k) * ROWS, ROWS), ROWS)],
            rx.at[1, k, 2 + c],
            own_sem.at[k],
        )
        for k in range(NK)
    ]
    for copy in own:
        copy.start()

    turn = selector(128, 128, lambda r: (r & 15) * 8 + (r >> 4))
    place = selector(
        BLOCK,
        BLOCK,
        lambda r: (((r >> 1) & 7) * 16 + ((r >> 4) & 7) * 2 + (r & 1)) * NK + (r >> 7),
    )
    eye = selector(LANES, LANES, lambda r: r)

    pl.semaphore_wait(barrier, len(peers))
    for i in range(4):
        half = i // 2
        for k in range(NK):
            for cc in range(NC) if i < 3 else (1 - c,):
                pltpu.make_async_remote_copy(
                    src_ref=sx.at[
                        sectors[i], pl.ds(pl.multiple_of((cc * NK + k) * ROWS, ROWS), ROWS)
                    ],
                    dst_ref=rx.at[half, k, 2 * (i % 2) + c],
                    send_sem=sx_sem.at[0],
                    recv_sem=rx_sem.at[half, k],
                    device_id=(blk_of(z, y, cc), sectors[i]),
                    device_id_type=MESH,
                ).start()

    def wait_for(view, sem):
        pltpu.make_async_copy(view, view, sem).wait()

    def stage_x(half, k):
        wait_for(rx.at[half, k, pl.ds(0, 4 - half)], rx_sem.at[half, k])
        if half == 1:
            own[k].wait()
        parts = [
            (rx[half, k, cc].astype(F32) + rx[half, k, 2 + cc].astype(F32)).reshape(NZ, NY, LANES)
            for cc in range(NC)
        ]
        zs[half, k] = jnp.concatenate(parts, axis=1).astype(BF16)
        for d in RING:
            zz = lax.rem(z + d, NZ)
            pltpu.make_async_remote_copy(
                src_ref=zs.at[half, k, zz],
                dst_ref=zr.at[half, k, z],
                send_sem=zs_sem.at[0],
                recv_sem=zr_sem.at[half, k],
                device_id=(blk_of(zz, y, c), x),
                device_id_type=MESH,
            ).start()
        zr[half, k, pl.ds(z, 1)] = zs[half, k, pl.ds(z, 1)]

    def stage_z(half, k):
        wait_for(zr.at[half, k, pl.ds(0, NZ - 1)], zr_sem.at[half, k])
        turned = jnp.dot(turn, zr[half, k].reshape(128, LANES), preferred_element_type=F32)
        ys[half, k] = turned.astype(BF16).reshape(NY, 16, LANES)
        for d in RING:
            yy = lax.rem(y + d, NY)
            pltpu.make_async_remote_copy(
                src_ref=ys.at[half, k, yy],
                dst_ref=yr.at[half, k, y],
                send_sem=ys_sem.at[0],
                recv_sem=yr_sem.at[half, k],
                device_id=(blk_of(z, yy, c), x),
                device_id_type=MESH,
            ).start()
        yr[half, k, pl.ds(y, 1)] = ys[half, k, pl.ds(y, 1)]

    def stage_y(half, k, total):
        wait_for(yr.at[half, k, pl.ds(0, NY - 1)], yr_sem.at[half, k])
        turned = nt(eye, yr[half, k].reshape(128, LANES)).astype(BF16)
        part = jnp.dot(turned, place[k * 128 : (k + 1) * 128], preferred_element_type=F32)
        return part if total is None else total + part

    def put(half, total):
        t_v[half] = total.astype(BF16)
        near = lax.rem(x + 1 + half, 2)
        pltpu.make_async_copy(t_v.at[half], out_ref.at[near], t_sem.at[half]).start()

    chunks = [(half, k) for half in range(2) for k in range(NK)]
    for t in range(len(chunks) + 1):
        if t < len(chunks):
            stage_x(*chunks[t])
        if t >= 1:
            stage_z(*chunks[t - 1])
    for half in range(2):
        total = None
        for k in range(NK):
            total = stage_y(half, k, total)
        put(half, total)

    wait_for(sx.at[pl.ds(0, 3)], sx_sem.at[0])
    wait_for(sx.at[3, pl.ds(0, BLOCK // 2)], sx_sem.at[0])
    wait_for(zs.at[:, :, pl.ds(0, NZ - 1)], zs_sem.at[0])
    wait_for(ys.at[:, :, pl.ds(0, NY - 1)], ys_sem.at[0])
    for half in range(2):
        wait_for(t_v.at[half], t_sem.at[half])


def spread(t_ref, out_ref, t_v, o_v, t_sem, o_sem):
    loads = [pltpu.make_async_copy(t_ref.at[n], t_v.at[n], t_sem.at[n]) for n in range(2)]
    for load in loads:
        load.start()
    stores = []
    for n in range(2):
        loads[n].wait()
        values = t_v[n].astype(F32)
        flag = values[OUT : OUT + 1]
        for far, weight in enumerate((flag, 1.0 - flag)):
            slot = n + 2 * far
            o_v[slot] = (values[:OUT] * weight).astype(BF16)
            store = pltpu.make_async_copy(
                o_v.at[slot], out_ref.at[:, pl.ds(slot * BLOCK, BLOCK)], o_sem.at[slot]
            )
            store.start()
            stores.append(store)
    for store in stores:
        store.wait()


def shards(
    features, daylit_list, daylit_count, in_weight, in_bias, mid_weight, mid_bias, out_weight, out_bias
):
    hbm = pl.BlockSpec(memory_space=pltpu.HBM)
    dma = pltpu.SemaphoreType.DMA
    values = pl.pallas_call(
        network,
        out_shape=jax.ShapeDtypeStruct((NX, BLOCK, LANES), BF16),
        in_specs=[pl.BlockSpec(memory_space=pltpu.SMEM)] + [hbm] * 8,
        out_specs=hbm,
        scratch_shapes=[
            pltpu.VMEM((COLS,), jnp.int32),
            pltpu.VMEM((2, FEAT, 2 * BLOCK), BF16),
            pltpu.VMEM((FEAT, HID), BF16),
            pltpu.VMEM((HID,), F32),
            pltpu.VMEM((2, HID, HID), BF16),
            pltpu.VMEM((2, HID), F32),
            pltpu.VMEM((LANES, HID), BF16),
            pltpu.VMEM((OUT,), F32),
            pltpu.VMEM((16, 128), F32),
            pltpu.VMEM((HID, FEAT), BF16),
            pltpu.VMEM((NX, BLOCK, LANES), BF16),
            dma((9,)),
            dma((4,)),
        ],
        compiler_params=pltpu.CompilerParams(vmem_limit_bytes=VMEM),
    )(
        daylit_count,
        daylit_list,
        features,
        in_weight,
        in_bias,
        mid_weight,
        mid_bias,
        out_weight,
        out_bias,
    )
    halves = pl.pallas_call(
        regroup,
        out_shape=jax.ShapeDtypeStruct((2, LANES, BLOCK), BF16),
        in_specs=[hbm],
        out_specs=hbm,
        scratch_shapes=[
            pltpu.VMEM((2, NK, 4, ROWS, LANES), BF16),
            pltpu.VMEM((2, NK, NZ, 16, LANES), BF16),
            pltpu.VMEM((2, NK, NZ, 16, LANES), BF16),
            pltpu.VMEM((2, NK, NY, 16, LANES), BF16),
            pltpu.VMEM((2, NK, NY, 16, LANES), BF16),
            pltpu.VMEM((2, LANES, BLOCK), BF16),
            dma((NK,)),
            dma((1,)),
            dma((2, NK)),
            dma((1,)),
            dma((2, NK)),
            dma((1,)),
            dma((2, NK)),
            dma((2,)),
        ],
        compiler_params=pltpu.CompilerParams(
            collective_id=0, has_side_effects=True, vmem_limit_bytes=VMEM
        ),
    )(values)
    return pl.pallas_call(
        spread,
        out_shape=jax.ShapeDtypeStruct((OUT, COLS), BF16),
        in_specs=[hbm],
        out_specs=hbm,
        scratch_shapes=[
            pltpu.VMEM((2, LANES, BLOCK), BF16),
            pltpu.VMEM((4, OUT, BLOCK), BF16),
            dma((2,)),
            dma((4,)),
        ],
        compiler_params=pltpu.CompilerParams(vmem_limit_bytes=VMEM),
    )(halves)


def solution(mesh):
    in_specs = (
        P(None, ("blk", "pair")),
        P(("blk", "pair")),
        P(("blk", "pair")),
        P(),
        P(),
        P(),
        P(),
        P(),
        P(),
    )
    out_specs = P(None, ("blk", "pair"))
    return jax.shard_map(shards, mesh=mesh, in_specs=in_specs, out_specs=out_specs, check_vma=False)
```

```python
import jax
import jax.numpy as jnp
from jax import lax
from jax.experimental import pallas as pl
from jax.experimental.pallas import tpu as pltpu
from jax.sharding import PartitionSpec as P

FEAT, HID, OUT = 557, 512, 368
LANES = 384
NX, NZ, NY, NC, NK = 4, 8, 8, 2, 3
BLOCK = NZ * NY * NC * NK
ROWS = NZ * NY
COLS = NX * BLOCK
OFFSETS = (1, 3, 2, 0)
RING = (4, 3, 5, 2, 6, 1, 7)
VMEM = 62 * 1024 * 1024
BF16, F32 = jnp.bfloat16, jnp.float32
MESH = pl.DeviceIdType.MESH


def nt(a, b):
    return lax.dot_general(a, b, (((1,), (1,)), ((), ())), preferred_element_type=F32)


def leaky(t):
    return jnp.maximum(t, 0.15 * t)


def selector(rows, cols, column_of_row):
    r = lax.broadcasted_iota(jnp.int32, (rows, cols), 0)
    c = lax.broadcasted_iota(jnp.int32, (rows, cols), 1)
    return jnp.where(c == column_of_row(r), 1.0, 0.0).astype(BF16)


def column(row):
    return jnp.transpose(jnp.broadcast_to(row, (128, row.shape[1])))


def kernel(
    count_ref, list_ref, feat_ref, w0_ref, b0_ref, wm_ref, bm_ref, wo_ref, bo_ref, out_ref,
    list_v, f_v, w0_v, b0_v, wm_v, bm_v, wo_v, bo_v, day_v, w0t_v, sx, rx, zs, zr, ys, yr, t_v,
    load_sem, sx_sem, rx_sem, zs_sem, zr_sem, ys_sem, yr_sem, t_sem,
):
    x = lax.axis_index("pair")
    blk = lax.axis_index("blk")
    z, y, c = blk // (NY * NC), (blk // NC) % NY, blk % NC
    width = 2 * BLOCK

    def blk_of(zz, yy, cc):
        return (zz * NY + yy) * NC + cc

    sectors = [lax.rem(x + off, NX) for off in OFFSETS]

    def features_of(i):
        return (
            feat_ref.at[:, pl.ds(pl.multiple_of(sectors[i] * BLOCK, 128), BLOCK)],
            f_v.at[i // 2, :, pl.ds((i % 2) * BLOCK, BLOCK)],
        )

    loads = [
        pltpu.make_async_copy(src, dst, load_sem.at[n])
        for n, (src, dst) in enumerate(
            (
                (list_ref, list_v),
                (b0_ref, b0_v),
                (bm_ref, bm_v),
                (bo_ref, bo_v),
                (w0_ref, w0_v),
                features_of(0),
                features_of(1),
                (wm_ref, wm_v),
                (wo_ref, wo_v.at[pl.ds(0, OUT)]),
                features_of(2),
                features_of(3),
            )
        )
    ]
    for load in loads:
        load.start()

    barrier = pltpu.get_barrier_semaphore()
    peers = []
    for a in sectors:
        peers.append((blk_of(z, y, 1 - c), a))
    for a in sectors[:3]:
        peers.append((blk, a))
    for d in RING:
        peers.append((blk_of(lax.rem(z + d, NZ), y, c), x))
    for d in RING:
        peers.append((blk_of(z, lax.rem(y + d, NY), c), x))
    for peer in peers:
        pl.semaphore_signal(barrier, inc=1, device_id=peer, device_id_type=MESH)

    group = selector(BLOCK, BLOCK, lambda r: (r & (ROWS - 1)) * (NC * NK) + (r >> 6))
    wo_v[pl.ds(OUT, LANES - OUT), :] = jnp.zeros((LANES - OUT, HID), BF16)

    for load in loads[:4]:
        load.wait()
    entries = list_v[...].reshape(1, COLS)
    usable = lax.broadcasted_iota(jnp.int32, (1, COLS), 1) < count_ref[0]
    high = jnp.where(usable, entries >> 7, -1)
    high = jnp.broadcast_to(high, (16, COLS)) == lax.broadcasted_iota(jnp.int32, (16, COLS), 0)
    low = jnp.broadcast_to(entries & 127, (128, COLS)) == lax.broadcasted_iota(
        jnp.int32, (128, COLS), 0
    )
    day_v[...] = nt(
        jnp.where(high, 1.0, 0.0).astype(BF16), jnp.where(low, 1.0, 0.0).astype(BF16)
    )
    biases = [column(b0_v[...].reshape(1, HID))]
    biases += [column(bm_v[pl.ds(n, 1), :]) for n in range(2)]
    bias_out = jnp.concatenate([bo_v[...].reshape(1, OUT), jnp.zeros((1, LANES - OUT), F32)], axis=1)
    biases.append(column(bias_out))
    biases = [jnp.concatenate([b] * (width // 128), axis=1) for b in biases]
    first_half = jnp.where(x < NX // 2, 1.0, 0.0)
    feat = lax.broadcasted_iota(jnp.int32, (LANES, width), 0)

    loads[4].wait()
    w0t_v[...] = nt(selector(HID, HID, lambda r: r), w0_v[...]).astype(BF16)

    def network(n):
        for load in loads[5:7] if n == 0 else loads[9:11]:
            load.wait()
        h = jnp.dot(w0t_v[...], f_v[n], preferred_element_type=F32)
        h = leaky(h + biases[0]).astype(BF16)
        if n == 0:
            loads[7].wait()
        for layer in range(2):
            h = jnp.dot(wm_v[layer], h, preferred_element_type=F32)
            h = leaky(h + biases[1 + layer]).astype(BF16)
        if n == 0:
            loads[8].wait()
        v = jnp.dot(wo_v[...], h, preferred_element_type=F32) + biases[3]
        day = jnp.concatenate(
            [
                day_v[pl.ds(sectors[2 * n + t // NK] * NK + t % NK, 1), :]
                for t in range(2 * NK)
            ],
            axis=1,
        )
        v = jnp.where(feat == OUT, first_half, v) * jnp.where(day > 0.5, 1.0, 0.0)
        v = v.astype(BF16)
        for t in range(2):
            sx[2 * n + t] = nt(group, v[:, t * BLOCK : (t + 1) * BLOCK]).astype(BF16)

    def send_x(half, k):
        for i in (2 * half, 2 * half + 1):
            for cc in range(NC) if i < 3 else (1 - c,):
                pltpu.make_async_remote_copy(
                    src_ref=sx.at[i, pl.ds(pl.multiple_of((cc * NK + k) * ROWS, ROWS), ROWS)],
                    dst_ref=rx.at[half, k, 2 * (i % 2) + c],
                    send_sem=sx_sem.at[0],
                    recv_sem=rx_sem.at[half, k],
                    device_id=(blk_of(z, y, cc), sectors[i]),
                    device_id_type=MESH,
                ).start()

    turn = selector(128, 128, lambda r: (r & 15) * 8 + (r >> 4))
    place = selector(
        BLOCK,
        BLOCK,
        lambda r: (((r >> 1) & 7) * 16 + ((r >> 4) & 7) * 2 + (r & 1)) * NK + (r >> 7),
    )
    eye = selector(LANES, LANES, lambda r: r)

    def wait_for(view, sem):
        pltpu.make_async_copy(view, view, sem).wait()

    def stage_x(half, k):
        wait_for(rx.at[half, k, pl.ds(0, 4 - half)], rx_sem.at[half, k])
        if half * NK + k + 2 < 2 * NK:
            send_x(*chunks[half * NK + k + 2])
        parts = [
            (rx[half, k, cc].astype(F32) + rx[half, k, 2 + cc].astype(F32)).reshape(NZ, NY, LANES)
            for cc in range(NC)
        ]
        zs[half, k] = jnp.concatenate(parts, axis=1).astype(BF16)
        for d in RING:
            zz = lax.rem(z + d, NZ)
            pltpu.make_async_remote_copy(
                src_ref=zs.at[half, k, zz],
                dst_ref=zr.at[half, k, z],
                send_sem=zs_sem.at[0],
                recv_sem=zr_sem.at[half, k],
                device_id=(blk_of(zz, y, c), x),
                device_id_type=MESH,
            ).start()
        zr[half, k, pl.ds(z, 1)] = zs[half, k, pl.ds(z, 1)]

    def stage_z(half, k):
        wait_for(zr.at[half, k, pl.ds(0, NZ - 1)], zr_sem.at[half, k])
        turned = jnp.dot(turn, zr[half, k].reshape(128, LANES), preferred_element_type=F32)
        ys[half, k] = turned.astype(BF16).reshape(NY, 16, LANES)
        for d in RING:
            yy = lax.rem(y + d, NY)
            pltpu.make_async_remote_copy(
                src_ref=ys.at[half, k, yy],
                dst_ref=yr.at[half, k, y],
                send_sem=ys_sem.at[0],
                recv_sem=yr_sem.at[half, k],
                device_id=(blk_of(z, yy, c), x),
                device_id_type=MESH,
            ).start()
        yr[half, k, pl.ds(y, 1)] = ys[half, k, pl.ds(y, 1)]

    def stage_y(half, k, total):
        wait_for(yr.at[half, k, pl.ds(0, NY - 1)], yr_sem.at[half, k])
        turned = nt(eye, yr[half, k].reshape(128, LANES)).astype(BF16)
        part = jnp.dot(turned, place[k * 128 : (k + 1) * 128], preferred_element_type=F32)
        return part if total is None else total + part

    def put(half, total):
        t_v[half] = total.astype(BF16)
        near = lax.rem(x + 1 + half, 2)
        pltpu.make_async_copy(t_v.at[half], out_ref.at[near], t_sem.at[half]).start()

    chunks = [(half, k) for half in range(2) for k in range(NK)]
    network(0)
    pl.semaphore_wait(barrier, len(peers))
    send_x(*chunks[0])
    send_x(*chunks[1])
    network(1)
    for k in range(NK):
        rx[1, k, pl.ds(2 + c, 1)] = sx[
            3, pl.ds(pl.multiple_of((c * NK + k) * ROWS, ROWS), ROWS)
        ][None]
    for t in range(len(chunks) + 1):
        if t < len(chunks):
            stage_x(*chunks[t])
        if t >= 1:
            stage_z(*chunks[t - 1])
    for half in range(2):
        total = None
        for k in range(NK):
            total = stage_y(half, k, total)
        put(half, total)

    wait_for(sx.at[pl.ds(0, 3)], sx_sem.at[0])
    wait_for(sx.at[3, pl.ds(0, BLOCK // 2)], sx_sem.at[0])
    wait_for(zs.at[:, :, pl.ds(0, NZ - 1)], zs_sem.at[0])
    wait_for(ys.at[:, :, pl.ds(0, NY - 1)], ys_sem.at[0])
    for half in range(2):
        wait_for(t_v.at[half], t_sem.at[half])


def spread(t_ref, out_ref, t_v, o_v, t_sem, o_sem):
    loads = [pltpu.make_async_copy(t_ref.at[n], t_v.at[n], t_sem.at[n]) for n in range(2)]
    for load in loads:
        load.start()
    stores = []
    for n in range(2):
        loads[n].wait()
        values = t_v[n].astype(F32)
        flag = values[OUT : OUT + 1]
        for far, weight in enumerate((flag, 1.0 - flag)):
            slot = n + 2 * far
            o_v[slot] = (values[:OUT] * weight).astype(BF16)
            store = pltpu.make_async_copy(
                o_v.at[slot], out_ref.at[:, pl.ds(slot * BLOCK, BLOCK)], o_sem.at[slot]
            )
            store.start()
            stores.append(store)
    for store in stores:
        store.wait()


def shards(
    features, daylit_list, daylit_count, in_weight, in_bias, mid_weight, mid_bias, out_weight, out_bias
):
    hbm = pl.BlockSpec(memory_space=pltpu.HBM)
    dma = pltpu.SemaphoreType.DMA
    halves = pl.pallas_call(
        kernel,
        out_shape=jax.ShapeDtypeStruct((2, LANES, BLOCK), BF16),
        in_specs=[pl.BlockSpec(memory_space=pltpu.SMEM)] + [hbm] * 8,
        out_specs=hbm,
        scratch_shapes=[
            pltpu.VMEM((COLS,), jnp.int32),
            pltpu.VMEM((2, FEAT, 2 * BLOCK), BF16),
            pltpu.VMEM((FEAT, HID), BF16),
            pltpu.VMEM((HID,), F32),
            pltpu.VMEM((2, HID, HID), BF16),
            pltpu.VMEM((2, HID), F32),
            pltpu.VMEM((LANES, HID), BF16),
            pltpu.VMEM((OUT,), F32),
            pltpu.VMEM((16, 128), F32),
            pltpu.VMEM((HID, FEAT), BF16),
            pltpu.VMEM((NX, BLOCK, LANES), BF16),
            pltpu.VMEM((2, NK, 4, ROWS, LANES), BF16),
            pltpu.VMEM((2, NK, NZ, 16, LANES), BF16),
            pltpu.VMEM((2, NK, NZ, 16, LANES), BF16),
            pltpu.VMEM((2, NK, NY, 16, LANES), BF16),
            pltpu.VMEM((2, NK, NY, 16, LANES), BF16),
            pltpu.VMEM((2, LANES, BLOCK), BF16),
            dma((11,)),
            dma((1,)),
            dma((2, NK)),
            dma((1,)),
            dma((2, NK)),
            dma((1,)),
            dma((2, NK)),
            dma((2,)),
        ],
        compiler_params=pltpu.CompilerParams(
            collective_id=0, has_side_effects=True, vmem_limit_bytes=VMEM
        ),
    )(
        daylit_count,
        daylit_list,
        features,
        in_weight,
        in_bias,
        mid_weight,
        mid_bias,
        out_weight,
        out_bias,
    )
    return pl.pallas_call(
        spread,
        out_shape=jax.ShapeDtypeStruct((OUT, COLS), BF16),
        in_specs=[hbm],
        out_specs=hbm,
        scratch_shapes=[
            pltpu.VMEM((2, LANES, BLOCK), BF16),
            pltpu.VMEM((4, OUT, BLOCK), BF16),
            dma((2,)),
            dma((4,)),
        ],
        compiler_params=pltpu.CompilerParams(vmem_limit_bytes=VMEM),
    )(halves)


def solution(mesh):
    in_specs = (
        P(None, ("blk", "pair")),
        P(("blk", "pair")),
        P(("blk", "pair")),
        P(),
        P(),
        P(),
        P(),
        P(),
        P(),
    )
    out_specs = P(None, ("blk", "pair"))
    return jax.shard_map(shards, mesh=mesh, in_specs=in_specs, out_specs=out_specs, check_vma=False)
```

```python
import jax
import jax.numpy as jnp
from jax import lax
from jax.experimental import pallas as pl
from jax.experimental.pallas import tpu as pltpu
from jax.sharding import PartitionSpec as P

FEAT, HID, OUT = 557, 512, 368
LANES = 384
NX, NZ, NY, NC, NK = 4, 8, 8, 2, 3
BLOCK = NZ * NY * NC * NK
ROWS = NZ * NY
COLS = NX * BLOCK
OFFSETS = (1, 3, 2, 0)
RING = (4, 3, 5, 2, 6, 1, 7)
VMEM = 62 * 1024 * 1024
BF16, F32 = jnp.bfloat16, jnp.float32
MESH = pl.DeviceIdType.MESH


def nt(a, b):
    return lax.dot_general(a, b, (((1,), (1,)), ((), ())), preferred_element_type=F32)


def leaky(t):
    return jnp.maximum(t, 0.15 * t)


def selector(rows, cols, column_of_row):
    r = lax.broadcasted_iota(jnp.int32, (rows, cols), 0)
    c = lax.broadcasted_iota(jnp.int32, (rows, cols), 1)
    return jnp.where(c == column_of_row(r), 1.0, 0.0).astype(BF16)


def column(row):
    return jnp.transpose(jnp.broadcast_to(row, (128, row.shape[1])))


def kernel(
    count_ref, list_ref, feat_ref, w0_ref, b0_ref, wm_ref, bm_ref, wo_ref, bo_ref, out_ref,
    list_v, f_v, w0_v, b0_v, wm_v, bm_v, wo_v, bo_v, day_v, w0t_v, sx, rx, zs, zr, ys, yr, t_v,
    load_sem, sx_sem, rx_sem, zs_sem, zr_sem, ys_sem, yr_sem, t_sem,
):
    x = lax.axis_index("pair")
    blk = lax.axis_index("blk")
    z, y, c = blk // (NY * NC), (blk // NC) % NY, blk % NC
    width = 2 * BLOCK

    def blk_of(zz, yy, cc):
        return (zz * NY + yy) * NC + cc

    sectors = [lax.rem(x + off, NX) for off in OFFSETS]

    def features_of(i):
        return (
            feat_ref.at[:, pl.ds(pl.multiple_of(sectors[i] * BLOCK, 128), BLOCK)],
            f_v.at[i // 2, :, pl.ds((i % 2) * BLOCK, BLOCK)],
        )

    loads = [
        pltpu.make_async_copy(src, dst, load_sem.at[n])
        for n, (src, dst) in enumerate(
            (
                (list_ref, list_v),
                (b0_ref, b0_v),
                (bm_ref, bm_v),
                (bo_ref, bo_v),
                (w0_ref, w0_v),
                features_of(0),
                features_of(1),
                (wm_ref, wm_v),
                (wo_ref, wo_v.at[pl.ds(0, OUT)]),
                features_of(2),
                features_of(3),
            )
        )
    ]
    for load in loads:
        load.start()

    barrier = pltpu.get_barrier_semaphore()
    peers = []
    for a in sectors:
        peers.append((blk_of(z, y, 1 - c), a))
    for a in sectors[:3]:
        peers.append((blk, a))
    for d in RING:
        peers.append((blk_of(lax.rem(z + d, NZ), y, c), x))
    for d in RING:
        peers.append((blk_of(z, lax.rem(y + d, NY), c), x))
    for peer in peers:
        pl.semaphore_signal(barrier, inc=1, device_id=peer, device_id_type=MESH)

    group = selector(BLOCK, BLOCK, lambda r: (r & (ROWS - 1)) * (NC * NK) + (r >> 6))
    wo_v[pl.ds(OUT, LANES - OUT), :] = jnp.zeros((LANES - OUT, HID), BF16)

    for load in loads[:4]:
        load.wait()
    entries = list_v[...].reshape(1, COLS)
    usable = lax.broadcasted_iota(jnp.int32, (1, COLS), 1) < count_ref[0]
    high = jnp.where(usable, entries >> 7, -1)
    high = jnp.broadcast_to(high, (16, COLS)) == lax.broadcasted_iota(jnp.int32, (16, COLS), 0)
    low = jnp.broadcast_to(entries & 127, (128, COLS)) == lax.broadcasted_iota(
        jnp.int32, (128, COLS), 0
    )
    day_v[...] = nt(
        jnp.where(high, 1.0, 0.0).astype(BF16), jnp.where(low, 1.0, 0.0).astype(BF16)
    )
    biases = [column(b0_v[...].reshape(1, HID))]
    biases += [column(bm_v[pl.ds(n, 1), :]) for n in range(2)]
    bias_out = jnp.concatenate([bo_v[...].reshape(1, OUT), jnp.zeros((1, LANES - OUT), F32)], axis=1)
    biases.append(column(bias_out))
    biases = [jnp.concatenate([b] * (width // 128), axis=1) for b in biases]
    first_half = jnp.where(x < NX // 2, 1.0, 0.0)
    feat = lax.broadcasted_iota(jnp.int32, (LANES, width), 0)

    loads[4].wait()
    w0t_v[...] = nt(selector(HID, HID, lambda r: r), w0_v[...]).astype(BF16)

    def network(n):
        for load in loads[5:7] if n == 0 else loads[9:11]:
            load.wait()
        h = jnp.dot(w0t_v[...], f_v[n], preferred_element_type=F32)
        h = leaky(h + biases[0]).astype(BF16)
        if n == 0:
            loads[7].wait()
        for layer in range(2):
            h = jnp.dot(wm_v[layer], h, preferred_element_type=F32)
            h = leaky(h + biases[1 + layer]).astype(BF16)
        if n == 0:
            loads[8].wait()
        v = jnp.dot(wo_v[...], h, preferred_element_type=F32) + biases[3]
        day = jnp.concatenate(
            [
                day_v[pl.ds(sectors[2 * n + t // NK] * NK + t % NK, 1), :]
                for t in range(2 * NK)
            ],
            axis=1,
        )
        v = jnp.where(feat == OUT, first_half, v) * jnp.where(day > 0.5, 1.0, 0.0)
        v = v.astype(BF16)
        for t in range(2):
            sx[2 * n + t] = nt(group, v[:, t * BLOCK : (t + 1) * BLOCK]).astype(BF16)

    def send_x(half, k):
        for i in (2 * half, 2 * half + 1):
            for cc in range(NC) if i < 3 else (1 - c,):
                pltpu.make_async_remote_copy(
                    src_ref=sx.at[i, pl.ds(pl.multiple_of((cc * NK + k) * ROWS, ROWS), ROWS)],
                    dst_ref=rx.at[half, k, 2 * (i % 2) + c],
                    send_sem=sx_sem.at[0],
                    recv_sem=rx_sem.at[half, k],
                    device_id=(blk_of(z, y, cc), sectors[i]),
                    device_id_type=MESH,
                ).start()

    turn = selector(128, 128, lambda r: (r & 15) * 8 + (r >> 4))
    place = selector(
        BLOCK,
        BLOCK,
        lambda r: (((r >> 1) & 7) * 16 + ((r >> 4) & 7) * 2 + (r & 1)) * NK + (r >> 7),
    )
    eye = selector(LANES, LANES, lambda r: r)

    def wait_for(view, sem):
        pltpu.make_async_copy(view, view, sem).wait()

    def stage_x(half, k):
        wait_for(rx.at[half, k, pl.ds(0, 4 - half)], rx_sem.at[half, k])
        if half * NK + k + 2 < 2 * NK:
            send_x(*chunks[half * NK + k + 2])
        parts = [
            (rx[half, k, cc].astype(F32) + rx[half, k, 2 + cc].astype(F32)).reshape(NZ, NY, LANES)
            for cc in range(NC)
        ]
        zs[half, k] = jnp.concatenate(parts, axis=1).astype(BF16)
        for d in RING:
            zz = lax.rem(z + d, NZ)
            pltpu.make_async_remote_copy(
                src_ref=zs.at[half, k, zz],
                dst_ref=zr.at[half, k, z],
                send_sem=zs_sem.at[0],
                recv_sem=zr_sem.at[half, k],
                device_id=(blk_of(zz, y, c), x),
                device_id_type=MESH,
            ).start()
        zr[half, k, pl.ds(z, 1)] = zs[half, k, pl.ds(z, 1)]

    def stage_z(half, k):
        wait_for(zr.at[half, k, pl.ds(0, NZ - 1)], zr_sem.at[half, k])
        turned = jnp.dot(turn, zr[half, k].reshape(128, LANES), preferred_element_type=F32)
        ys[half, k] = turned.astype(BF16).reshape(NY, 16, LANES)
        for d in RING:
            yy = lax.rem(y + d, NY)
            pltpu.make_async_remote_copy(
                src_ref=ys.at[half, k, yy],
                dst_ref=yr.at[half, k, y],
                send_sem=ys_sem.at[0],
                recv_sem=yr_sem.at[half, k],
                device_id=(blk_of(z, yy, c), x),
                device_id_type=MESH,
            ).start()
        yr[half, k, pl.ds(y, 1)] = ys[half, k, pl.ds(y, 1)]

    def stage_y(half, k, total):
        wait_for(yr.at[half, k, pl.ds(0, NY - 1)], yr_sem.at[half, k])
        turned = nt(eye, yr[half, k].reshape(128, LANES)).astype(BF16)
        part = jnp.dot(turned, place[k * 128 : (k + 1) * 128], preferred_element_type=F32)
        return part if total is None else total + part

    def put(half, total):
        t_v[half] = total.astype(BF16)
        near = lax.rem(x + 1 + half, 2)
        pltpu.make_async_copy(t_v.at[half], out_ref.at[near], t_sem.at[half]).start()

    chunks = [(half, k) for half in range(2) for k in range(NK)]
    network(0)
    pl.semaphore_wait(barrier, len(peers))
    send_x(*chunks[0])
    send_x(*chunks[1])
    network(1)
    for k in range(NK):
        rx[1, k, pl.ds(2 + c, 1)] = sx[
            3, pl.ds(pl.multiple_of((c * NK + k) * ROWS, ROWS), ROWS)
        ][None]
    lag = 2
    for t in range(len(chunks) + lag):
        if t < len(chunks):
            stage_x(*chunks[t])
        if t >= lag:
            stage_z(*chunks[t - lag])
    for half in range(2):
        total = None
        for k in range(NK):
            total = stage_y(half, k, total)
        put(half, total)

    wait_for(sx.at[pl.ds(0, 3)], sx_sem.at[0])
    wait_for(sx.at[3, pl.ds(0, BLOCK // 2)], sx_sem.at[0])
    wait_for(zs.at[:, :, pl.ds(0, NZ - 1)], zs_sem.at[0])
    wait_for(ys.at[:, :, pl.ds(0, NY - 1)], ys_sem.at[0])
    for half in range(2):
        wait_for(t_v.at[half], t_sem.at[half])


def spread(t_ref, out_ref, t_v, o_v, t_sem, o_sem):
    loads = [pltpu.make_async_copy(t_ref.at[n], t_v.at[n], t_sem.at[n]) for n in range(2)]
    for load in loads:
        load.start()
    stores = []
    for n in range(2):
        loads[n].wait()
        values = t_v[n].astype(F32)
        flag = values[OUT : OUT + 1]
        for far, weight in enumerate((flag, 1.0 - flag)):
            slot = n + 2 * far
            o_v[slot] = (values[:OUT] * weight).astype(BF16)
            store = pltpu.make_async_copy(
                o_v.at[slot], out_ref.at[:, pl.ds(slot * BLOCK, BLOCK)], o_sem.at[slot]
            )
            store.start()
            stores.append(store)
    for store in stores:
        store.wait()


def shards(
    features, daylit_list, daylit_count, in_weight, in_bias, mid_weight, mid_bias, out_weight, out_bias
):
    hbm = pl.BlockSpec(memory_space=pltpu.HBM)
    dma = pltpu.SemaphoreType.DMA
    halves = pl.pallas_call(
        kernel,
        out_shape=jax.ShapeDtypeStruct((2, LANES, BLOCK), BF16),
        in_specs=[pl.BlockSpec(memory_space=pltpu.SMEM)] + [hbm] * 8,
        out_specs=hbm,
        scratch_shapes=[
            pltpu.VMEM((COLS,), jnp.int32),
            pltpu.VMEM((2, FEAT, 2 * BLOCK), BF16),
            pltpu.VMEM((FEAT, HID), BF16),
            pltpu.VMEM((HID,), F32),
            pltpu.VMEM((2, HID, HID), BF16),
            pltpu.VMEM((2, HID), F32),
            pltpu.VMEM((LANES, HID), BF16),
            pltpu.VMEM((OUT,), F32),
            pltpu.VMEM((16, 128), F32),
            pltpu.VMEM((HID, FEAT), BF16),
            pltpu.VMEM((NX, BLOCK, LANES), BF16),
            pltpu.VMEM((2, NK, 4, ROWS, LANES), BF16),
            pltpu.VMEM((2, NK, NZ, 16, LANES), BF16),
            pltpu.VMEM((2, NK, NZ, 16, LANES), BF16),
            pltpu.VMEM((2, NK, NY, 16, LANES), BF16),
            pltpu.VMEM((2, NK, NY, 16, LANES), BF16),
            pltpu.VMEM((2, LANES, BLOCK), BF16),
            dma((11,)),
            dma((1,)),
            dma((2, NK)),
            dma((1,)),
            dma((2, NK)),
            dma((1,)),
            dma((2, NK)),
            dma((2,)),
        ],
        compiler_params=pltpu.CompilerParams(
            collective_id=0, has_side_effects=True, vmem_limit_bytes=VMEM
        ),
    )(
        daylit_count,
        daylit_list,
        features,
        in_weight,
        in_bias,
        mid_weight,
        mid_bias,
        out_weight,
        out_bias,
    )
    return pl.pallas_call(
        spread,
        out_shape=jax.ShapeDtypeStruct((OUT, COLS), BF16),
        in_specs=[hbm],
        out_specs=hbm,
        scratch_shapes=[
            pltpu.VMEM((2, LANES, BLOCK), BF16),
            pltpu.VMEM((4, OUT, BLOCK), BF16),
            dma((2,)),
            dma((4,)),
        ],
        compiler_params=pltpu.CompilerParams(vmem_limit_bytes=VMEM),
    )(halves)


def solution(mesh):
    in_specs = (
        P(None, ("blk", "pair")),
        P(("blk", "pair")),
        P(("blk", "pair")),
        P(),
        P(),
        P(),
        P(),
        P(),
        P(),
    )
    out_specs = P(None, ("blk", "pair"))
    return jax.shard_map(shards, mesh=mesh, in_specs=in_specs, out_specs=out_specs, check_vma=False)
```

```python
import jax
import jax.numpy as jnp
from jax import lax
from jax.experimental import pallas as pl
from jax.experimental.pallas import tpu as pltpu
from jax.sharding import PartitionSpec as P

FEAT, HID, OUT = 557, 512, 368
LANES = 384
NX, NZ, NY, NC, NK = 4, 8, 8, 2, 3
BLOCK = NZ * NY * NC * NK
ROWS = NZ * NY
COLS = NX * BLOCK
OFFSETS = (2, 1, 3, 0)
RING = (4, 3, 5, 2, 6, 1, 7)
VMEM = 62 * 1024 * 1024
BF16, F32 = jnp.bfloat16, jnp.float32
MESH = pl.DeviceIdType.MESH


def nt(a, b):
    return lax.dot_general(a, b, (((1,), (1,)), ((), ())), preferred_element_type=F32)


def leaky(t):
    return jnp.maximum(t, 0.15 * t)


def selector(rows, cols, column_of_row):
    r = lax.broadcasted_iota(jnp.int32, (rows, cols), 0)
    c = lax.broadcasted_iota(jnp.int32, (rows, cols), 1)
    return jnp.where(c == column_of_row(r), 1.0, 0.0).astype(BF16)


def column(row):
    return jnp.transpose(jnp.broadcast_to(row, (128, row.shape[1])))


def kernel(
    count_ref, list_ref, feat_ref, w0_ref, b0_ref, wm_ref, bm_ref, wo_ref, bo_ref, out_ref,
    list_v, f_v, w0_v, b0_v, wm_v, bm_v, wo_v, bo_v, day_v, w0t_v, sx, fx, rx, zs, zr, ys, yr, t_v,
    load_sem, sx_sem, fx_sem, fs_sem, rx_sem, zs_sem, zr_sem, ys_sem, yr_sem, t_sem,
):
    x = lax.axis_index("pair")
    blk = lax.axis_index("blk")
    z, y, c = blk // (NY * NC), (blk // NC) % NY, blk % NC

    def blk_of(zz, yy, cc):
        return (zz * NY + yy) * NC + cc

    sectors = [lax.rem(x + off, NX) for off in OFFSETS]

    def features_of(i):
        return (
            feat_ref.at[:, pl.ds(pl.multiple_of(sectors[i] * BLOCK, 128), BLOCK)],
            f_v.at[i],
        )

    loads = [
        pltpu.make_async_copy(src, dst, load_sem.at[n])
        for n, (src, dst) in enumerate(
            (
                (list_ref, list_v),
                (b0_ref, b0_v),
                (bm_ref, bm_v),
                (bo_ref, bo_v),
                (w0_ref, w0_v),
                (wm_ref, wm_v),
                (wo_ref, wo_v.at[pl.ds(0, OUT)]),
                *(features_of(i) for i in range(4)),
            )
        )
    ]
    for n in (0, 1, 2, 3, 4, 7, 5, 6, 8, 9, 10):
        loads[n].start()

    barrier = pltpu.get_barrier_semaphore()
    peers = []
    for a in sectors[1:]:
        peers.append((blk_of(z, y, 1 - c), a))
    for a in sectors[1:3]:
        peers.append((blk, a))
    for d in RING:
        peers.append((blk_of(lax.rem(z + d, NZ), y, c), x))
    for d in RING:
        peers.append((blk_of(z, lax.rem(y + d, NY), c), x))
    for peer in peers:
        pl.semaphore_signal(barrier, inc=1, device_id=peer, device_id_type=MESH)

    group = selector(BLOCK, BLOCK, lambda r: (r & (ROWS - 1)) * (NC * NK) + (r >> 6))
    wo_v[pl.ds(OUT, LANES - OUT), :] = jnp.zeros((LANES - OUT, HID), BF16)

    for load in loads[:4]:
        load.wait()
    entries = list_v[...].reshape(1, COLS)
    usable = lax.broadcasted_iota(jnp.int32, (1, COLS), 1) < count_ref[0]
    high = jnp.where(usable, entries >> 7, -1)
    high = jnp.broadcast_to(high, (16, COLS)) == lax.broadcasted_iota(jnp.int32, (16, COLS), 0)
    low = jnp.broadcast_to(entries & 127, (128, COLS)) == lax.broadcasted_iota(
        jnp.int32, (128, COLS), 0
    )
    day_v[...] = nt(
        jnp.where(high, 1.0, 0.0).astype(BF16), jnp.where(low, 1.0, 0.0).astype(BF16)
    )
    biases = [column(b0_v[...].reshape(1, HID))]
    biases += [column(bm_v[pl.ds(n, 1), :]) for n in range(2)]
    bias_out = jnp.concatenate([bo_v[...].reshape(1, OUT), jnp.zeros((1, LANES - OUT), F32)], axis=1)
    biases.append(column(bias_out))
    first_half = jnp.where(x < NX // 2, 1.0, 0.0)

    loads[4].wait()
    w0t_v[...] = nt(selector(HID, HID, lambda r: r), w0_v[...]).astype(BF16)

    def network(first, count):
        width = count * BLOCK
        tiled = [jnp.concatenate([b] * (width // 128), axis=1) for b in biases]
        for i in range(first, first + count):
            loads[7 + i].wait()
        h = jnp.concatenate([f_v[i] for i in range(first, first + count)], axis=1)
        h = jnp.dot(w0t_v[...], h, preferred_element_type=F32)
        h = leaky(h + tiled[0]).astype(BF16)
        if first == 0:
            loads[5].wait()
        for layer in range(2):
            h = jnp.dot(wm_v[layer], h, preferred_element_type=F32)
            h = leaky(h + tiled[1 + layer]).astype(BF16)
        if first == 0:
            loads[6].wait()
        v = jnp.dot(wo_v[...], h, preferred_element_type=F32) + tiled[3]
        day = jnp.concatenate(
            [
                day_v[pl.ds(sectors[first + t // NK] * NK + t % NK, 1), :]
                for t in range(count * NK)
            ],
            axis=1,
        )
        feat = lax.broadcasted_iota(jnp.int32, (LANES, width), 0)
        v = jnp.where(feat == OUT, first_half, v) * jnp.where(day > 0.5, 1.0, 0.0)
        v = v.astype(BF16)
        for t in range(count):
            sx[first + t] = nt(group, v[:, t * BLOCK : (t + 1) * BLOCK]).astype(BF16)

    def rows_of(cc, k):
        return pl.ds(pl.multiple_of((cc * NK + k) * ROWS, ROWS), ROWS)

    def send(src, dst, send_sem, recv_sem, device):
        pltpu.make_async_remote_copy(
            src_ref=src,
            dst_ref=dst,
            send_sem=send_sem,
            recv_sem=recv_sem,
            device_id=device,
            device_id_type=MESH,
        ).start()

    def send_far(k):
        for cc in range(NC):
            src = sx.at[0, rows_of(cc, k)]
            send(src, fx.at[k, cc], sx_sem.at[0], fx_sem.at[k, cc], (blk, sectors[1 + cc]))

    def send_near(k):
        for i in (1, 2):
            for cc in range(NC):
                dst = rx.at[0, k, 2 * (i - 1) + c]
                device = (blk_of(z, y, cc), sectors[i])
                send(sx.at[i, rows_of(cc, k)], dst, sx_sem.at[0], rx_sem.at[0, k], device)

    def send_own(k):
        dst = rx.at[1, k, 2 + c]
        device = (blk_of(z, y, 1 - c), x)
        send(sx.at[3, rows_of(1 - c, k)], dst, sx_sem.at[0], rx_sem.at[1, k], device)
        rx[1, k, pl.ds(2 + c, 1)] = sx[3, rows_of(c, k)][None]

    def forward(k):
        for cc in range(NC):
            wait_for(fx.at[k, cc], fx_sem.at[k, cc])
            device = (blk_of(z, y, cc), sectors[1 + cc])
            send(fx.at[k, cc], rx.at[1, k, c], fs_sem.at[0], rx_sem.at[1, k], device)

    turn = selector(128, 128, lambda r: (r & 15) * 8 + (r >> 4))
    place = selector(
        BLOCK,
        BLOCK,
        lambda r: (((r >> 1) & 7) * 16 + ((r >> 4) & 7) * 2 + (r & 1)) * NK + (r >> 7),
    )
    eye = selector(LANES, LANES, lambda r: r)

    def wait_for(view, sem):
        pltpu.make_async_copy(view, view, sem).wait()

    def stage_x(half, k):
        wait_for(rx.at[half, k, pl.ds(0, 4 - half)], rx_sem.at[half, k])
        if half == 0:
            forward(k)
        parts = [
            (rx[half, k, cc].astype(F32) + rx[half, k, 2 + cc].astype(F32)).reshape(NZ, NY, LANES)
            for cc in range(NC)
        ]
        zs[half, k] = jnp.concatenate(parts, axis=1).astype(BF16)
        for d in RING:
            zz = lax.rem(z + d, NZ)
            device = (blk_of(zz, y, c), x)
            send(
                zs.at[half, k, zz], zr.at[half, k, z], zs_sem.at[0], zr_sem.at[half, k], device
            )
        zr[half, k, pl.ds(z, 1)] = zs[half, k, pl.ds(z, 1)]

    def stage_z(half, k):
        wait_for(zr.at[half, k, pl.ds(0, NZ - 1)], zr_sem.at[half, k])
        turned = jnp.dot(turn, zr[half, k].reshape(128, LANES), preferred_element_type=F32)
        ys[half, k] = turned.astype(BF16).reshape(NY, 16, LANES)
        for d in RING:
            yy = lax.rem(y + d, NY)
            device = (blk_of(z, yy, c), x)
            send(
                ys.at[half, k, yy], yr.at[half, k, y], ys_sem.at[0], yr_sem.at[half, k], device
            )
        yr[half, k, pl.ds(y, 1)] = ys[half, k, pl.ds(y, 1)]

    def stage_y(half, k, total):
        wait_for(yr.at[half, k, pl.ds(0, NY - 1)], yr_sem.at[half, k])
        turned = nt(eye, yr[half, k].reshape(128, LANES)).astype(BF16)
        part = jnp.dot(turned, place[k * 128 : (k + 1) * 128], preferred_element_type=F32)
        return part if total is None else total + part

    def put(half, total):
        t_v[half] = total.astype(BF16)
        near = lax.rem(x + 1 + half, 2)
        pltpu.make_async_copy(t_v.at[half], out_ref.at[near], t_sem.at[half]).start()

    chunks = [(half, k) for half in range(2) for k in range(NK)]
    network(0, 1)
    pl.semaphore_wait(barrier, len(peers))
    for k in range(NK):
        send_far(k)
    network(1, 2)
    send_near(0)
    send_near(1)
    network(3, 1)
    send_near(2)
    for k in range(NK):
        send_own(k)
    for t in range(len(chunks) + 1):
        if t < len(chunks):
            stage_x(*chunks[t])
        if t >= 1:
            stage_z(*chunks[t - 1])
    for half in range(2):
        total = None
        for k in range(NK):
            total = stage_y(half, k, total)
        put(half, total)

    wait_for(sx.at[pl.ds(0, 3)], sx_sem.at[0])
    wait_for(sx.at[3, pl.ds(0, BLOCK // 2)], sx_sem.at[0])
    wait_for(fx, fs_sem.at[0])
    wait_for(zs.at[:, :, pl.ds(0, NZ - 1)], zs_sem.at[0])
    wait_for(ys.at[:, :, pl.ds(0, NY - 1)], ys_sem.at[0])
    for half in range(2):
        wait_for(t_v.at[half], t_sem.at[half])


def spread(t_ref, out_ref, t_v, o_v, t_sem, o_sem):
    loads = [pltpu.make_async_copy(t_ref.at[n], t_v.at[n], t_sem.at[n]) for n in range(2)]
    for load in loads:
        load.start()
    stores = []
    for n in range(2):
        loads[n].wait()
        values = t_v[n].astype(F32)
        flag = values[OUT : OUT + 1]
        for far, weight in enumerate((flag, 1.0 - flag)):
            slot = n + 2 * far
            o_v[slot] = (values[:OUT] * weight).astype(BF16)
            store = pltpu.make_async_copy(
                o_v.at[slot], out_ref.at[:, pl.ds(slot * BLOCK, BLOCK)], o_sem.at[slot]
            )
            store.start()
            stores.append(store)
    for store in stores:
        store.wait()


def shards(
    features, daylit_list, daylit_count, in_weight, in_bias, mid_weight, mid_bias, out_weight, out_bias
):
    hbm = pl.BlockSpec(memory_space=pltpu.HBM)
    dma = pltpu.SemaphoreType.DMA
    halves = pl.pallas_call(
        kernel,
        out_shape=jax.ShapeDtypeStruct((2, LANES, BLOCK), BF16),
        in_specs=[pl.BlockSpec(memory_space=pltpu.SMEM)] + [hbm] * 8,
        out_specs=hbm,
        scratch_shapes=[
            pltpu.VMEM((COLS,), jnp.int32),
            pltpu.VMEM((4, FEAT, BLOCK), BF16),
            pltpu.VMEM((FEAT, HID), BF16),
            pltpu.VMEM((HID,), F32),
            pltpu.VMEM((2, HID, HID), BF16),
            pltpu.VMEM((2, HID), F32),
            pltpu.VMEM((LANES, HID), BF16),
            pltpu.VMEM((OUT,), F32),
            pltpu.VMEM((16, 128), F32),
            pltpu.VMEM((HID, FEAT), BF16),
            pltpu.VMEM((NX, BLOCK, LANES), BF16),
            pltpu.VMEM((NK, NC, ROWS, LANES), BF16),
            pltpu.VMEM((2, NK, 4, ROWS, LANES), BF16),
            pltpu.VMEM((2, NK, NZ, 16, LANES), BF16),
            pltpu.VMEM((2, NK, NZ, 16, LANES), BF16),
            pltpu.VMEM((2, NK, NY, 16, LANES), BF16),
            pltpu.VMEM((2, NK, NY, 16, LANES), BF16),
            pltpu.VMEM((2, LANES, BLOCK), BF16),
            dma((11,)),
            dma((1,)),
            dma((NK, NC)),
            dma((1,)),
            dma((2, NK)),
            dma((1,)),
            dma((2, NK)),
            dma((1,)),
            dma((2, NK)),
            dma((2,)),
        ],
        compiler_params=pltpu.CompilerParams(
            collective_id=0, has_side_effects=True, vmem_limit_bytes=VMEM
        ),
    )(
        daylit_count,
        daylit_list,
        features,
        in_weight,
        in_bias,
        mid_weight,
        mid_bias,
        out_weight,
        out_bias,
    )
    return pl.pallas_call(
        spread,
        out_shape=jax.ShapeDtypeStruct((OUT, COLS), BF16),
        in_specs=[hbm],
        out_specs=hbm,
        scratch_shapes=[
            pltpu.VMEM((2, LANES, BLOCK), BF16),
            pltpu.VMEM((4, OUT, BLOCK), BF16),
            dma((2,)),
            dma((4,)),
        ],
        compiler_params=pltpu.CompilerParams(vmem_limit_bytes=VMEM),
    )(halves)


def solution(mesh):
    in_specs = (
        P(None, ("blk", "pair")),
        P(("blk", "pair")),
        P(("blk", "pair")),
        P(),
        P(),
        P(),
        P(),
        P(),
        P(),
    )
    out_specs = P(None, ("blk", "pair"))
    return jax.shard_map(shards, mesh=mesh, in_specs=in_specs, out_specs=out_specs, check_vma=False)
```

```python
import jax
import jax.numpy as jnp
from jax import lax
from jax.experimental import pallas as pl
from jax.experimental.pallas import tpu as pltpu
from jax.sharding import PartitionSpec as P

FEAT, HID, OUT = 557, 512, 368
LANES = 384
NX, NZ, NY, NC, NK = 4, 8, 8, 2, 3
BLOCK = NZ * NY * NC * NK
ROWS = NZ * NY
COLS = NX * BLOCK
OFFSETS = (1, 3, 2, 0)
RING = (4, 3, 5, 2, 6, 1, 7)
VMEM = 62 * 1024 * 1024
BF16, F32 = jnp.bfloat16, jnp.float32
MESH = pl.DeviceIdType.MESH


def nt(a, b):
    return lax.dot_general(a, b, (((1,), (1,)), ((), ())), preferred_element_type=F32)


def leaky(t):
    return jnp.maximum(t, 0.15 * t)


def selector(rows, cols, column_of_row):
    r = lax.broadcasted_iota(jnp.int32, (rows, cols), 0)
    c = lax.broadcasted_iota(jnp.int32, (rows, cols), 1)
    return jnp.where(c == column_of_row(r), 1.0, 0.0).astype(BF16)


def column(row):
    return jnp.transpose(jnp.broadcast_to(row, (128, row.shape[1])))


def kernel(
    count_ref, list_ref, feat_ref, w0_ref, b0_ref, wm_ref, bm_ref, wo_ref, bo_ref, out_ref,
    list_v, f_v, w0_v, b0_v, wm_v, bm_v, wo_v, bo_v, day_v, w0t_v, sx, rx, zs, zr, ys, yr, t_v,
    load_sem, sx_sem, rx_sem, zs_sem, zr_sem, ys_sem, yr_sem, t_sem,
):
    x = lax.axis_index("pair")
    blk = lax.axis_index("blk")
    z, y, c = blk // (NY * NC), (blk // NC) % NY, blk % NC
    width = 2 * BLOCK

    def blk_of(zz, yy, cc):
        return (zz * NY + yy) * NC + cc

    sectors = [lax.rem(x + off, NX) for off in OFFSETS]

    def features_of(i):
        return (
            feat_ref.at[:, pl.ds(pl.multiple_of(sectors[i] * BLOCK, 128), BLOCK)],
            f_v.at[i // 2, :, pl.ds((i % 2) * BLOCK, BLOCK)],
        )

    loads = [
        pltpu.make_async_copy(src, dst, load_sem.at[n])
        for n, (src, dst) in enumerate(
            (
                (list_ref, list_v),
                (b0_ref, b0_v),
                (bm_ref, bm_v),
                (bo_ref, bo_v),
                (w0_ref, w0_v),
                features_of(0),
                features_of(1),
                (wm_ref, wm_v),
                (wo_ref, wo_v.at[pl.ds(0, OUT)]),
                features_of(2),
                features_of(3),
            )
        )
    ]
    for load in loads:
        load.start()

    barrier = pltpu.get_barrier_semaphore()
    peers = []
    for a in sectors:
        peers.append((blk_of(z, y, 1 - c), a))
    for a in sectors[:3]:
        peers.append((blk, a))
    for d in RING:
        peers.append((blk_of(lax.rem(z + d, NZ), y, c), x))
    for d in RING:
        peers.append((blk_of(z, lax.rem(y + d, NY), c), x))
    for peer in peers:
        pl.semaphore_signal(barrier, inc=1, device_id=peer, device_id_type=MESH)

    group = selector(BLOCK, BLOCK, lambda r: (r & (ROWS - 1)) * (NC * NK) + (r >> 6))
    wo_v[pl.ds(OUT, LANES - OUT), :] = jnp.zeros((LANES - OUT, HID), BF16)

    for load in loads[:4]:
        load.wait()
    entries = list_v[...].reshape(1, COLS)
    usable = lax.broadcasted_iota(jnp.int32, (1, COLS), 1) < count_ref[0]
    high = jnp.where(usable, entries >> 7, -1)
    high = jnp.broadcast_to(high, (16, COLS)) == lax.broadcasted_iota(jnp.int32, (16, COLS), 0)
    low = jnp.broadcast_to(entries & 127, (128, COLS)) == lax.broadcasted_iota(
        jnp.int32, (128, COLS), 0
    )
    day_v[...] = nt(
        jnp.where(high, 1.0, 0.0).astype(BF16), jnp.where(low, 1.0, 0.0).astype(BF16)
    )
    biases = [column(b0_v[...].reshape(1, HID))]
    biases += [column(bm_v[pl.ds(n, 1), :]) for n in range(2)]
    bias_out = jnp.concatenate([bo_v[...].reshape(1, OUT), jnp.zeros((1, LANES - OUT), F32)], axis=1)
    biases.append(column(bias_out))
    biases = [jnp.concatenate([b] * (width // 128), axis=1) for b in biases]
    first_half = jnp.where(x < NX // 2, 1.0, 0.0)
    feat = lax.broadcasted_iota(jnp.int32, (LANES, width), 0)

    loads[4].wait()
    w0t_v[...] = nt(selector(HID, HID, lambda r: r), w0_v[...]).astype(BF16)

    def network(n):
        for load in loads[5:7] if n == 0 else loads[9:11]:
            load.wait()
        h = jnp.dot(w0t_v[...], f_v[n], preferred_element_type=F32)
        h = leaky(h + biases[0]).astype(BF16)
        if n == 0:
            loads[7].wait()
        for layer in range(2):
            h = jnp.dot(wm_v[layer], h, preferred_element_type=F32)
            h = leaky(h + biases[1 + layer]).astype(BF16)
        if n == 0:
            loads[8].wait()
        v = jnp.dot(wo_v[...], h, preferred_element_type=F32) + biases[3]
        day = jnp.concatenate(
            [
                day_v[pl.ds(sectors[2 * n + t // NK] * NK + t % NK, 1), :]
                for t in range(2 * NK)
            ],
            axis=1,
        )
        v = jnp.where(feat == OUT, first_half, v) * jnp.where(day > 0.5, 1.0, 0.0)
        v = v.astype(BF16)
        for t in range(2):
            sx[2 * n + t] = nt(group, v[:, t * BLOCK : (t + 1) * BLOCK]).astype(BF16)

    def send_x(half, k):
        for i in (2 * half, 2 * half + 1):
            for cc in range(NC) if i < 3 else (1 - c,):
                pltpu.make_async_remote_copy(
                    src_ref=sx.at[i, pl.ds(pl.multiple_of((cc * NK + k) * ROWS, ROWS), ROWS)],
                    dst_ref=rx.at[half, k, 2 * (i % 2) + c],
                    send_sem=sx_sem.at[0],
                    recv_sem=rx_sem.at[half, k],
                    device_id=(blk_of(z, y, cc), sectors[i]),
                    device_id_type=MESH,
                ).start()

    turn = selector(128, 128, lambda r: (r & 15) * 8 + (r >> 4))
    place = selector(
        BLOCK,
        BLOCK,
        lambda r: (((r >> 1) & 7) * 16 + ((r >> 4) & 7) * 2 + (r & 1)) * NK + (r >> 7),
    )
    eye = selector(LANES, LANES, lambda r: r)

    def wait_for(view, sem):
        pltpu.make_async_copy(view, view, sem).wait()

    def stage_x(q):
        for u in range(2):
            n = 2 * q + u
            half, k = chunks[n]
            wait_for(rx.at[half, k, pl.ds(0, 4 - half)], rx_sem.at[half, k])
            if n + 2 < len(chunks):
                send_x(*chunks[n + 2])
            parts = [
                (rx[half, k, cc].astype(F32) + rx[half, k, 2 + cc].astype(F32)).reshape(
                    NZ, NY, LANES
                )
                for cc in range(NC)
            ]
            zs[q, :, u] = jnp.concatenate(parts, axis=1).astype(BF16)
        for d in RING:
            zz = lax.rem(z + d, NZ)
            pltpu.make_async_remote_copy(
                src_ref=zs.at[q, zz],
                dst_ref=zr.at[q, z],
                send_sem=zs_sem.at[0],
                recv_sem=zr_sem.at[q],
                device_id=(blk_of(zz, y, c), x),
                device_id_type=MESH,
            ).start()
        zr[q, pl.ds(z, 1)] = zs[q, pl.ds(z, 1)]

    def stage_z(q):
        wait_for(zr.at[q, pl.ds(0, NZ - 1)], zr_sem.at[q])
        for u in range(2):
            rows = zr[q, :, u].reshape(128, LANES)
            turned = jnp.dot(turn, rows, preferred_element_type=F32)
            ys[q, :, u] = turned.astype(BF16).reshape(NY, 16, LANES)
        for d in RING:
            yy = lax.rem(y + d, NY)
            pltpu.make_async_remote_copy(
                src_ref=ys.at[q, yy],
                dst_ref=yr.at[q, y],
                send_sem=ys_sem.at[0],
                recv_sem=yr_sem.at[q],
                device_id=(blk_of(z, yy, c), x),
                device_id_type=MESH,
            ).start()
        yr[q, pl.ds(y, 1)] = ys[q, pl.ds(y, 1)]

    def stage_y(n, total):
        q, u = n // 2, n % 2
        if u == 0:
            wait_for(yr.at[q, pl.ds(0, NY - 1)], yr_sem.at[q])
        k = n % NK
        turned = nt(eye, yr[q, :, u].reshape(128, LANES)).astype(BF16)
        part = jnp.dot(turned, place[k * 128 : (k + 1) * 128], preferred_element_type=F32)
        return part if total is None else total + part

    def put(half, total):
        t_v[half] = total.astype(BF16)
        near = lax.rem(x + 1 + half, 2)
        pltpu.make_async_copy(t_v.at[half], out_ref.at[near], t_sem.at[half]).start()

    chunks = [(half, k) for half in range(2) for k in range(NK)]
    network(0)
    pl.semaphore_wait(barrier, len(peers))
    send_x(*chunks[0])
    send_x(*chunks[1])
    network(1)
    for k in range(NK):
        rx[1, k, pl.ds(2 + c, 1)] = sx[
            3, pl.ds(pl.multiple_of((c * NK + k) * ROWS, ROWS), ROWS)
        ][None]
    for q in range(4):
        if q < 3:
            stage_x(q)
        if q >= 1:
            stage_z(q - 1)
    for half in range(2):
        total = None
        for k in range(NK):
            total = stage_y(half * NK + k, total)
        put(half, total)

    wait_for(sx.at[pl.ds(0, 3)], sx_sem.at[0])
    wait_for(sx.at[3, pl.ds(0, BLOCK // 2)], sx_sem.at[0])
    wait_for(zs.at[:, pl.ds(0, NZ - 1)], zs_sem.at[0])
    wait_for(ys.at[:, pl.ds(0, NY - 1)], ys_sem.at[0])
    for half in range(2):
        wait_for(t_v.at[half], t_sem.at[half])


def spread(t_ref, out_ref, t_v, o_v, t_sem, o_sem):
    loads = [pltpu.make_async_copy(t_ref.at[n], t_v.at[n], t_sem.at[n]) for n in range(2)]
    for load in loads:
        load.start()
    stores = []
    for n in range(2):
        loads[n].wait()
        values = t_v[n].astype(F32)
        flag = values[OUT : OUT + 1]
        for far, weight in enumerate((flag, 1.0 - flag)):
            slot = n + 2 * far
            o_v[slot] = (values[:OUT] * weight).astype(BF16)
            store = pltpu.make_async_copy(
                o_v.at[slot], out_ref.at[:, pl.ds(slot * BLOCK, BLOCK)], o_sem.at[slot]
            )
            store.start()
            stores.append(store)
    for store in stores:
        store.wait()


def shards(
    features, daylit_list, daylit_count, in_weight, in_bias, mid_weight, mid_bias, out_weight, out_bias
):
    hbm = pl.BlockSpec(memory_space=pltpu.HBM)
    dma = pltpu.SemaphoreType.DMA
    halves = pl.pallas_call(
        kernel,
        out_shape=jax.ShapeDtypeStruct((2, LANES, BLOCK), BF16),
        in_specs=[pl.BlockSpec(memory_space=pltpu.SMEM)] + [hbm] * 8,
        out_specs=hbm,
        scratch_shapes=[
            pltpu.VMEM((COLS,), jnp.int32),
            pltpu.VMEM((2, FEAT, 2 * BLOCK), BF16),
            pltpu.VMEM((FEAT, HID), BF16),
            pltpu.VMEM((HID,), F32),
            pltpu.VMEM((2, HID, HID), BF16),
            pltpu.VMEM((2, HID), F32),
            pltpu.VMEM((LANES, HID), BF16),
            pltpu.VMEM((OUT,), F32),
            pltpu.VMEM((16, 128), F32),
            pltpu.VMEM((HID, FEAT), BF16),
            pltpu.VMEM((NX, BLOCK, LANES), BF16),
            pltpu.VMEM((2, NK, 4, ROWS, LANES), BF16),
            pltpu.VMEM((3, NZ, 2, 16, LANES), BF16),
            pltpu.VMEM((3, NZ, 2, 16, LANES), BF16),
            pltpu.VMEM((3, NY, 2, 16, LANES), BF16),
            pltpu.VMEM((3, NY, 2, 16, LANES), BF16),
            pltpu.VMEM((2, LANES, BLOCK), BF16),
            dma((11,)),
            dma((1,)),
            dma((2, NK)),
            dma((1,)),
            dma((3,)),
            dma((1,)),
            dma((3,)),
            dma((2,)),
        ],
        compiler_params=pltpu.CompilerParams(
            collective_id=0, has_side_effects=True, vmem_limit_bytes=VMEM
        ),
    )(
        daylit_count,
        daylit_list,
        features,
        in_weight,
        in_bias,
        mid_weight,
        mid_bias,
        out_weight,
        out_bias,
    )
    return pl.pallas_call(
        spread,
        out_shape=jax.ShapeDtypeStruct((OUT, COLS), BF16),
        in_specs=[hbm],
        out_specs=hbm,
        scratch_shapes=[
            pltpu.VMEM((2, LANES, BLOCK), BF16),
            pltpu.VMEM((4, OUT, BLOCK), BF16),
            dma((2,)),
            dma((4,)),
        ],
        compiler_params=pltpu.CompilerParams(vmem_limit_bytes=VMEM),
    )(halves)


def solution(mesh):
    in_specs = (
        P(None, ("blk", "pair")),
        P(("blk", "pair")),
        P(("blk", "pair")),
        P(),
        P(),
        P(),
        P(),
        P(),
        P(),
    )
    out_specs = P(None, ("blk", "pair"))
    return jax.shard_map(shards, mesh=mesh, in_specs=in_specs, out_specs=out_specs, check_vma=False)
```

```python
import jax
import jax.numpy as jnp
from jax import lax
from jax.experimental import pallas as pl
from jax.experimental.pallas import tpu as pltpu
from jax.sharding import PartitionSpec as P

FEAT, HID, OUT = 557, 512, 368
LANES = 384
NX, NZ, NY, NC, NK = 4, 8, 8, 2, 3
BLOCK = NZ * NY * NC * NK
ROWS = NZ * NY
COLS = NX * BLOCK
OFFSETS = (1, 3, 2, 0)
RING = (4, 3, 5, 2, 6, 1, 7)
VMEM = 62 * 1024 * 1024
LOADED = (5, 6, 9, 10)
BF16, F32 = jnp.bfloat16, jnp.float32
MESH = pl.DeviceIdType.MESH


def nt(a, b):
    return lax.dot_general(a, b, (((1,), (1,)), ((), ())), preferred_element_type=F32)


def leaky(t):
    return jnp.maximum(t, 0.15 * t)


def selector(rows, cols, column_of_row):
    r = lax.broadcasted_iota(jnp.int32, (rows, cols), 0)
    c = lax.broadcasted_iota(jnp.int32, (rows, cols), 1)
    return jnp.where(c == column_of_row(r), 1.0, 0.0).astype(BF16)


def column(row):
    return jnp.transpose(jnp.broadcast_to(row, (128, row.shape[1])))


def kernel(
    count_ref, list_ref, feat_ref, w0_ref, b0_ref, wm_ref, bm_ref, wo_ref, bo_ref, out_ref,
    list_v, f_v, w0_v, b0_v, wm_v, bm_v, wo_v, bo_v, day_v, w0t_v, pick_v, place_v, sx, rx, zs, zr, ys, yr, t_v,
    load_sem, sx_sem, rx_sem, zs_sem, zr_sem, ys_sem, yr_sem, t_sem,
):
    x = lax.axis_index("pair")
    blk = lax.axis_index("blk")
    z, y, c = blk // (NY * NC), (blk // NC) % NY, blk % NC

    def blk_of(zz, yy, cc):
        return (zz * NY + yy) * NC + cc

    sectors = [lax.rem(x + off, NX) for off in OFFSETS]

    def features_of(i):
        return (
            feat_ref.at[:, pl.ds(pl.multiple_of(sectors[i] * BLOCK, 128), BLOCK)],
            f_v.at[i],
        )

    loads = [
        pltpu.make_async_copy(src, dst, load_sem.at[n])
        for n, (src, dst) in enumerate(
            (
                (list_ref, list_v),
                (b0_ref, b0_v),
                (bm_ref, bm_v),
                (bo_ref, bo_v),
                (w0_ref, w0_v),
                features_of(0),
                features_of(1),
                (wm_ref, wm_v),
                (wo_ref, wo_v.at[pl.ds(0, OUT)]),
                features_of(2),
                features_of(3),
            )
        )
    ]
    for load in loads:
        load.start()

    barrier = pltpu.get_barrier_semaphore()
    peers = []
    for a in sectors:
        peers.append((blk_of(z, y, 1 - c), a))
    for a in sectors[:3]:
        peers.append((blk, a))
    for d in RING:
        peers.append((blk_of(lax.rem(z + d, NZ), y, c), x))
    for d in RING:
        peers.append((blk_of(z, lax.rem(y + d, NY), c), x))
    for peer in peers:
        pl.semaphore_signal(barrier, inc=1, device_id=peer, device_id_type=MESH)

    pick_v[...] = selector(
        BLOCK, BLOCK, lambda r: (r % NK) * 128 + ((r // NK) & 1) * ROWS + r // (NK * NC)
    )
    wo_v[pl.ds(OUT, LANES - OUT), :] = jnp.zeros((LANES - OUT, HID), BF16)

    for load in loads[:4]:
        load.wait()
    entries = list_v[...].reshape(1, COLS)
    usable = lax.broadcasted_iota(jnp.int32, (1, COLS), 1) < count_ref[0]
    high = jnp.where(usable, entries >> 7, -1)
    high = jnp.broadcast_to(high, (16, COLS)) == lax.broadcasted_iota(jnp.int32, (16, COLS), 0)
    low = jnp.broadcast_to(entries & 127, (128, COLS)) == lax.broadcasted_iota(
        jnp.int32, (128, COLS), 0
    )
    day_v[...] = nt(
        jnp.where(high, 1.0, 0.0).astype(BF16), jnp.where(low, 1.0, 0.0).astype(BF16)
    )
    biases = [column(b0_v[...].reshape(1, HID))]
    biases += [column(bm_v[pl.ds(n, 1), :]) for n in range(2)]
    bias_out = jnp.concatenate([bo_v[...].reshape(1, OUT), jnp.zeros((1, LANES - OUT), F32)], axis=1)
    biases.append(column(bias_out))
    first_half = jnp.where(x < NX // 2, 1.0, 0.0)

    loads[4].wait()
    eye = selector(256, 256, lambda r: r)
    for lo in range(0, HID, 256):
        w0t_v[pl.ds(lo, 256), :] = nt(eye, w0_v[:, pl.ds(lo, 256)]).astype(BF16)

    def network(half, first, count):
        picked, days = [], []
        lanes = pl.ds(first * 128, count * 128)
        for i in (2 * half, 2 * half + 1):
            if first == 0:
                loads[LOADED[i]].wait()
            part = jnp.dot(f_v[i], pick_v[:, lanes], preferred_element_type=F32)
            picked.append(part.astype(BF16))
            day = jnp.concatenate(
                [day_v[pl.ds(sectors[i] * NK + t, 1), :] for t in range(NK)], axis=1
            )
            day = jnp.broadcast_to(jnp.where(day > 0.5, 1.0, 0.0), (16, BLOCK)).astype(BF16)
            days.append(jnp.dot(day, pick_v[:, lanes], preferred_element_type=F32)[:1])
        h, day = jnp.concatenate(picked, axis=1), jnp.concatenate(days, axis=1)
        tiled = [jnp.concatenate([b] * (2 * count), axis=1) for b in biases]
        h = jnp.dot(w0t_v[...], h, preferred_element_type=F32)
        h = leaky(h + tiled[0]).astype(BF16)
        if half == 0 and first == 0:
            loads[7].wait()
        for layer in range(2):
            h = jnp.dot(wm_v[layer], h, preferred_element_type=F32)
            h = leaky(h + tiled[1 + layer]).astype(BF16)
        if half == 0 and first == 0:
            loads[8].wait()
        v = jnp.dot(wo_v[...], h, preferred_element_type=F32) + tiled[3]
        feat = lax.broadcasted_iota(jnp.int32, v.shape, 0)
        v = (jnp.where(feat == OUT, first_half, v) * day).astype(BF16)
        for n in range(2 * count):
            rows = nt(eye[:128, :128], v[:, n * 128 : (n + 1) * 128]).astype(BF16)
            sx[2 * half + n // count, first + n % count] = rows.reshape(NC, ROWS, LANES)

    def send(src, dst, send_sem, recv_sem, device):
        pltpu.make_async_remote_copy(
            src_ref=src,
            dst_ref=dst,
            send_sem=send_sem,
            recv_sem=recv_sem,
            device_id=device,
            device_id_type=MESH,
        ).start()

    def send_x(half, k):
        for i in (2 * half, 2 * half + 1):
            for cc in range(NC) if i < 3 else (1 - c,):
                dst = rx.at[half, k, 2 * (i % 2) + c]
                device = (blk_of(z, y, cc), sectors[i])
                send(sx.at[i, k, cc], dst, sx_sem.at[0], rx_sem.at[half, k], device)
        if half == 1:
            rx[1, k, pl.ds(2 + c, 1)] = sx[3, k, pl.ds(c, 1)]

    def wait_for(view, sem):
        pltpu.make_async_copy(view, view, sem).wait()

    def parts_of(half, k):
        return ((0, 256), (256, 128)) if (half, k) == (1, NK - 1) else ((0, LANES),)

    def stage_x(half, k):
        wait_for(rx.at[half, k, pl.ds(0, 4 - half)], rx_sem.at[half, k])
        sums = [
            (rx[half, k, cc].astype(F32) + rx[half, k, 2 + cc].astype(F32)).reshape(NZ, NY, LANES)
            for cc in range(NC)
        ]
        zs[half, k] = jnp.concatenate(sums, axis=1).astype(BF16)
        for p, (lo, width) in enumerate(parts_of(half, k)):
            lanes = pl.ds(lo, width)
            for d in RING:
                zz = lax.rem(z + d, NZ)
                src, dst = zs.at[half, k, zz, :, lanes], zr.at[half, k, z, :, lanes]
                send(src, dst, zs_sem.at[0], zr_sem.at[half, k, p], (blk_of(zz, y, c), x))
        zr[half, k, pl.ds(z, 1)] = zs[half, k, pl.ds(z, 1)]

    def stage_z(half, k):
        for p, (lo, width) in enumerate(parts_of(half, k)):
            lanes = pl.ds(lo, width)
            wait_for(zr.at[half, k, pl.ds(0, NZ - 1), :, lanes], zr_sem.at[half, k, p])
            rows = zr[half, k, :, :, lanes].reshape(128, width)
            turned = jnp.dot(turn, rows, preferred_element_type=F32)
            ys[half, k, :, :, lanes] = turned.astype(BF16).reshape(NY, 16, width)
            for d in RING:
                yy = lax.rem(y + d, NY)
                src, dst = ys.at[half, k, yy, :, lanes], yr.at[half, k, y, :, lanes]
                send(src, dst, ys_sem.at[0], yr_sem.at[half, k, p], (blk_of(z, yy, c), x))
        yr[half, k, pl.ds(y, 1)] = ys[half, k, pl.ds(y, 1)]

    def stage_y(half):
        near = lax.rem(x + 1 + half, 2)
        total = 0.0
        for k in range(NK):
            place = place_v[pl.ds(k * 128, 128), :]
            for p, (lo, width) in enumerate(parts_of(half, k)):
                lanes = pl.ds(lo, width)
                wait_for(yr.at[half, k, pl.ds(0, NY - 1), :, lanes], yr_sem.at[half, k, p])
                rows = yr[half, k, :, :, lanes].reshape(128, width)
                feats = [
                    nt(eye[:128, :128], rows[:, n : n + 128]).astype(BF16)
                    for n in range(0, width, 128)
                ]
                part = jnp.dot(
                    jnp.concatenate(feats, axis=0), place, preferred_element_type=F32
                )
                if k < NK - 1:
                    total = total + part
                    continue
                t_v[half, lanes] = (total[lo : lo + width] + part).astype(BF16)
                pltpu.make_async_copy(
                    t_v.at[half, lanes], out_ref.at[near, lanes], t_sem.at[half]
                ).start()

    chunks = [(half, k) for half in range(2) for k in range(NK)]
    network(0, 0, 1)
    pl.semaphore_wait(barrier, len(peers))
    send_x(0, 0)
    network(0, 1, 2)
    send_x(0, 1)
    send_x(0, 2)
    turn = selector(128, 128, lambda r: (r & 15) * 8 + (r >> 4))
    network(1, 0, 1)
    send_x(1, 0)
    stage_x(0, 0)
    network(1, 1, 2)
    send_x(1, 1)
    send_x(1, 2)
    place_v[...] = selector(
        BLOCK,
        BLOCK,
        lambda r: (((r >> 1) & 7) * 16 + ((r >> 4) & 7) * 2 + (r & 1)) * NK + (r >> 7),
    )
    for t in range(1, len(chunks) + 1):
        if t < len(chunks):
            stage_x(*chunks[t])
        stage_z(*chunks[t - 1])
    for half in range(2):
        stage_y(half)

    wait_for(sx.at[pl.ds(0, 3)], sx_sem.at[0])
    wait_for(sx.at[3, :, 0], sx_sem.at[0])
    wait_for(zs.at[:, :, pl.ds(0, NZ - 1)], zs_sem.at[0])
    wait_for(ys.at[:, :, pl.ds(0, NY - 1)], ys_sem.at[0])
    for half in range(2):
        wait_for(t_v.at[half], t_sem.at[half])


def spread(t_ref, out_ref, t_v, o_v, t_sem, o_sem):
    pieces = [(n, pl.ds(b * 128, 128)) for n in range(2) for b in range(NK)]
    loads = [
        pltpu.make_async_copy(t_ref.at[n, :, lanes], t_v.at[m], t_sem.at[m])
        for m, (n, lanes) in enumerate(pieces)
    ]
    for load in loads:
        load.start()
    stores = []
    for m, (n, _) in enumerate(pieces):
        loads[m].wait()
        values = t_v[m].astype(F32)
        flag = values[OUT : OUT + 1]
        for far, weight in enumerate((flag, 1.0 - flag)):
            slot = m + 6 * far
            o_v[slot] = (values[:OUT] * weight).astype(BF16)
            store = pltpu.make_async_copy(
                o_v.at[slot], out_ref.at[:, pl.ds(slot * 128, 128)], o_sem.at[slot]
            )
            store.start()
            stores.append(store)
    for store in stores:
        store.wait()


def shards(
    features, daylit_list, daylit_count, in_weight, in_bias, mid_weight, mid_bias, out_weight, out_bias
):
    hbm = pl.BlockSpec(memory_space=pltpu.HBM)
    dma = pltpu.SemaphoreType.DMA
    halves = pl.pallas_call(
        kernel,
        out_shape=jax.ShapeDtypeStruct((2, LANES, BLOCK), BF16),
        in_specs=[pl.BlockSpec(memory_space=pltpu.SMEM)] + [hbm] * 8,
        out_specs=hbm,
        scratch_shapes=[
            pltpu.VMEM((COLS,), jnp.int32),
            pltpu.VMEM((4, FEAT, BLOCK), BF16),
            pltpu.VMEM((FEAT, HID), BF16),
            pltpu.VMEM((HID,), F32),
            pltpu.VMEM((2, HID, HID), BF16),
            pltpu.VMEM((2, HID), F32),
            pltpu.VMEM((LANES, HID), BF16),
            pltpu.VMEM((OUT,), F32),
            pltpu.VMEM((16, 128), F32),
            pltpu.VMEM((HID, FEAT), BF16),
            pltpu.VMEM((BLOCK, BLOCK), BF16),
            pltpu.VMEM((BLOCK, BLOCK), BF16),
            pltpu.VMEM((NX, NK, NC, ROWS, LANES), BF16),
            pltpu.VMEM((2, NK, 4, ROWS, LANES), BF16),
            pltpu.VMEM((2, NK, NZ, 16, LANES), BF16),
            pltpu.VMEM((2, NK, NZ, 16, LANES), BF16),
            pltpu.VMEM((2, NK, NY, 16, LANES), BF16),
            pltpu.VMEM((2, NK, NY, 16, LANES), BF16),
            pltpu.VMEM((2, LANES, BLOCK), BF16),
            dma((11,)),
            dma((1,)),
            dma((2, NK)),
            dma((1,)),
            dma((2, NK, 2)),
            dma((1,)),
            dma((2, NK, 2)),
            dma((2,)),
        ],
        compiler_params=pltpu.CompilerParams(
            collective_id=0, has_side_effects=True, vmem_limit_bytes=VMEM
        ),
    )(
        daylit_count,
        daylit_list,
        features,
        in_weight,
        in_bias,
        mid_weight,
        mid_bias,
        out_weight,
        out_bias,
    )
    return pl.pallas_call(
        spread,
        out_shape=jax.ShapeDtypeStruct((OUT, COLS), BF16),
        in_specs=[hbm],
        out_specs=hbm,
        scratch_shapes=[
            pltpu.VMEM((6, LANES, 128), BF16),
            pltpu.VMEM((12, OUT, 128), BF16),
            dma((6,)),
            dma((12,)),
        ],
        compiler_params=pltpu.CompilerParams(vmem_limit_bytes=VMEM),
    )(halves)


def solution(mesh):
    in_specs = (
        P(None, ("blk", "pair")),
        P(("blk", "pair")),
        P(("blk", "pair")),
        P(),
        P(),
        P(),
        P(),
        P(),
        P(),
    )
    out_specs = P(None, ("blk", "pair"))
    return jax.shard_map(shards, mesh=mesh, in_specs=in_specs, out_specs=out_specs, check_vma=False)
```

```python
import jax
import jax.numpy as jnp
from jax import lax
from jax.experimental import pallas as pl
from jax.experimental.pallas import tpu as pltpu
from jax.sharding import PartitionSpec as P

FEAT, HID, OUT = 557, 512, 368
LANES = 384
NX, NZ, NY, NC, NK = 4, 8, 8, 2, 3
BLOCK = NZ * NY * NC * NK
ROWS = NZ * NY
COLS = NX * BLOCK
OFFSETS = (1, 3, 2, 0)
RING = (4, 3, 5, 2, 6, 1, 7)
VMEM = 62 * 1024 * 1024
LOADED = (5, 6, 9, 10)
BF16, F32 = jnp.bfloat16, jnp.float32
MESH = pl.DeviceIdType.MESH


def nt(a, b):
    return lax.dot_general(a, b, (((1,), (1,)), ((), ())), preferred_element_type=F32)


def leaky(t):
    return jnp.maximum(t, 0.15 * t)


def selector(rows, cols, column_of_row):
    r = lax.broadcasted_iota(jnp.int32, (rows, cols), 0)
    c = lax.broadcasted_iota(jnp.int32, (rows, cols), 1)
    return jnp.where(c == column_of_row(r), 1.0, 0.0).astype(BF16)


def column(row):
    return jnp.transpose(jnp.broadcast_to(row, (128, row.shape[1])))


def kernel(
    count_ref, list_ref, feat_ref, w0_ref, b0_ref, wm_ref, bm_ref, wo_ref, bo_ref, out_ref,
    list_v, f_v, w0_v, b0_v, wm_v, bm_v, wo_v, bo_v, day_v, w0t_v, pick_v, place_v, sx, fx, rx, zs, zr, ys, yr, t_v,
    load_sem, sx_sem, fx_sem, fs_sem, rx_sem, zs_sem, zr_sem, ys_sem, yr_sem, t_sem,
):
    x = lax.axis_index("pair")
    blk = lax.axis_index("blk")
    z, y, c = blk // (NY * NC), (blk // NC) % NY, blk % NC

    def blk_of(zz, yy, cc):
        return (zz * NY + yy) * NC + cc

    sectors = [lax.rem(x + off, NX) for off in OFFSETS]

    def features_of(i):
        return (
            feat_ref.at[:, pl.ds(pl.multiple_of(sectors[i] * BLOCK, 128), BLOCK)],
            f_v.at[i],
        )

    loads = [
        pltpu.make_async_copy(src, dst, load_sem.at[n])
        for n, (src, dst) in enumerate(
            (
                (list_ref, list_v),
                (b0_ref, b0_v),
                (bm_ref, bm_v),
                (bo_ref, bo_v),
                (w0_ref, w0_v),
                features_of(0),
                features_of(1),
                (wm_ref, wm_v),
                (wo_ref, wo_v.at[pl.ds(0, OUT)]),
                features_of(2),
                features_of(3),
            )
        )
    ]
    for load in loads:
        load.start()

    barrier = pltpu.get_barrier_semaphore()
    peers = []
    for a in (*sectors[:2], x):
        peers.append((blk_of(z, y, 1 - c), a))
    for a in sectors[:2]:
        peers.append((blk, a))
    for d in RING:
        peers.append((blk_of(lax.rem(z + d, NZ), y, c), x))
    for d in RING:
        peers.append((blk_of(z, lax.rem(y + d, NY), c), x))
    for peer in peers:
        pl.semaphore_signal(barrier, inc=1, device_id=peer, device_id_type=MESH)

    pick_v[...] = selector(
        BLOCK, BLOCK, lambda r: (r % NK) * 128 + ((r // NK) & 1) * ROWS + r // (NK * NC)
    )
    wo_v[pl.ds(OUT, LANES - OUT), :] = jnp.zeros((LANES - OUT, HID), BF16)

    for load in loads[:4]:
        load.wait()
    entries = list_v[...].reshape(1, COLS)
    usable = lax.broadcasted_iota(jnp.int32, (1, COLS), 1) < count_ref[0]
    high = jnp.where(usable, entries >> 7, -1)
    high = jnp.broadcast_to(high, (16, COLS)) == lax.broadcasted_iota(jnp.int32, (16, COLS), 0)
    low = jnp.broadcast_to(entries & 127, (128, COLS)) == lax.broadcasted_iota(
        jnp.int32, (128, COLS), 0
    )
    day_v[...] = nt(
        jnp.where(high, 1.0, 0.0).astype(BF16), jnp.where(low, 1.0, 0.0).astype(BF16)
    )
    biases = [column(b0_v[...].reshape(1, HID))]
    biases += [column(bm_v[pl.ds(n, 1), :]) for n in range(2)]
    bias_out = jnp.concatenate([bo_v[...].reshape(1, OUT), jnp.zeros((1, LANES - OUT), F32)], axis=1)
    biases.append(column(bias_out))
    first_half = jnp.where(x < NX // 2, 1.0, 0.0)

    loads[4].wait()
    eye = selector(256, 256, lambda r: r)
    for lo in range(0, HID, 256):
        w0t_v[pl.ds(lo, 256), :] = nt(eye, w0_v[:, pl.ds(lo, 256)]).astype(BF16)

    def network(slots, first, count):
        picked, days = [], []
        lanes = pl.ds(first * 128, count * 128)
        for i in slots:
            if first == 0:
                loads[LOADED[i]].wait()
            part = jnp.dot(f_v[i], pick_v[:, lanes], preferred_element_type=F32)
            picked.append(part.astype(BF16))
            day = jnp.concatenate(
                [day_v[pl.ds(sectors[i] * NK + t, 1), :] for t in range(NK)], axis=1
            )
            day = jnp.broadcast_to(jnp.where(day > 0.5, 1.0, 0.0), (16, BLOCK)).astype(BF16)
            days.append(jnp.dot(day, pick_v[:, lanes], preferred_element_type=F32)[:1])
        h, day = jnp.concatenate(picked, axis=1), jnp.concatenate(days, axis=1)
        tiled = [jnp.concatenate([b] * (len(slots) * count), axis=1) for b in biases]
        h = jnp.dot(w0t_v[...], h, preferred_element_type=F32)
        h = leaky(h + tiled[0]).astype(BF16)
        if 0 in slots and first == 0:
            loads[7].wait()
        for layer in range(2):
            h = jnp.dot(wm_v[layer], h, preferred_element_type=F32)
            h = leaky(h + tiled[1 + layer]).astype(BF16)
        if 0 in slots and first == 0:
            loads[8].wait()
        v = jnp.dot(wo_v[...], h, preferred_element_type=F32) + tiled[3]
        feat = lax.broadcasted_iota(jnp.int32, v.shape, 0)
        v = (jnp.where(feat == OUT, first_half, v) * day).astype(BF16)
        for n in range(len(slots) * count):
            rows = nt(eye[:128, :128], v[:, n * 128 : (n + 1) * 128]).astype(BF16)
            sx[slots[n // count], first + n % count] = rows.reshape(NC, ROWS, LANES)

    def send(src, dst, send_sem, recv_sem, device):
        pltpu.make_async_remote_copy(
            src_ref=src,
            dst_ref=dst,
            send_sem=send_sem,
            recv_sem=recv_sem,
            device_id=device,
            device_id_type=MESH,
        ).start()

    def send_near(k):
        for i in range(2):
            for cc in range(NC):
                dst = rx.at[0, k, 2 * i + c]
                device = (blk_of(z, y, cc), sectors[i])
                send(sx.at[i, k, cc], dst, sx_sem.at[0], rx_sem.at[0, k], device)

    def send_far(k):
        for cc in range(NC):
            device = (blk, sectors[cc])
            send(sx.at[2, k, cc], fx.at[k, cc], sx_sem.at[0], fx_sem.at[k, cc], device)

    def forward(k):
        for cc in range(NC):
            wait_for(fx.at[k, cc], fx_sem.at[k, cc])
            device = (blk_of(z, y, cc), sectors[cc])
            send(fx.at[k, cc], rx.at[1, k, c], fs_sem.at[0], rx_sem.at[1, k], device)

    def send_own(k):
        device = (blk_of(z, y, 1 - c), x)
        send(sx.at[3, k, 1 - c], rx.at[1, k, 2 + c], sx_sem.at[0], rx_sem.at[1, k], device)
        rx[1, k, pl.ds(2 + c, 1)] = sx[3, k, pl.ds(c, 1)]

    def wait_for(view, sem):
        pltpu.make_async_copy(view, view, sem).wait()

    def parts_of(half, k):
        return ((0, 256), (256, 128)) if (half, k) == (1, NK - 1) else ((0, LANES),)

    def stage_x(half, k):
        wait_for(rx.at[half, k, pl.ds(0, 4 - half)], rx_sem.at[half, k])
        sums = [
            (rx[half, k, cc].astype(F32) + rx[half, k, 2 + cc].astype(F32)).reshape(NZ, NY, LANES)
            for cc in range(NC)
        ]
        zs[half, k] = jnp.concatenate(sums, axis=1).astype(BF16)
        for p, (lo, width) in enumerate(parts_of(half, k)):
            lanes = pl.ds(lo, width)
            for d in RING:
                zz = lax.rem(z + d, NZ)
                src, dst = zs.at[half, k, zz, :, lanes], zr.at[half, k, z, :, lanes]
                send(src, dst, zs_sem.at[0], zr_sem.at[half, k, p], (blk_of(zz, y, c), x))
        zr[half, k, pl.ds(z, 1)] = zs[half, k, pl.ds(z, 1)]

    def stage_z(half, k):
        for p, (lo, width) in enumerate(parts_of(half, k)):
            lanes = pl.ds(lo, width)
            wait_for(zr.at[half, k, pl.ds(0, NZ - 1), :, lanes], zr_sem.at[half, k, p])
            rows = zr[half, k, :, :, lanes].reshape(128, width)
            turned = jnp.dot(turn, rows, preferred_element_type=F32)
            ys[half, k, :, :, lanes] = turned.astype(BF16).reshape(NY, 16, width)
            for d in RING:
                yy = lax.rem(y + d, NY)
                src, dst = ys.at[half, k, yy, :, lanes], yr.at[half, k, y, :, lanes]
                send(src, dst, ys_sem.at[0], yr_sem.at[half, k, p], (blk_of(z, yy, c), x))
        yr[half, k, pl.ds(y, 1)] = ys[half, k, pl.ds(y, 1)]

    def stage_y(half):
        near = lax.rem(x + 1 + half, 2)
        total = 0.0
        for k in range(NK):
            place = place_v[pl.ds(k * 128, 128), :]
            for p, (lo, width) in enumerate(parts_of(half, k)):
                lanes = pl.ds(lo, width)
                wait_for(yr.at[half, k, pl.ds(0, NY - 1), :, lanes], yr_sem.at[half, k, p])
                rows = yr[half, k, :, :, lanes].reshape(128, width)
                feats = [
                    nt(eye[:128, :128], rows[:, n : n + 128]).astype(BF16)
                    for n in range(0, width, 128)
                ]
                part = jnp.dot(
                    jnp.concatenate(feats, axis=0), place, preferred_element_type=F32
                )
                if k < NK - 1:
                    total = total + part
                    continue
                t_v[half, lanes] = (total[lo : lo + width] + part).astype(BF16)
                pltpu.make_async_copy(
                    t_v.at[half, lanes], out_ref.at[near, lanes], t_sem.at[half]
                ).start()

    chunks = [(half, k) for half in range(2) for k in range(NK)]
    network((0, 1), 0, 1)
    pl.semaphore_wait(barrier, len(peers))
    send_near(0)
    network((2,), 0, NK)
    for k in range(NK):
        send_far(k)
    network((0, 1), 1, 2)
    send_near(1)
    send_near(2)
    turn = selector(128, 128, lambda r: (r & 15) * 8 + (r >> 4))
    stage_x(0, 0)
    forward(0)
    network((3,), 0, NK)
    for k in range(NK):
        send_own(k)
    forward(1)
    forward(2)
    place_v[...] = selector(
        BLOCK,
        BLOCK,
        lambda r: (((r >> 1) & 7) * 16 + ((r >> 4) & 7) * 2 + (r & 1)) * NK + (r >> 7),
    )
    for t in range(1, len(chunks) + 1):
        if t < len(chunks):
            stage_x(*chunks[t])
        stage_z(*chunks[t - 1])
    for half in range(2):
        stage_y(half)

    wait_for(sx.at[pl.ds(0, 3)], sx_sem.at[0])
    wait_for(sx.at[3, :, 0], sx_sem.at[0])
    wait_for(fx, fs_sem.at[0])
    wait_for(zs.at[:, :, pl.ds(0, NZ - 1)], zs_sem.at[0])
    wait_for(ys.at[:, :, pl.ds(0, NY - 1)], ys_sem.at[0])
    for half in range(2):
        wait_for(t_v.at[half], t_sem.at[half])


def spread(t_ref, out_ref, t_v, o_v, t_sem, o_sem):
    pieces = [(n, pl.ds(b * 128, 128)) for n in range(2) for b in range(NK)]
    loads = [
        pltpu.make_async_copy(t_ref.at[n, :, lanes], t_v.at[m], t_sem.at[m])
        for m, (n, lanes) in enumerate(pieces)
    ]
    for load in loads:
        load.start()
    stores = []
    for m, (n, _) in enumerate(pieces):
        loads[m].wait()
        values = t_v[m].astype(F32)
        flag = values[OUT : OUT + 1]
        for far, weight in enumerate((flag, 1.0 - flag)):
            slot = m + 6 * far
            o_v[slot] = (values[:OUT] * weight).astype(BF16)
            store = pltpu.make_async_copy(
                o_v.at[slot], out_ref.at[:, pl.ds(slot * 128, 128)], o_sem.at[slot]
            )
            store.start()
            stores.append(store)
    for store in stores:
        store.wait()


def shards(
    features, daylit_list, daylit_count, in_weight, in_bias, mid_weight, mid_bias, out_weight, out_bias
):
    hbm = pl.BlockSpec(memory_space=pltpu.HBM)
    dma = pltpu.SemaphoreType.DMA
    halves = pl.pallas_call(
        kernel,
        out_shape=jax.ShapeDtypeStruct((2, LANES, BLOCK), BF16),
        in_specs=[pl.BlockSpec(memory_space=pltpu.SMEM)] + [hbm] * 8,
        out_specs=hbm,
        scratch_shapes=[
            pltpu.VMEM((COLS,), jnp.int32),
            pltpu.VMEM((4, FEAT, BLOCK), BF16),
            pltpu.VMEM((FEAT, HID), BF16),
            pltpu.VMEM((HID,), F32),
            pltpu.VMEM((2, HID, HID), BF16),
            pltpu.VMEM((2, HID), F32),
            pltpu.VMEM((LANES, HID), BF16),
            pltpu.VMEM((OUT,), F32),
            pltpu.VMEM((16, 128), F32),
            pltpu.VMEM((HID, FEAT), BF16),
            pltpu.VMEM((BLOCK, BLOCK), BF16),
            pltpu.VMEM((BLOCK, BLOCK), BF16),
            pltpu.VMEM((NX, NK, NC, ROWS, LANES), BF16),
            pltpu.VMEM((NK, NC, ROWS, LANES), BF16),
            pltpu.VMEM((2, NK, 4, ROWS, LANES), BF16),
            pltpu.VMEM((2, NK, NZ, 16, LANES), BF16),
            pltpu.VMEM((2, NK, NZ, 16, LANES), BF16),
            pltpu.VMEM((2, NK, NY, 16, LANES), BF16),
            pltpu.VMEM((2, NK, NY, 16, LANES), BF16),
            pltpu.VMEM((2, LANES, BLOCK), BF16),
            dma((11,)),
            dma((1,)),
            dma((NK, NC)),
            dma((1,)),
            dma((2, NK)),
            dma((1,)),
            dma((2, NK, 2)),
            dma((1,)),
            dma((2, NK, 2)),
            dma((2,)),
        ],
        compiler_params=pltpu.CompilerParams(
            collective_id=0, has_side_effects=True, vmem_limit_bytes=VMEM
        ),
    )(
        daylit_count,
        daylit_list,
        features,
        in_weight,
        in_bias,
        mid_weight,
        mid_bias,
        out_weight,
        out_bias,
    )
    return pl.pallas_call(
        spread,
        out_shape=jax.ShapeDtypeStruct((OUT, COLS), BF16),
        in_specs=[hbm],
        out_specs=hbm,
        scratch_shapes=[
            pltpu.VMEM((6, LANES, 128), BF16),
            pltpu.VMEM((12, OUT, 128), BF16),
            dma((6,)),
            dma((12,)),
        ],
        compiler_params=pltpu.CompilerParams(vmem_limit_bytes=VMEM),
    )(halves)


def solution(mesh):
    in_specs = (
        P(None, ("blk", "pair")),
        P(("blk", "pair")),
        P(("blk", "pair")),
        P(),
        P(),
        P(),
        P(),
        P(),
        P(),
    )
    out_specs = P(None, ("blk", "pair"))
    return jax.shard_map(shards, mesh=mesh, in_specs=in_specs, out_specs=out_specs, check_vma=False)
```

```python
import jax
import jax.numpy as jnp
from jax import lax
from jax.experimental import pallas as pl
from jax.experimental.pallas import tpu as pltpu
from jax.sharding import PartitionSpec as P

FEAT, HID, OUT = 557, 512, 368
LANES = 384
NX, NZ, NY, NC, NK = 4, 8, 8, 2, 3
BLOCK = NZ * NY * NC * NK
ROWS = NZ * NY
COLS = NX * BLOCK
OFFSETS = (1, 3, 2, 0)
RING = (4, 3, 5, 2, 6, 1, 7)
VMEM = 62 * 1024 * 1024
LOADED = (5, 6, 9, 10)
BF16, F32 = jnp.bfloat16, jnp.float32
MESH = pl.DeviceIdType.MESH


def nt(a, b):
    return lax.dot_general(a, b, (((1,), (1,)), ((), ())), preferred_element_type=F32)


def leaky(t):
    return jnp.maximum(t, 0.15 * t)


def selector(rows, cols, column_of_row):
    r = lax.broadcasted_iota(jnp.int32, (rows, cols), 0)
    c = lax.broadcasted_iota(jnp.int32, (rows, cols), 1)
    return jnp.where(c == column_of_row(r), 1.0, 0.0).astype(BF16)


def column(row):
    return jnp.transpose(jnp.broadcast_to(row, (128, row.shape[1])))


def kernel(
    count_ref, list_ref, feat_ref, w0_ref, b0_ref, wm_ref, bm_ref, wo_ref, bo_ref, out_ref,
    list_v, f_v, w0_v, b0_v, wm_v, bm_v, wo_v, bo_v, day_v, w0t_v, pick_v, place_v, sx, rx, zs, zr, ys, yr, t_v,
    load_sem, sx_sem, rx_sem, zs_sem, zr_sem, ys_sem, yr_sem, t_sem,
):
    x = lax.axis_index("pair")
    blk = lax.axis_index("blk")
    z, y, c = blk // (NY * NC), (blk // NC) % NY, blk % NC

    def blk_of(zz, yy, cc):
        return (zz * NY + yy) * NC + cc

    sectors = [lax.rem(x + off, NX) for off in OFFSETS]

    def features_of(i):
        return (
            feat_ref.at[:, pl.ds(pl.multiple_of(sectors[i] * BLOCK, 128), BLOCK)],
            f_v.at[i],
        )

    loads = [
        pltpu.make_async_copy(src, dst, load_sem.at[n])
        for n, (src, dst) in enumerate(
            (
                (list_ref, list_v),
                (b0_ref, b0_v),
                (bm_ref, bm_v),
                (bo_ref, bo_v),
                (w0_ref, w0_v),
                features_of(0),
                features_of(1),
                (wm_ref, wm_v),
                (wo_ref, wo_v.at[pl.ds(0, OUT)]),
                features_of(2),
                features_of(3),
            )
        )
    ]
    for load in loads:
        load.start()

    barrier = pltpu.get_barrier_semaphore()
    peers = []
    for a in sectors:
        peers.append((blk_of(z, y, 1 - c), a))
    for a in sectors[:3]:
        peers.append((blk, a))
    for d in RING:
        peers.append((blk_of(lax.rem(z + d, NZ), y, c), x))
    for d in RING:
        peers.append((blk_of(z, lax.rem(y + d, NY), c), x))
    for peer in peers:
        pl.semaphore_signal(barrier, inc=1, device_id=peer, device_id_type=MESH)

    pick_v[...] = selector(
        BLOCK, BLOCK, lambda r: (r % NK) * 128 + ((r // NK) & 1) * ROWS + r // (NK * NC)
    )
    wo_v[pl.ds(OUT, LANES - OUT), :] = jnp.zeros((LANES - OUT, HID), BF16)

    for load in loads[:4]:
        load.wait()
    entries = list_v[...].reshape(1, COLS)
    usable = lax.broadcasted_iota(jnp.int32, (1, COLS), 1) < count_ref[0]
    high = jnp.where(usable, entries >> 7, -1)
    high = jnp.broadcast_to(high, (16, COLS)) == lax.broadcasted_iota(jnp.int32, (16, COLS), 0)
    low = jnp.broadcast_to(entries & 127, (128, COLS)) == lax.broadcasted_iota(
        jnp.int32, (128, COLS), 0
    )
    day_v[...] = nt(
        jnp.where(high, 1.0, 0.0).astype(BF16), jnp.where(low, 1.0, 0.0).astype(BF16)
    )
    biases = [column(b0_v[...].reshape(1, HID))]
    biases += [column(bm_v[pl.ds(n, 1), :]) for n in range(2)]
    bias_out = jnp.concatenate([bo_v[...].reshape(1, OUT), jnp.zeros((1, LANES - OUT), F32)], axis=1)
    biases.append(column(bias_out))
    first_half = jnp.where(x < NX // 2, 1.0, 0.0)

    loads[4].wait()
    eye = selector(256, 256, lambda r: r)
    for lo in range(0, HID, 256):
        w0t_v[pl.ds(lo, 256), :] = nt(eye, w0_v[:, pl.ds(lo, 256)]).astype(BF16)

    def network(slots, first, count):
        picked, days = [], []
        lanes = pl.ds(first * 128, count * 128)
        for i in slots:
            if first == 0:
                loads[LOADED[i]].wait()
            part = jnp.dot(f_v[i], pick_v[:, lanes], preferred_element_type=F32)
            picked.append(part.astype(BF16))
            day = jnp.concatenate(
                [day_v[pl.ds(sectors[i] * NK + t, 1), :] for t in range(NK)], axis=1
            )
            day = jnp.broadcast_to(jnp.where(day > 0.5, 1.0, 0.0), (16, BLOCK)).astype(BF16)
            days.append(jnp.dot(day, pick_v[:, lanes], preferred_element_type=F32)[:1])
        h, day = jnp.concatenate(picked, axis=1), jnp.concatenate(days, axis=1)
        tiled = [jnp.concatenate([b] * (len(slots) * count), axis=1) for b in biases]
        h = jnp.dot(w0t_v[...], h, preferred_element_type=F32)
        h = leaky(h + tiled[0]).astype(BF16)
        if 0 in slots and first == 0:
            loads[7].wait()
        for layer in range(2):
            h = jnp.dot(wm_v[layer], h, preferred_element_type=F32)
            h = leaky(h + tiled[1 + layer]).astype(BF16)
        if 0 in slots and first == 0:
            loads[8].wait()
        v = jnp.dot(wo_v[...], h, preferred_element_type=F32) + tiled[3]
        feat = lax.broadcasted_iota(jnp.int32, v.shape, 0)
        v = (jnp.where(feat == OUT, first_half, v) * day).astype(BF16)
        for n in range(len(slots) * count):
            rows = nt(eye[:128, :128], v[:, n * 128 : (n + 1) * 128]).astype(BF16)
            sx[slots[n // count], first + n % count] = rows.reshape(NC, ROWS, LANES)

    def send(src, dst, send_sem, recv_sem, device):
        pltpu.make_async_remote_copy(
            src_ref=src,
            dst_ref=dst,
            send_sem=send_sem,
            recv_sem=recv_sem,
            device_id=device,
            device_id_type=MESH,
        ).start()

    def send_near(k):
        for i in range(2):
            for cc in range(NC):
                dst = rx.at[0, k, 2 * i + c]
                device = (blk_of(z, y, cc), sectors[i])
                send(sx.at[i, k, cc], dst, sx_sem.at[0], rx_sem.at[0, k], device)

    def send_far(k):
        for cc in range(NC):
            device = (blk_of(z, y, cc), sectors[2])
            send(sx.at[2, k, cc], rx.at[1, k, c], sx_sem.at[0], rx_sem.at[1, k], device)

    def send_own(k):
        device = (blk_of(z, y, 1 - c), x)
        send(sx.at[3, k, 1 - c], rx.at[1, k, 2 + c], sx_sem.at[0], rx_sem.at[1, k], device)
        rx[1, k, pl.ds(2 + c, 1)] = sx[3, k, pl.ds(c, 1)]

    def wait_for(view, sem):
        pltpu.make_async_copy(view, view, sem).wait()

    def parts_of(half, k):
        return ((0, 256), (256, 128)) if (half, k) == (1, NK - 1) else ((0, LANES),)

    def stage_x(half, k):
        wait_for(rx.at[half, k, pl.ds(0, 4 - half)], rx_sem.at[half, k])
        sums = [
            (rx[half, k, cc].astype(F32) + rx[half, k, 2 + cc].astype(F32)).reshape(NZ, NY, LANES)
            for cc in range(NC)
        ]
        zs[half, k] = jnp.concatenate(sums, axis=1).astype(BF16)
        for p, (lo, width) in enumerate(parts_of(half, k)):
            lanes = pl.ds(lo, width)
            for d in RING:
                zz = lax.rem(z + d, NZ)
                src, dst = zs.at[half, k, zz, :, lanes], zr.at[half, k, z, :, lanes]
                send(src, dst, zs_sem.at[0], zr_sem.at[half, k, p], (blk_of(zz, y, c), x))
        zr[half, k, pl.ds(z, 1)] = zs[half, k, pl.ds(z, 1)]

    def stage_z(half, k):
        for p, (lo, width) in enumerate(parts_of(half, k)):
            lanes = pl.ds(lo, width)
            wait_for(zr.at[half, k, pl.ds(0, NZ - 1), :, lanes], zr_sem.at[half, k, p])
            rows = zr[half, k, :, :, lanes].reshape(128, width)
            turned = jnp.dot(turn, rows, preferred_element_type=F32)
            ys[half, k, :, :, lanes] = turned.astype(BF16).reshape(NY, 16, width)
            for d in RING:
                yy = lax.rem(y + d, NY)
                src, dst = ys.at[half, k, yy, :, lanes], yr.at[half, k, y, :, lanes]
                send(src, dst, ys_sem.at[0], yr_sem.at[half, k, p], (blk_of(z, yy, c), x))
        yr[half, k, pl.ds(y, 1)] = ys[half, k, pl.ds(y, 1)]

    def stage_y(half):
        near = lax.rem(x + 1 + half, 2)
        total = 0.0
        for k in range(NK):
            place = place_v[pl.ds(k * 128, 128), :]
            for p, (lo, width) in enumerate(parts_of(half, k)):
                lanes = pl.ds(lo, width)
                wait_for(yr.at[half, k, pl.ds(0, NY - 1), :, lanes], yr_sem.at[half, k, p])
                rows = yr[half, k, :, :, lanes].reshape(128, width)
                feats = [
                    nt(eye[:128, :128], rows[:, n : n + 128]).astype(BF16)
                    for n in range(0, width, 128)
                ]
                part = jnp.dot(
                    jnp.concatenate(feats, axis=0), place, preferred_element_type=F32
                )
                if k < NK - 1:
                    total = total + part
                    continue
                t_v[half, lanes] = (total[lo : lo + width] + part).astype(BF16)
                pltpu.make_async_copy(
                    t_v.at[half, lanes], out_ref.at[near, lanes], t_sem.at[half]
                ).start()

    chunks = [(half, k) for half in range(2) for k in range(NK)]
    network((0, 1), 0, 1)
    pl.semaphore_wait(barrier, len(peers))
    send_near(0)
    network((2,), 0, NK)
    for k in range(NK):
        send_far(k)
    network((0, 1), 1, 2)
    send_near(1)
    send_near(2)
    turn = selector(128, 128, lambda r: (r & 15) * 8 + (r >> 4))
    stage_x(0, 0)
    network((3,), 0, NK)
    for k in range(NK):
        send_own(k)
    place_v[...] = selector(
        BLOCK,
        BLOCK,
        lambda r: (((r >> 1) & 7) * 16 + ((r >> 4) & 7) * 2 + (r & 1)) * NK + (r >> 7),
    )
    for t in range(1, len(chunks) + 1):
        if t < len(chunks):
            stage_x(*chunks[t])
        stage_z(*chunks[t - 1])
    for half in range(2):
        stage_y(half)

    wait_for(sx.at[pl.ds(0, 3)], sx_sem.at[0])
    wait_for(sx.at[3, :, 0], sx_sem.at[0])
    wait_for(zs.at[:, :, pl.ds(0, NZ - 1)], zs_sem.at[0])
    wait_for(ys.at[:, :, pl.ds(0, NY - 1)], ys_sem.at[0])
    for half in range(2):
        wait_for(t_v.at[half], t_sem.at[half])


def spread(t_ref, out_ref, t_v, o_v, t_sem, o_sem):
    pieces = [(n, pl.ds(b * 128, 128)) for n in range(2) for b in range(NK)]
    loads = [
        pltpu.make_async_copy(t_ref.at[n, :, lanes], t_v.at[m], t_sem.at[m])
        for m, (n, lanes) in enumerate(pieces)
    ]
    for load in loads:
        load.start()
    stores = []
    for m, (n, _) in enumerate(pieces):
        loads[m].wait()
        values = t_v[m].astype(F32)
        flag = values[OUT : OUT + 1]
        for far, weight in enumerate((flag, 1.0 - flag)):
            slot = m + 6 * far
            o_v[slot] = (values[:OUT] * weight).astype(BF16)
            store = pltpu.make_async_copy(
                o_v.at[slot], out_ref.at[:, pl.ds(slot * 128, 128)], o_sem.at[slot]
            )
            store.start()
            stores.append(store)
    for store in stores:
        store.wait()


def shards(
    features, daylit_list, daylit_count, in_weight, in_bias, mid_weight, mid_bias, out_weight, out_bias
):
    hbm = pl.BlockSpec(memory_space=pltpu.HBM)
    dma = pltpu.SemaphoreType.DMA
    halves = pl.pallas_call(
        kernel,
        out_shape=jax.ShapeDtypeStruct((2, LANES, BLOCK), BF16),
        in_specs=[pl.BlockSpec(memory_space=pltpu.SMEM)] + [hbm] * 8,
        out_specs=hbm,
        scratch_shapes=[
            pltpu.VMEM((COLS,), jnp.int32),
            pltpu.VMEM((4, FEAT, BLOCK), BF16),
            pltpu.VMEM((FEAT, HID), BF16),
            pltpu.VMEM((HID,), F32),
            pltpu.VMEM((2, HID, HID), BF16),
            pltpu.VMEM((2, HID), F32),
            pltpu.VMEM((LANES, HID), BF16),
            pltpu.VMEM((OUT,), F32),
            pltpu.VMEM((16, 128), F32),
            pltpu.VMEM((HID, FEAT), BF16),
            pltpu.VMEM((BLOCK, BLOCK), BF16),
            pltpu.VMEM((BLOCK, BLOCK), BF16),
            pltpu.VMEM((NX, NK, NC, ROWS, LANES), BF16),
            pltpu.VMEM((2, NK, 4, ROWS, LANES), BF16),
            pltpu.VMEM((2, NK, NZ, 16, LANES), BF16),
            pltpu.VMEM((2, NK, NZ, 16, LANES), BF16),
            pltpu.VMEM((2, NK, NY, 16, LANES), BF16),
            pltpu.VMEM((2, NK, NY, 16, LANES), BF16),
            pltpu.VMEM((2, LANES, BLOCK), BF16),
            dma((11,)),
            dma((1,)),
            dma((2, NK)),
            dma((1,)),
            dma((2, NK, 2)),
            dma((1,)),
            dma((2, NK, 2)),
            dma((2,)),
        ],
        compiler_params=pltpu.CompilerParams(
            collective_id=0, has_side_effects=True, vmem_limit_bytes=VMEM
        ),
    )(
        daylit_count,
        daylit_list,
        features,
        in_weight,
        in_bias,
        mid_weight,
        mid_bias,
        out_weight,
        out_bias,
    )
    return pl.pallas_call(
        spread,
        out_shape=jax.ShapeDtypeStruct((OUT, COLS), BF16),
        in_specs=[hbm],
        out_specs=hbm,
        scratch_shapes=[
            pltpu.VMEM((6, LANES, 128), BF16),
            pltpu.VMEM((12, OUT, 128), BF16),
            dma((6,)),
            dma((12,)),
        ],
        compiler_params=pltpu.CompilerParams(vmem_limit_bytes=VMEM),
    )(halves)


def solution(mesh):
    in_specs = (
        P(None, ("blk", "pair")),
        P(("blk", "pair")),
        P(("blk", "pair")),
        P(),
        P(),
        P(),
        P(),
        P(),
        P(),
    )
    out_specs = P(None, ("blk", "pair"))
    return jax.shard_map(shards, mesh=mesh, in_specs=in_specs, out_specs=out_specs, check_vma=False)
```

```python
import jax
import jax.numpy as jnp
from jax import lax
from jax.experimental import pallas as pl
from jax.experimental.pallas import tpu as pltpu
from jax.sharding import PartitionSpec as P

FEAT, HID, OUT = 557, 512, 368
LANES = 384
NX, NZ, NY, NC, NK = 4, 8, 8, 2, 3
BLOCK = NZ * NY * NC * NK
ROWS = NZ * NY
COLS = NX * BLOCK
OFFSETS = (1, 3, 2, 0)
RING = (4, 3, 5, 2, 6, 1, 7)
VMEM = 62 * 1024 * 1024
LOADED = (5, 6, 9, 10)
BF16, F32 = jnp.bfloat16, jnp.float32
MESH = pl.DeviceIdType.MESH


def nt(a, b):
    return lax.dot_general(a, b, (((1,), (1,)), ((), ())), preferred_element_type=F32)


def leaky(t):
    return jnp.maximum(t, 0.15 * t)


def selector(rows, cols, column_of_row):
    r = lax.broadcasted_iota(jnp.int32, (rows, cols), 0)
    c = lax.broadcasted_iota(jnp.int32, (rows, cols), 1)
    return jnp.where(c == column_of_row(r), 1.0, 0.0).astype(BF16)


def column(row):
    return jnp.transpose(jnp.broadcast_to(row, (128, row.shape[1])))


def kernel(
    count_ref, list_ref, feat_ref, w0_ref, b0_ref, wm_ref, bm_ref, wo_ref, bo_ref, out_ref,
    list_v, f_v, w0_v, b0_v, wm_v, bm_v, wo_v, bo_v, day_v, w0t_v, pick_v, place_v, sx, fx, rx, zs, zr, ys, yr, t_v,
    load_sem, sx_sem, fx_sem, fs_sem, rx_sem, zs_sem, zr_sem, ys_sem, yr_sem, t_sem,
):
    x = lax.axis_index("pair")
    blk = lax.axis_index("blk")
    z, y, c = blk // (NY * NC), (blk // NC) % NY, blk % NC

    def blk_of(zz, yy, cc):
        return (zz * NY + yy) * NC + cc

    sectors = [lax.rem(x + off, NX) for off in OFFSETS]

    def features_of(i):
        return (
            feat_ref.at[:, pl.ds(pl.multiple_of(sectors[i] * BLOCK, 128), BLOCK)],
            f_v.at[i],
        )

    loads = [
        pltpu.make_async_copy(src, dst, load_sem.at[n])
        for n, (src, dst) in enumerate(
            (
                (list_ref, list_v),
                (b0_ref, b0_v),
                (bm_ref, bm_v),
                (bo_ref, bo_v),
                (w0_ref, w0_v),
                features_of(0),
                features_of(1),
                (wm_ref, wm_v),
                (wo_ref, wo_v.at[pl.ds(0, OUT)]),
                features_of(2),
                features_of(3),
            )
        )
    ]
    for load in loads:
        load.start()

    barrier = pltpu.get_barrier_semaphore()
    peers = []
    for a in (*sectors[:2], x):
        peers.append((blk_of(z, y, 1 - c), a))
    for a in sectors[:2]:
        peers.append((blk, a))
    for d in RING:
        peers.append((blk_of(lax.rem(z + d, NZ), y, c), x))
    for d in RING:
        peers.append((blk_of(z, lax.rem(y + d, NY), c), x))
    for peer in peers:
        pl.semaphore_signal(barrier, inc=1, device_id=peer, device_id_type=MESH)

    pick_v[...] = selector(
        BLOCK, BLOCK, lambda r: (r % NK) * 128 + ((r // NK) & 1) * ROWS + r // (NK * NC)
    )
    wo_v[pl.ds(OUT, LANES - OUT), :] = jnp.zeros((LANES - OUT, HID), BF16)

    for load in loads[:4]:
        load.wait()
    entries = list_v[...].reshape(1, COLS)
    usable = lax.broadcasted_iota(jnp.int32, (1, COLS), 1) < count_ref[0]
    high = jnp.where(usable, entries >> 7, -1)
    high = jnp.broadcast_to(high, (16, COLS)) == lax.broadcasted_iota(jnp.int32, (16, COLS), 0)
    low = jnp.broadcast_to(entries & 127, (128, COLS)) == lax.broadcasted_iota(
        jnp.int32, (128, COLS), 0
    )
    day_v[...] = nt(
        jnp.where(high, 1.0, 0.0).astype(BF16), jnp.where(low, 1.0, 0.0).astype(BF16)
    )
    biases = [column(b0_v[...].reshape(1, HID))]
    biases += [column(bm_v[pl.ds(n, 1), :]) for n in range(2)]
    bias_out = jnp.concatenate([bo_v[...].reshape(1, OUT), jnp.zeros((1, LANES - OUT), F32)], axis=1)
    biases.append(column(bias_out))
    first_half = jnp.where(x < NX // 2, 1.0, 0.0)

    loads[4].wait()
    eye = selector(256, 256, lambda r: r)
    for lo in range(0, HID, 256):
        w0t_v[pl.ds(lo, 256), :] = nt(eye, w0_v[:, pl.ds(lo, 256)]).astype(BF16)

    def network(slots, first, count):
        picked, days = [], []
        lanes = pl.ds(first * 128, count * 128)
        for i in slots:
            if first == 0:
                loads[LOADED[i]].wait()
            part = jnp.dot(f_v[i], pick_v[:, lanes], preferred_element_type=F32)
            picked.append(part.astype(BF16))
            day = jnp.concatenate(
                [day_v[pl.ds(sectors[i] * NK + t, 1), :] for t in range(NK)], axis=1
            )
            day = jnp.broadcast_to(jnp.where(day > 0.5, 1.0, 0.0), (16, BLOCK)).astype(BF16)
            days.append(jnp.dot(day, pick_v[:, lanes], preferred_element_type=F32)[:1])
        h, day = jnp.concatenate(picked, axis=1), jnp.concatenate(days, axis=1)
        tiled = [jnp.concatenate([b] * (len(slots) * count), axis=1) for b in biases]
        h = jnp.dot(w0t_v[...], h, preferred_element_type=F32)
        h = leaky(h + tiled[0]).astype(BF16)
        if 0 in slots and first == 0:
            loads[7].wait()
        for layer in range(2):
            h = jnp.dot(wm_v[layer], h, preferred_element_type=F32)
            h = leaky(h + tiled[1 + layer]).astype(BF16)
        if 0 in slots and first == 0:
            loads[8].wait()
        v = jnp.dot(wo_v[...], h, preferred_element_type=F32) + tiled[3]
        feat = lax.broadcasted_iota(jnp.int32, v.shape, 0)
        v = (jnp.where(feat == OUT, first_half, v) * day).astype(BF16)
        for n in range(len(slots) * count):
            rows = nt(eye[:128, :128], v[:, n * 128 : (n + 1) * 128]).astype(BF16)
            sx[slots[n // count], first + n % count] = rows.reshape(NC, ROWS, LANES)

    def send(src, dst, send_sem, recv_sem, device):
        pltpu.make_async_remote_copy(
            src_ref=src,
            dst_ref=dst,
            send_sem=send_sem,
            recv_sem=recv_sem,
            device_id=device,
            device_id_type=MESH,
        ).start()

    def send_near(k):
        for i in range(2):
            for cc in range(NC):
                dst = rx.at[0, k, 2 * i + c]
                device = (blk_of(z, y, cc), sectors[i])
                send(sx.at[i, k, cc], dst, sx_sem.at[0], rx_sem.at[0, k], device)

    def send_far(k):
        for cc in range(NC):
            device = (blk, sectors[cc])
            send(sx.at[2, k, cc], fx.at[k, cc], sx_sem.at[0], fx_sem.at[k, cc], device)

    def forward(k):
        for cc in range(NC):
            wait_for(fx.at[k, cc], fx_sem.at[k, cc])
            device = (blk_of(z, y, cc), sectors[cc])
            send(fx.at[k, cc], rx.at[1, k, c], fs_sem.at[0], rx_sem.at[1, k], device)

    def send_own(k):
        device = (blk_of(z, y, 1 - c), x)
        send(sx.at[3, k, 1 - c], rx.at[1, k, 2 + c], sx_sem.at[0], rx_sem.at[1, k], device)
        rx[1, k, pl.ds(2 + c, 1)] = sx[3, k, pl.ds(c, 1)]

    def wait_for(view, sem):
        pltpu.make_async_copy(view, view, sem).wait()

    def parts_of(half, k):
        return ((0, 256), (256, 128)) if (half, k) == (1, NK - 1) else ((0, LANES),)

    def stage_x(half, k):
        wait_for(rx.at[half, k, pl.ds(0, 4 - half)], rx_sem.at[half, k])
        sums = [
            (rx[half, k, cc].astype(F32) + rx[half, k, 2 + cc].astype(F32)).reshape(NZ, NY, LANES)
            for cc in range(NC)
        ]
        zs[half, k] = jnp.concatenate(sums, axis=1).astype(BF16)
        for p, (lo, width) in enumerate(parts_of(half, k)):
            lanes = pl.ds(lo, width)
            for d in RING:
                zz = lax.rem(z + d, NZ)
                src, dst = zs.at[half, k, zz, :, lanes], zr.at[half, k, z, :, lanes]
                send(src, dst, zs_sem.at[0], zr_sem.at[half, k, p], (blk_of(zz, y, c), x))
        zr[half, k, pl.ds(z, 1)] = zs[half, k, pl.ds(z, 1)]

    def stage_z(half, k):
        for p, (lo, width) in enumerate(parts_of(half, k)):
            lanes = pl.ds(lo, width)
            wait_for(zr.at[half, k, pl.ds(0, NZ - 1), :, lanes], zr_sem.at[half, k, p])
            rows = zr[half, k, :, :, lanes].reshape(128, width)
            turned = jnp.dot(turn, rows, preferred_element_type=F32)
            ys[half, k, :, :, lanes] = turned.astype(BF16).reshape(NY, 16, width)
            for d in RING:
                yy = lax.rem(y + d, NY)
                src, dst = ys.at[half, k, yy, :, lanes], yr.at[half, k, y, :, lanes]
                send(src, dst, ys_sem.at[0], yr_sem.at[half, k, p], (blk_of(z, yy, c), x))
        yr[half, k, pl.ds(y, 1)] = ys[half, k, pl.ds(y, 1)]

    def stage_y(half):
        near = lax.rem(x + 1 + half, 2)
        total = 0.0
        for k in range(NK):
            place = place_v[pl.ds(k * 128, 128), :]
            for p, (lo, width) in enumerate(parts_of(half, k)):
                lanes = pl.ds(lo, width)
                wait_for(yr.at[half, k, pl.ds(0, NY - 1), :, lanes], yr_sem.at[half, k, p])
                rows = yr[half, k, :, :, lanes].reshape(128, width)
                feats = [
                    nt(eye[:128, :128], rows[:, n : n + 128]).astype(BF16)
                    for n in range(0, width, 128)
                ]
                part = jnp.dot(
                    jnp.concatenate(feats, axis=0), place, preferred_element_type=F32
                )
                if k < NK - 1:
                    total = total + part
                    continue
                t_v[half, lanes] = (total[lo : lo + width] + part).astype(BF16)
                pltpu.make_async_copy(
                    t_v.at[half, lanes], out_ref.at[near, lanes], t_sem.at[half]
                ).start()

    network((0, 1), 0, 1)
    pl.semaphore_wait(barrier, len(peers))
    send_near(0)
    network((0, 1), 1, 2)
    send_near(1)
    send_near(2)
    turn = selector(128, 128, lambda r: (r & 15) * 8 + (r >> 4))
    network((2,), 0, NK)
    stage_x(0, 0)
    send_far(0)
    network((3,), 0, NK)
    send_far(1)
    send_far(2)
    for k in range(NK):
        send_own(k)
    place_v[...] = selector(
        BLOCK,
        BLOCK,
        lambda r: (((r >> 1) & 7) * 16 + ((r >> 4) & 7) * 2 + (r & 1)) * NK + (r >> 7),
    )
    stage_x(0, 1)
    stage_z(0, 0)
    stage_x(0, 2)
    forward(0)
    stage_z(0, 1)
    forward(1)
    forward(2)
    stage_z(0, 2)
    stage_x(1, 0)
    stage_x(1, 1)
    stage_z(1, 0)
    stage_x(1, 2)
    stage_z(1, 1)
    stage_z(1, 2)
    for half in range(2):
        stage_y(half)

    wait_for(sx.at[pl.ds(0, 3)], sx_sem.at[0])
    wait_for(sx.at[3, :, 0], sx_sem.at[0])
    wait_for(fx, fs_sem.at[0])
    wait_for(zs.at[:, :, pl.ds(0, NZ - 1)], zs_sem.at[0])
    wait_for(ys.at[:, :, pl.ds(0, NY - 1)], ys_sem.at[0])
    for half in range(2):
        wait_for(t_v.at[half], t_sem.at[half])


def spread(t_ref, out_ref, t_v, o_v, t_sem, o_sem):
    pieces = [(n, pl.ds(b * 128, 128)) for n in range(2) for b in range(NK)]
    loads = [
        pltpu.make_async_copy(t_ref.at[n, :, lanes], t_v.at[m], t_sem.at[m])
        for m, (n, lanes) in enumerate(pieces)
    ]
    for load in loads:
        load.start()
    stores = []
    for m, (n, _) in enumerate(pieces):
        loads[m].wait()
        values = t_v[m].astype(F32)
        flag = values[OUT : OUT + 1]
        for far, weight in enumerate((flag, 1.0 - flag)):
            slot = m + 6 * far
            o_v[slot] = (values[:OUT] * weight).astype(BF16)
            store = pltpu.make_async_copy(
                o_v.at[slot], out_ref.at[:, pl.ds(slot * 128, 128)], o_sem.at[slot]
            )
            store.start()
            stores.append(store)
    for store in stores:
        store.wait()


def shards(
    features, daylit_list, daylit_count, in_weight, in_bias, mid_weight, mid_bias, out_weight, out_bias
):
    hbm = pl.BlockSpec(memory_space=pltpu.HBM)
    dma = pltpu.SemaphoreType.DMA
    halves = pl.pallas_call(
        kernel,
        out_shape=jax.ShapeDtypeStruct((2, LANES, BLOCK), BF16),
        in_specs=[pl.BlockSpec(memory_space=pltpu.SMEM)] + [hbm] * 8,
        out_specs=hbm,
        scratch_shapes=[
            pltpu.VMEM((COLS,), jnp.int32),
            pltpu.VMEM((4, FEAT, BLOCK), BF16),
            pltpu.VMEM((FEAT, HID), BF16),
            pltpu.VMEM((HID,), F32),
            pltpu.VMEM((2, HID, HID), BF16),
            pltpu.VMEM((2, HID), F32),
            pltpu.VMEM((LANES, HID), BF16),
            pltpu.VMEM((OUT,), F32),
            pltpu.VMEM((16, 128), F32),
            pltpu.VMEM((HID, FEAT), BF16),
            pltpu.VMEM((BLOCK, BLOCK), BF16),
            pltpu.VMEM((BLOCK, BLOCK), BF16),
            pltpu.VMEM((NX, NK, NC, ROWS, LANES), BF16),
            pltpu.VMEM((NK, NC, ROWS, LANES), BF16),
            pltpu.VMEM((2, NK, 4, ROWS, LANES), BF16),
            pltpu.VMEM((2, NK, NZ, 16, LANES), BF16),
            pltpu.VMEM((2, NK, NZ, 16, LANES), BF16),
            pltpu.VMEM((2, NK, NY, 16, LANES), BF16),
            pltpu.VMEM((2, NK, NY, 16, LANES), BF16),
            pltpu.VMEM((2, LANES, BLOCK), BF16),
            dma((11,)),
            dma((1,)),
            dma((NK, NC)),
            dma((1,)),
            dma((2, NK)),
            dma((1,)),
            dma((2, NK, 2)),
            dma((1,)),
            dma((2, NK, 2)),
            dma((2,)),
        ],
        compiler_params=pltpu.CompilerParams(
            collective_id=0, has_side_effects=True, vmem_limit_bytes=VMEM
        ),
    )(
        daylit_count,
        daylit_list,
        features,
        in_weight,
        in_bias,
        mid_weight,
        mid_bias,
        out_weight,
        out_bias,
    )
    return pl.pallas_call(
        spread,
        out_shape=jax.ShapeDtypeStruct((OUT, COLS), BF16),
        in_specs=[hbm],
        out_specs=hbm,
        scratch_shapes=[
            pltpu.VMEM((6, LANES, 128), BF16),
            pltpu.VMEM((12, OUT, 128), BF16),
            dma((6,)),
            dma((12,)),
        ],
        compiler_params=pltpu.CompilerParams(vmem_limit_bytes=VMEM),
    )(halves)


def solution(mesh):
    in_specs = (
        P(None, ("blk", "pair")),
        P(("blk", "pair")),
        P(("blk", "pair")),
        P(),
        P(),
        P(),
        P(),
        P(),
        P(),
    )
    out_specs = P(None, ("blk", "pair"))
    return jax.shard_map(shards, mesh=mesh, in_specs=in_specs, out_specs=out_specs, check_vma=False)
```

```python
import jax
import jax.numpy as jnp
from jax import lax
from jax.experimental import pallas as pl
from jax.experimental.pallas import tpu as pltpu
from jax.sharding import PartitionSpec as P

FEAT, HID, OUT = 557, 512, 368
LANES = 384
NX, NZ, NY, NC, NK = 4, 8, 8, 2, 3
BLOCK = NZ * NY * NC * NK
ROWS = NZ * NY
COLS = NX * BLOCK
OFFSETS = (1, 3, 2, 0)
RING = (4, 3, 5, 2, 6, 1, 7)
VMEM = 62 * 1024 * 1024
LOADED = (5, 6, 9, 10)
BF16, F32 = jnp.bfloat16, jnp.float32
MESH = pl.DeviceIdType.MESH


def nt(a, b):
    return lax.dot_general(a, b, (((1,), (1,)), ((), ())), preferred_element_type=F32)


def leaky(t):
    return jnp.maximum(t, 0.15 * t)


def selector(rows, cols, row_of_column):
    r = lax.broadcasted_iota(jnp.int32, (rows, cols), 0)
    wanted = row_of_column(lax.broadcasted_iota(jnp.int32, (1, cols), 1))
    return jnp.where(r == wanted, 1.0, 0.0).astype(BF16)


def column(row):
    return jnp.transpose(jnp.broadcast_to(row, (128, row.shape[1])))


def kernel(
    count_ref, list_ref, feat_ref, w0_ref, b0_ref, wm_ref, bm_ref, wo_ref, bo_ref, out_ref,
    list_v, f_v, w0_v, b0_v, wm_v, bm_v, wo_v, bo_v, day_v, w0t_v, pick_v, place_v, sx, rx, zs, zr, ys, yr, t_v,
    load_sem, sx_sem, rx_sem, zs_sem, zr_sem, ys_sem, yr_sem, t_sem,
):
    x = lax.axis_index("pair")
    blk = lax.axis_index("blk")
    z, y, c = blk // (NY * NC), (blk // NC) % NY, blk % NC

    def blk_of(zz, yy, cc):
        return (zz * NY + yy) * NC + cc

    sectors = [lax.rem(x + off, NX) for off in OFFSETS]

    def features_of(i):
        return (
            feat_ref.at[:, pl.ds(pl.multiple_of(sectors[i] * BLOCK, 128), BLOCK)],
            f_v.at[i],
        )

    loads = [
        pltpu.make_async_copy(src, dst, load_sem.at[n])
        for n, (src, dst) in enumerate(
            (
                (list_ref, list_v),
                (b0_ref, b0_v),
                (bm_ref, bm_v),
                (bo_ref, bo_v),
                (w0_ref, w0_v),
                features_of(0),
                features_of(1),
                (wm_ref, wm_v),
                (wo_ref, wo_v.at[pl.ds(0, OUT)]),
                features_of(2),
                features_of(3),
            )
        )
    ]
    for load in loads:
        load.start()

    barrier = pltpu.get_barrier_semaphore()
    other = blk_of(z, y, 1 - c)
    cores = (blk, other)
    along_z = [blk_of(lax.rem(z + d, NZ), y, c) for d in range(NZ)]
    along_y = [blk_of(z, lax.rem(y + d, NY), c) for d in range(NY)]
    peers = [(other, a) for a in sectors]
    peers += [(blk, a) for a in sectors[:3]]
    peers += [(along_z[d], x) for d in RING]
    peers += [(along_y[d], x) for d in RING]
    for peer in peers:
        pl.semaphore_signal(barrier, inc=1, device_id=peer, device_id_type=MESH)

    def picked_from(q):
        zz, yy = ((q >> 3) + z) & 7, (q + y) & 7
        return (zz * NY + yy) * (NC * NK) + (((q >> 6) & 1) ^ c) * NK + (q >> 7)

    pick_v[...] = selector(BLOCK, BLOCK, picked_from)
    wo_v[pl.ds(OUT, LANES - OUT), :] = jnp.zeros((LANES - OUT, HID), BF16)

    for load in loads[:4]:
        load.wait()
    entries = list_v[...].reshape(1, COLS)
    usable = lax.broadcasted_iota(jnp.int32, (1, COLS), 1) < count_ref[0]
    high = jnp.where(usable, entries >> 7, -1)
    high = jnp.broadcast_to(high, (16, COLS)) == lax.broadcasted_iota(jnp.int32, (16, COLS), 0)
    low = jnp.broadcast_to(entries & 127, (128, COLS)) == lax.broadcasted_iota(
        jnp.int32, (128, COLS), 0
    )
    day_v[...] = nt(
        jnp.where(high, 1.0, 0.0).astype(BF16), jnp.where(low, 1.0, 0.0).astype(BF16)
    )
    biases = [column(b0_v[...].reshape(1, HID))]
    biases += [column(bm_v[pl.ds(n, 1), :]) for n in range(2)]
    bias_out = jnp.concatenate([bo_v[...].reshape(1, OUT), jnp.zeros((1, LANES - OUT), F32)], axis=1)
    biases.append(column(bias_out))
    first_half = jnp.where(x < NX // 2, 1.0, 0.0)

    loads[4].wait()
    eye = selector(256, 256, lambda r: r)
    for lo in range(0, HID, 256):
        w0t_v[pl.ds(lo, 256), :] = nt(eye, w0_v[:, pl.ds(lo, 256)]).astype(BF16)

    def network(half, first, count):
        picked, days = [], []
        lanes = pl.ds(first * 128, count * 128)
        for i in (2 * half, 2 * half + 1):
            if first == 0:
                loads[LOADED[i]].wait()
            part = jnp.dot(f_v[i], pick_v[:, lanes], preferred_element_type=F32)
            picked.append(part.astype(BF16))
            day = jnp.concatenate(
                [day_v[pl.ds(sectors[i] * NK + t, 1), :] for t in range(NK)], axis=1
            )
            day = jnp.broadcast_to(jnp.where(day > 0.5, 1.0, 0.0), (16, BLOCK)).astype(BF16)
            days.append(jnp.dot(day, pick_v[:, lanes], preferred_element_type=F32)[:1])
        h, day = jnp.concatenate(picked, axis=1), jnp.concatenate(days, axis=1)
        tiled = [jnp.concatenate([b] * (2 * count), axis=1) for b in biases]
        h = jnp.dot(w0t_v[...], h, preferred_element_type=F32)
        h = leaky(h + tiled[0]).astype(BF16)
        if half == 0 and first == 0:
            loads[7].wait()
        for layer in range(2):
            h = jnp.dot(wm_v[layer], h, preferred_element_type=F32)
            h = leaky(h + tiled[1 + layer]).astype(BF16)
        if half == 0 and first == 0:
            loads[8].wait()
        v = jnp.dot(wo_v[...], h, preferred_element_type=F32) + tiled[3]
        feat = lax.broadcasted_iota(jnp.int32, v.shape, 0)
        v = (jnp.where(feat == OUT, first_half, v) * day).astype(BF16)
        for n in range(2 * count):
            rows = nt(eye[:128, :128], v[:, n * 128 : (n + 1) * 128]).astype(BF16)
            sx[2 * half + n // count, first + n % count] = rows.reshape(NC, ROWS, LANES)

    def send(src, dst, send_sem, recv_sem, device):
        pltpu.make_async_remote_copy(
            src_ref=src,
            dst_ref=dst,
            send_sem=send_sem,
            recv_sem=recv_sem,
            device_id=device,
            device_id_type=MESH,
        ).start()

    def send_x(half, k):
        for i in (2 * half, 2 * half + 1):
            for r in range(NC) if i < 3 else (1,):
                dst = rx.at[half, k, 2 * (i % 2) + r]
                device = (cores[r], sectors[i])
                send(sx.at[i, k, r], dst, sx_sem.at[0], rx_sem.at[half, k], device)

    def wait_for(view, sem):
        pltpu.make_async_copy(view, view, sem).wait()

    def stage_x(half, k):
        slots = (0, 1, 2, 3) if half == 0 else (0, 1, 3)
        wait_for(rx.at[half, k, pl.ds(0, len(slots))], rx_sem.at[half, k])
        sums = []
        for r in range(NC):
            near = sx[3, k, 0] if half == 1 and r == 0 else rx[half, k, 2 + r]
            total = rx[half, k, r].astype(F32) + near.astype(F32)
            sums.append(total.reshape(NZ, NY, LANES))
        merged = jnp.concatenate(sums, axis=1).astype(BF16)
        zs[half, k] = merged
        for d in RING:
            dst = zr.at[half, k, d]
            send(zs.at[half, k, d], dst, zs_sem.at[0], zr_sem.at[half, k], (along_z[d], x))
        zr[half, k, 0] = merged[0]

    def stage_z(half, k):
        wait_for(zr.at[half, k, pl.ds(1, NZ - 1)], zr_sem.at[half, k])
        rows = zr[half, k].reshape(128, LANES)
        turned = jnp.dot(turn, rows, preferred_element_type=F32)
        turned = turned.astype(BF16).reshape(NY, 16, LANES)
        ys[half, k] = turned
        for e in RING:
            dst = yr.at[half, k, e]
            send(ys.at[half, k, e], dst, ys_sem.at[0], yr_sem.at[half, k], (along_y[e], x))
        yr[half, k, 0] = turned[0]

    def stage_y(half):
        near = lax.rem(x + 1 + half, 2)
        total = 0.0
        for k in range(NK):
            wait_for(yr.at[half, k, pl.ds(1, NY - 1)], yr_sem.at[half, k])
            rows = yr[half, k].reshape(128, LANES)
            feats = [
                nt(eye[:128, :128], rows[:, n : n + 128]).astype(BF16)
                for n in range(0, LANES, 128)
            ]
            total = total + jnp.dot(
                jnp.concatenate(feats, axis=0),
                place_v[pl.ds(k * 128, 128), :],
                preferred_element_type=F32,
            )
        t_v[half] = total.astype(BF16)
        pltpu.make_async_copy(t_v.at[half], out_ref.at[near], t_sem.at[half]).start()

    chunks = [(half, k) for half in range(2) for k in range(NK)]
    network(0, 0, 1)
    pl.semaphore_wait(barrier, len(peers))
    send_x(0, 0)
    network(0, 1, 2)
    send_x(0, 1)
    send_x(0, 2)
    turn = selector(128, 128, lambda q: (q & 7) * 16 + (q >> 3))
    network(1, 0, 1)
    send_x(1, 0)
    stage_x(0, 0)
    network(1, 1, 2)
    send_x(1, 1)
    send_x(1, 2)
    def placed_from(q):
        source = (q * 21846) >> 16
        d, e = (z - (source >> 4)) & 7, (y - (source >> 1)) & 7
        return (q - source * NK) * 128 + e * 16 + d * 2 + ((source & 1) ^ c)

    place_v[...] = selector(BLOCK, BLOCK, placed_from)
    for t in range(1, len(chunks) + 1):
        if t < len(chunks):
            stage_x(*chunks[t])
        stage_z(*chunks[t - 1])
    for half in range(2):
        stage_y(half)

    wait_for(sx.at[pl.ds(0, 3)], sx_sem.at[0])
    wait_for(sx.at[3, :, 1], sx_sem.at[0])
    wait_for(zs.at[:, :, pl.ds(1, NZ - 1)], zs_sem.at[0])
    wait_for(ys.at[:, :, pl.ds(1, NY - 1)], ys_sem.at[0])
    for half in range(2):
        wait_for(t_v.at[half], t_sem.at[half])


def spread(t_ref, out_ref, t_v, o_v, t_sem, o_sem):
    pieces = [(n, pl.ds(b * 128, 128)) for n in range(2) for b in range(NK)]
    loads = [
        pltpu.make_async_copy(t_ref.at[n, :, lanes], t_v.at[m], t_sem.at[m])
        for m, (n, lanes) in enumerate(pieces)
    ]
    for load in loads:
        load.start()
    stores = []
    for m, (n, _) in enumerate(pieces):
        loads[m].wait()
        values = t_v[m].astype(F32)
        flag = values[OUT : OUT + 1]
        for far, weight in enumerate((flag, 1.0 - flag)):
            slot = m + 6 * far
            o_v[slot] = (values[:OUT] * weight).astype(BF16)
            store = pltpu.make_async_copy(
                o_v.at[slot], out_ref.at[:, pl.ds(slot * 128, 128)], o_sem.at[slot]
            )
            store.start()
            stores.append(store)
    for store in stores:
        store.wait()


def shards(
    features, daylit_list, daylit_count, in_weight, in_bias, mid_weight, mid_bias, out_weight, out_bias
):
    hbm = pl.BlockSpec(memory_space=pltpu.HBM)
    dma = pltpu.SemaphoreType.DMA
    halves = pl.pallas_call(
        kernel,
        out_shape=jax.ShapeDtypeStruct((2, LANES, BLOCK), BF16),
        in_specs=[pl.BlockSpec(memory_space=pltpu.SMEM)] + [hbm] * 8,
        out_specs=hbm,
        scratch_shapes=[
            pltpu.VMEM((COLS,), jnp.int32),
            pltpu.VMEM((4, FEAT, BLOCK), BF16),
            pltpu.VMEM((FEAT, HID), BF16),
            pltpu.VMEM((HID,), F32),
            pltpu.VMEM((2, HID, HID), BF16),
            pltpu.VMEM((2, HID), F32),
            pltpu.VMEM((LANES, HID), BF16),
            pltpu.VMEM((OUT,), F32),
            pltpu.VMEM((16, 128), F32),
            pltpu.VMEM((HID, FEAT), BF16),
            pltpu.VMEM((BLOCK, BLOCK), BF16),
            pltpu.VMEM((BLOCK, BLOCK), BF16),
            pltpu.VMEM((NX, NK, NC, ROWS, LANES), BF16),
            pltpu.VMEM((2, NK, 4, ROWS, LANES), BF16),
            pltpu.VMEM((2, NK, NZ, 16, LANES), BF16),
            pltpu.VMEM((2, NK, NZ, 16, LANES), BF16),
            pltpu.VMEM((2, NK, NY, 16, LANES), BF16),
            pltpu.VMEM((2, NK, NY, 16, LANES), BF16),
            pltpu.VMEM((2, LANES, BLOCK), BF16),
            dma((11,)),
            dma((1,)),
            dma((2, NK)),
            dma((1,)),
            dma((2, NK)),
            dma((1,)),
            dma((2, NK)),
            dma((2,)),
        ],
        compiler_params=pltpu.CompilerParams(
            collective_id=0, has_side_effects=True, vmem_limit_bytes=VMEM
        ),
    )(
        daylit_count,
        daylit_list,
        features,
        in_weight,
        in_bias,
        mid_weight,
        mid_bias,
        out_weight,
        out_bias,
    )
    return pl.pallas_call(
        spread,
        out_shape=jax.ShapeDtypeStruct((OUT, COLS), BF16),
        in_specs=[hbm],
        out_specs=hbm,
        scratch_shapes=[
            pltpu.VMEM((6, LANES, 128), BF16),
            pltpu.VMEM((12, OUT, 128), BF16),
            dma((6,)),
            dma((12,)),
        ],
        compiler_params=pltpu.CompilerParams(vmem_limit_bytes=VMEM),
    )(halves)


def solution(mesh):
    in_specs = (
        P(None, ("blk", "pair")),
        P(("blk", "pair")),
        P(("blk", "pair")),
        P(),
        P(),
        P(),
        P(),
        P(),
        P(),
    )
    out_specs = P(None, ("blk", "pair"))
    return jax.shard_map(shards, mesh=mesh, in_specs=in_specs, out_specs=out_specs, check_vma=False)
```

```python
import jax
import jax.numpy as jnp
from jax import lax
from jax.experimental import pallas as pl
from jax.experimental.pallas import tpu as pltpu
from jax.sharding import PartitionSpec as P

FEAT, HID, OUT = 557, 512, 368
LANES = 384
NX, NZ, NY, NC, NK = 4, 8, 8, 2, 3
BLOCK = NZ * NY * NC * NK
ROWS = NZ * NY
COLS = NX * BLOCK
OFFSETS = (1, 3, 2, 0)
RING = (4, 3, 5, 2, 6, 1, 7)
VMEM = 62 * 1024 * 1024
LOADED = (5, 6, 9, 10)
BF16, F32 = jnp.bfloat16, jnp.float32
MESH = pl.DeviceIdType.MESH


def nt(a, b):
    return lax.dot_general(a, b, (((1,), (1,)), ((), ())), preferred_element_type=F32)


def leaky(t):
    return jnp.maximum(t, 0.15 * t)


def selector(rows, cols, row_of_column):
    r = lax.broadcasted_iota(jnp.int32, (rows, cols), 0)
    wanted = row_of_column(lax.broadcasted_iota(jnp.int32, (1, cols), 1))
    return jnp.where(r == wanted, 1.0, 0.0).astype(BF16)


def column(row):
    return jnp.transpose(jnp.broadcast_to(row, (128, row.shape[1])))


def kernel(
    count_ref, list_ref, feat_ref, w0_ref, b0_ref, wm_ref, bm_ref, wo_ref, bo_ref, out_ref,
    list_v, f_v, w0_v, b0_v, wm_v, bm_v, wo_v, bo_v, day_v, w0t_v, pick_v, place_v, sx, rx, zs, zr, ys, yr, t_v,
    load_sem, sx_sem, rx_sem, zs_sem, zr_sem, ys_sem, yr_sem, t_sem,
):
    x = lax.axis_index("pair")
    blk = lax.axis_index("blk")
    z, y, c = blk // (NY * NC), (blk // NC) % NY, blk % NC

    def blk_of(zz, yy, cc):
        return (zz * NY + yy) * NC + cc

    sectors = [lax.rem(x + off, NX) for off in OFFSETS]

    def features_of(i):
        return (
            feat_ref.at[:, pl.ds(pl.multiple_of(sectors[i] * BLOCK, 128), BLOCK)],
            f_v.at[i],
        )

    loads = [
        pltpu.make_async_copy(src, dst, load_sem.at[n])
        for n, (src, dst) in enumerate(
            (
                (list_ref, list_v),
                (b0_ref, b0_v),
                (bm_ref, bm_v),
                (bo_ref, bo_v),
                (w0_ref, w0_v),
                features_of(0),
                features_of(1),
                (wm_ref, wm_v),
                (wo_ref, wo_v.at[pl.ds(0, OUT)]),
                features_of(2),
                features_of(3),
            )
        )
    ]
    for n in (4, 5, 6, 0, 1, 2, 3, 7, 8, 9, 10):
        loads[n].start()

    barrier = pltpu.get_barrier_semaphore()
    other = blk_of(z, y, 1 - c)
    cores = (blk, other)
    along_z = [blk_of(lax.rem(z + d, NZ), y, c) for d in range(NZ)]
    along_y = [blk_of(z, lax.rem(y + d, NY), c) for d in range(NY)]
    peers = [(other, a) for a in sectors]
    peers += [(blk, a) for a in sectors[:3]]
    peers += [(along_z[d], x) for d in RING]
    peers += [(along_y[d], x) for d in RING]
    def picked_from(q):
        zz, yy = ((q >> 3) + z) & 7, (q + y) & 7
        return (zz * NY + yy) * (NC * NK) + (((q >> 6) & 1) ^ c) * NK + (q >> 7)

    pick_v[...] = selector(BLOCK, BLOCK, picked_from)
    wo_v[pl.ds(OUT, LANES - OUT), :] = jnp.zeros((LANES - OUT, HID), BF16)

    eye = selector(256, 256, lambda r: r)
    turn = selector(128, 128, lambda q: (q & 7) * 16 + (q >> 3))

    for load in loads[:7]:
        load.wait()
    for peer in peers:
        pl.semaphore_signal(barrier, inc=1, device_id=peer, device_id_type=MESH)

    entries = list_v[...].reshape(1, COLS)
    usable = lax.broadcasted_iota(jnp.int32, (1, COLS), 1) < count_ref[0]
    high = jnp.where(usable, entries >> 7, -1)
    high = jnp.broadcast_to(high, (16, COLS)) == lax.broadcasted_iota(jnp.int32, (16, COLS), 0)
    low = jnp.broadcast_to(entries & 127, (128, COLS)) == lax.broadcasted_iota(
        jnp.int32, (128, COLS), 0
    )
    day_v[...] = nt(
        jnp.where(high, 1.0, 0.0).astype(BF16), jnp.where(low, 1.0, 0.0).astype(BF16)
    )
    biases = [column(b0_v[...].reshape(1, HID))]
    biases += [column(bm_v[pl.ds(n, 1), :]) for n in range(2)]
    bias_out = jnp.concatenate([bo_v[...].reshape(1, OUT), jnp.zeros((1, LANES - OUT), F32)], axis=1)
    biases.append(column(bias_out))
    first_half = jnp.where(x < NX // 2, 1.0, 0.0)

    for lo in range(0, HID, 256):
        w0t_v[pl.ds(lo, 256), :] = nt(eye, w0_v[:, pl.ds(lo, 256)]).astype(BF16)

    def network(half, first, count):
        picked, days = [], []
        lanes = pl.ds(first * 128, count * 128)
        for i in (2 * half, 2 * half + 1):
            if first == 0 and i >= 2:
                loads[LOADED[i]].wait()
            part = jnp.dot(f_v[i], pick_v[:, lanes], preferred_element_type=F32)
            picked.append(part.astype(BF16))
            day = jnp.concatenate(
                [day_v[pl.ds(sectors[i] * NK + t, 1), :] for t in range(NK)], axis=1
            )
            day = jnp.broadcast_to(jnp.where(day > 0.5, 1.0, 0.0), (16, BLOCK)).astype(BF16)
            days.append(jnp.dot(day, pick_v[:, lanes], preferred_element_type=F32)[:1])
        h, day = jnp.concatenate(picked, axis=1), jnp.concatenate(days, axis=1)
        tiled = [jnp.concatenate([b] * (2 * count), axis=1) for b in biases]
        h = jnp.dot(w0t_v[...], h, preferred_element_type=F32)
        h = leaky(h + tiled[0]).astype(BF16)
        if half == 0 and first == 0:
            loads[7].wait()
        for layer in range(2):
            h = jnp.dot(wm_v[layer], h, preferred_element_type=F32)
            h = leaky(h + tiled[1 + layer]).astype(BF16)
        if half == 0 and first == 0:
            loads[8].wait()
        v = jnp.dot(wo_v[...], h, preferred_element_type=F32) + tiled[3]
        feat = lax.broadcasted_iota(jnp.int32, v.shape, 0)
        v = (jnp.where(feat == OUT, first_half, v) * day).astype(BF16)
        for n in range(2 * count):
            rows = nt(eye[:128, :128], v[:, n * 128 : (n + 1) * 128]).astype(BF16)
            sx[2 * half + n // count, first + n % count] = rows.reshape(NC, ROWS, LANES)

    def send(src, dst, send_sem, recv_sem, device):
        pltpu.make_async_remote_copy(
            src_ref=src,
            dst_ref=dst,
            send_sem=send_sem,
            recv_sem=recv_sem,
            device_id=device,
            device_id_type=MESH,
        ).start()

    def send_x(half, k):
        for i in (2 * half, 2 * half + 1):
            for r in range(NC) if i < 3 else (1,):
                dst = rx.at[half, k, 2 * (i % 2) + r]
                device = (cores[r], sectors[i])
                send(sx.at[i, k, r], dst, sx_sem.at[0], rx_sem.at[half, k], device)

    def wait_for(view, sem):
        pltpu.make_async_copy(view, view, sem).wait()

    def stage_x(half, k):
        slots = (0, 1, 2, 3) if half == 0 else (0, 1, 3)
        wait_for(rx.at[half, k, pl.ds(0, len(slots))], rx_sem.at[half, k])
        sums = []
        for r in range(NC):
            near = sx[3, k, 0] if half == 1 and r == 0 else rx[half, k, 2 + r]
            total = rx[half, k, r].astype(F32) + near.astype(F32)
            sums.append(total.reshape(NZ, NY, LANES))
        merged = jnp.concatenate(sums, axis=1).astype(BF16)
        zs[half, k] = merged
        for d in RING:
            dst = zr.at[half, k, d]
            send(zs.at[half, k, d], dst, zs_sem.at[0], zr_sem.at[half, k], (along_z[d], x))
        zr[half, k, 0] = merged[0]

    def stage_z(half, k):
        wait_for(zr.at[half, k, pl.ds(1, NZ - 1)], zr_sem.at[half, k])
        rows = zr[half, k].reshape(128, LANES)
        turned = jnp.dot(turn, rows, preferred_element_type=F32)
        turned = turned.astype(BF16).reshape(NY, 16, LANES)
        ys[half, k] = turned
        for e in RING:
            dst = yr.at[half, k, e]
            send(ys.at[half, k, e], dst, ys_sem.at[0], yr_sem.at[half, k], (along_y[e], x))
        yr[half, k, 0] = turned[0]

    def stage_y(half):
        near = lax.rem(x + 1 + half, 2)
        total = 0.0
        for k in range(NK):
            wait_for(yr.at[half, k, pl.ds(1, NY - 1)], yr_sem.at[half, k])
            rows = yr[half, k].reshape(128, LANES)
            feats = [
                nt(eye[:128, :128], rows[:, n : n + 128]).astype(BF16)
                for n in range(0, LANES, 128)
            ]
            total = total + jnp.dot(
                jnp.concatenate(feats, axis=0),
                place_v[pl.ds(k * 128, 128), :],
                preferred_element_type=F32,
            )
        t_v[half] = total.astype(BF16)
        pltpu.make_async_copy(t_v.at[half], out_ref.at[near], t_sem.at[half]).start()

    chunks = [(half, k) for half in range(2) for k in range(NK)]
    network(0, 0, 1)
    pl.semaphore_wait(barrier, len(peers))
    send_x(0, 0)
    network(0, 1, 2)
    send_x(0, 1)
    network(1, 0, 1)
    send_x(0, 2)
    stage_x(0, 0)
    send_x(1, 0)
    network(1, 1, 2)
    def placed_from(q):
        source = (q * 21846) >> 16
        d, e = (z - (source >> 4)) & 7, (y - (source >> 1)) & 7
        return (q - source * NK) * 128 + e * 16 + d * 2 + ((source & 1) ^ c)

    place_v[...] = selector(BLOCK, BLOCK, placed_from)
    for t in range(1, len(chunks) + 1):
        if t < len(chunks):
            stage_x(*chunks[t])
        if t <= 2:
            send_x(1, t)
        stage_z(*chunks[t - 1])
    for half in range(2):
        stage_y(half)

    wait_for(sx.at[pl.ds(0, 3)], sx_sem.at[0])
    wait_for(sx.at[3, :, 1], sx_sem.at[0])
    wait_for(zs.at[:, :, pl.ds(1, NZ - 1)], zs_sem.at[0])
    wait_for(ys.at[:, :, pl.ds(1, NY - 1)], ys_sem.at[0])
    for half in range(2):
        wait_for(t_v.at[half], t_sem.at[half])


def spread(t_ref, out_ref, t_v, o_v, t_sem, o_sem):
    pieces = [(n, pl.ds(b * 128, 128)) for n in range(2) for b in range(NK)]
    loads = [
        pltpu.make_async_copy(t_ref.at[n, :, lanes], t_v.at[m], t_sem.at[m])
        for m, (n, lanes) in enumerate(pieces)
    ]
    for load in loads:
        load.start()
    stores = []
    for m, (n, _) in enumerate(pieces):
        loads[m].wait()
        values = t_v[m].astype(F32)
        flag = values[OUT : OUT + 1]
        for far, weight in enumerate((flag, 1.0 - flag)):
            slot = m + 6 * far
            o_v[slot] = (values[:OUT] * weight).astype(BF16)
            store = pltpu.make_async_copy(
                o_v.at[slot], out_ref.at[:, pl.ds(slot * 128, 128)], o_sem.at[slot]
            )
            store.start()
            stores.append(store)
    for store in stores:
        store.wait()


def shards(
    features, daylit_list, daylit_count, in_weight, in_bias, mid_weight, mid_bias, out_weight, out_bias
):
    hbm = pl.BlockSpec(memory_space=pltpu.HBM)
    dma = pltpu.SemaphoreType.DMA
    halves = pl.pallas_call(
        kernel,
        out_shape=jax.ShapeDtypeStruct((2, LANES, BLOCK), BF16),
        in_specs=[pl.BlockSpec(memory_space=pltpu.SMEM)] + [hbm] * 8,
        out_specs=hbm,
        scratch_shapes=[
            pltpu.VMEM((COLS,), jnp.int32),
            pltpu.VMEM((4, FEAT, BLOCK), BF16),
            pltpu.VMEM((FEAT, HID), BF16),
            pltpu.VMEM((HID,), F32),
            pltpu.VMEM((2, HID, HID), BF16),
            pltpu.VMEM((2, HID), F32),
            pltpu.VMEM((LANES, HID), BF16),
            pltpu.VMEM((OUT,), F32),
            pltpu.VMEM((16, 128), F32),
            pltpu.VMEM((HID, FEAT), BF16),
            pltpu.VMEM((BLOCK, BLOCK), BF16),
            pltpu.VMEM((BLOCK, BLOCK), BF16),
            pltpu.VMEM((NX, NK, NC, ROWS, LANES), BF16),
            pltpu.VMEM((2, NK, 4, ROWS, LANES), BF16),
            pltpu.VMEM((2, NK, NZ, 16, LANES), BF16),
            pltpu.VMEM((2, NK, NZ, 16, LANES), BF16),
            pltpu.VMEM((2, NK, NY, 16, LANES), BF16),
            pltpu.VMEM((2, NK, NY, 16, LANES), BF16),
            pltpu.VMEM((2, LANES, BLOCK), BF16),
            dma((11,)),
            dma((1,)),
            dma((2, NK)),
            dma((1,)),
            dma((2, NK)),
            dma((1,)),
            dma((2, NK)),
            dma((2,)),
        ],
        compiler_params=pltpu.CompilerParams(
            collective_id=0, has_side_effects=True, vmem_limit_bytes=VMEM
        ),
    )(
        daylit_count,
        daylit_list,
        features,
        in_weight,
        in_bias,
        mid_weight,
        mid_bias,
        out_weight,
        out_bias,
    )
    return pl.pallas_call(
        spread,
        out_shape=jax.ShapeDtypeStruct((OUT, COLS), BF16),
        in_specs=[hbm],
        out_specs=hbm,
        scratch_shapes=[
            pltpu.VMEM((6, LANES, 128), BF16),
            pltpu.VMEM((12, OUT, 128), BF16),
            dma((6,)),
            dma((12,)),
        ],
        compiler_params=pltpu.CompilerParams(vmem_limit_bytes=VMEM),
    )(halves)


def solution(mesh):
    in_specs = (
        P(None, ("blk", "pair")),
        P(("blk", "pair")),
        P(("blk", "pair")),
        P(),
        P(),
        P(),
        P(),
        P(),
        P(),
    )
    out_specs = P(None, ("blk", "pair"))
    return jax.shard_map(shards, mesh=mesh, in_specs=in_specs, out_specs=out_specs, check_vma=False)
```

```python
import jax
import jax.numpy as jnp
from jax import lax
from jax.experimental import pallas as pl
from jax.experimental.pallas import tpu as pltpu
from jax.sharding import PartitionSpec as P

FEAT, HID, OUT = 557, 512, 368
LANES = 384
NX, NZ, NY, NC, NK = 4, 8, 8, 2, 3
BLOCK = NZ * NY * NC * NK
ROWS = NZ * NY
COLS = NX * BLOCK
OFFSETS = (1, 3, 2, 0)
RING = (4, 3, 5, 2, 6, 1, 7)
VMEM = 62 * 1024 * 1024
LOADED = (5, 6, 9, 10)
BF16, F32 = jnp.bfloat16, jnp.float32
MESH = pl.DeviceIdType.MESH


def nt(a, b):
    return lax.dot_general(a, b, (((1,), (1,)), ((), ())), preferred_element_type=F32)


def leaky(t):
    return jnp.maximum(t, 0.15 * t)


def selector(rows, cols, row_of_column):
    r = lax.broadcasted_iota(jnp.int32, (rows, cols), 0)
    wanted = row_of_column(lax.broadcasted_iota(jnp.int32, (1, cols), 1))
    return jnp.where(r == wanted, 1.0, 0.0).astype(BF16)


def column(row):
    return jnp.transpose(jnp.broadcast_to(row, (128, row.shape[1])))


def kernel(
    count_ref, list_ref, feat_ref, w0_ref, b0_ref, wm_ref, bm_ref, wo_ref, bo_ref, out_ref,
    list_v, f_v, w0_v, b0_v, wm_v, bm_v, wo_v, bo_v, day_v, w0t_v, pick_v, place_v, sx, rx, zs, zr, ys, yr, t_v,
    load_sem, sx_sem, rx_sem, zs_sem, zr_sem, ys_sem, yr_sem, t_sem,
):
    x = lax.axis_index("pair")
    blk = lax.axis_index("blk")
    z, y, c = blk // (NY * NC), (blk // NC) % NY, blk % NC

    def blk_of(zz, yy, cc):
        return (zz * NY + yy) * NC + cc

    sectors = [lax.rem(x + off, NX) for off in OFFSETS]

    def features_of(i):
        return (
            feat_ref.at[:, pl.ds(pl.multiple_of(sectors[i] * BLOCK, 128), BLOCK)],
            f_v.at[i],
        )

    loads = [
        pltpu.make_async_copy(src, dst, load_sem.at[n])
        for n, (src, dst) in enumerate(
            (
                (list_ref, list_v),
                (b0_ref, b0_v),
                (bm_ref, bm_v),
                (bo_ref, bo_v),
                (w0_ref, w0_v),
                features_of(0),
                features_of(1),
                (wm_ref, wm_v),
                (wo_ref, wo_v.at[pl.ds(0, OUT)]),
                features_of(2),
                features_of(3),
            )
        )
    ]
    for n in (4, 5, 6, 0, 1, 2, 3, 7, 8, 9, 10):
        loads[n].start()

    barrier = pltpu.get_barrier_semaphore()
    other = blk_of(z, y, 1 - c)
    cores = (blk, other)
    along_z = [blk_of(lax.rem(z + d, NZ), y, c) for d in range(NZ)]
    along_y = [blk_of(z, lax.rem(y + d, NY), c) for d in range(NY)]
    peers = [(other, a) for a in sectors]
    peers += [(blk, a) for a in sectors[:3]]
    peers += [(along_z[d], x) for d in RING]
    peers += [(along_y[d], x) for d in RING]
    def picked_from(q):
        zz, yy = ((q >> 3) + z) & 7, (q + y) & 7
        return (zz * NY + yy) * (NC * NK) + (((q >> 6) & 1) ^ c) * NK + (q >> 7)

    pick_v[...] = selector(BLOCK, BLOCK, picked_from)
    wo_v[pl.ds(OUT, LANES - OUT), :] = jnp.zeros((LANES - OUT, HID), BF16)

    eye = selector(256, 256, lambda r: r)
    turn = selector(128, 128, lambda q: (q & 7) * 16 + (q >> 3))

    for load in loads[:7]:
        load.wait()
    for peer in peers:
        pl.semaphore_signal(barrier, inc=1, device_id=peer, device_id_type=MESH)

    entries = list_v[...].reshape(1, COLS)
    usable = lax.broadcasted_iota(jnp.int32, (1, COLS), 1) < count_ref[0]
    high = jnp.where(usable, entries >> 7, -1)
    high = jnp.broadcast_to(high, (16, COLS)) == lax.broadcasted_iota(jnp.int32, (16, COLS), 0)
    low = jnp.broadcast_to(entries & 127, (128, COLS)) == lax.broadcasted_iota(
        jnp.int32, (128, COLS), 0
    )
    day_v[...] = nt(
        jnp.where(high, 1.0, 0.0).astype(BF16), jnp.where(low, 1.0, 0.0).astype(BF16)
    )
    biases = [column(b0_v[...].reshape(1, HID))]
    biases += [column(bm_v[pl.ds(n, 1), :]) for n in range(2)]
    bias_out = jnp.concatenate([bo_v[...].reshape(1, OUT), jnp.zeros((1, LANES - OUT), F32)], axis=1)
    biases.append(column(bias_out))
    first_half = jnp.where(x < NX // 2, 1.0, 0.0)

    for lo in range(0, HID, 256):
        w0t_v[pl.ds(lo, 256), :] = nt(eye, w0_v[:, pl.ds(lo, 256)]).astype(BF16)

    def network(half, first, count):
        picked, days = [], []
        lanes = pl.ds(first * 128, count * 128)
        for i in (2 * half, 2 * half + 1):
            if first == 0 and i >= 2:
                loads[LOADED[i]].wait()
            part = jnp.dot(f_v[i], pick_v[:, lanes], preferred_element_type=F32)
            picked.append(part.astype(BF16))
            day = jnp.concatenate(
                [day_v[pl.ds(sectors[i] * NK + t, 1), :] for t in range(NK)], axis=1
            )
            day = jnp.broadcast_to(jnp.where(day > 0.5, 1.0, 0.0), (16, BLOCK)).astype(BF16)
            days.append(jnp.dot(day, pick_v[:, lanes], preferred_element_type=F32)[:1])
        h, day = jnp.concatenate(picked, axis=1), jnp.concatenate(days, axis=1)
        tiled = [jnp.concatenate([b] * (2 * count), axis=1) for b in biases]
        h = jnp.dot(w0t_v[...], h, preferred_element_type=F32)
        h = leaky(h + tiled[0]).astype(BF16)
        if half == 0 and first == 0:
            loads[7].wait()
        for layer in range(2):
            h = jnp.dot(wm_v[layer], h, preferred_element_type=F32)
            h = leaky(h + tiled[1 + layer]).astype(BF16)
        if half == 0 and first == 0:
            loads[8].wait()
        v = jnp.dot(wo_v[...], h, preferred_element_type=F32) + tiled[3]
        feat = lax.broadcasted_iota(jnp.int32, v.shape, 0)
        v = (jnp.where(feat == OUT, first_half, v) * day).astype(BF16)
        for n in range(2 * count):
            rows = nt(eye[:128, :128], v[:, n * 128 : (n + 1) * 128]).astype(BF16)
            sx[2 * half + n // count, first + n % count] = rows.reshape(NC, ROWS, LANES)

    def send(src, dst, send_sem, recv_sem, device):
        pltpu.make_async_remote_copy(
            src_ref=src,
            dst_ref=dst,
            send_sem=send_sem,
            recv_sem=recv_sem,
            device_id=device,
            device_id_type=MESH,
        ).start()

    def send_x(half, k):
        for i in (2 * half, 2 * half + 1):
            for r in range(NC) if i < 3 else (1,):
                dst = rx.at[half, k, 2 * (i % 2) + r]
                device = (cores[r], sectors[i])
                send(sx.at[i, k, r], dst, sx_sem.at[0], rx_sem.at[half, k], device)

    def wait_for(view, sem):
        pltpu.make_async_copy(view, view, sem).wait()

    def parts_of(half, k):
        return (pl.ds(0, 256), pl.ds(256, 128)) if (half, k) == (1, NK - 1) else (pl.ds(0, LANES),)

    def stage_x(half, k):
        slots = (0, 1, 2, 3) if half == 0 else (0, 1, 3)
        wait_for(rx.at[half, k, pl.ds(0, len(slots))], rx_sem.at[half, k])
        sums = []
        for r in range(NC):
            near = sx[3, k, 0] if half == 1 and r == 0 else rx[half, k, 2 + r]
            total = rx[half, k, r].astype(F32) + near.astype(F32)
            sums.append(total.reshape(NZ, NY, LANES))
        merged = jnp.concatenate(sums, axis=1).astype(BF16)
        zs[half, k] = merged
        for p, lanes in enumerate(parts_of(half, k)):
            for d in RING:
                src, dst = zs.at[half, k, d, :, lanes], zr.at[half, k, d, :, lanes]
                send(src, dst, zs_sem.at[0], zr_sem.at[half, k, p], (along_z[d], x))
        zr[half, k, 0] = merged[0]

    def stage_z(half, k):
        for p, lanes in enumerate(parts_of(half, k)):
            wait_for(zr.at[half, k, pl.ds(1, NZ - 1), :, lanes], zr_sem.at[half, k, p])
            rows = zr[half, k, :, :, lanes].reshape(128, lanes.size)
            turned = jnp.dot(turn, rows, preferred_element_type=F32)
            turned = turned.astype(BF16).reshape(NY, 16, lanes.size)
            ys[half, k, :, :, lanes] = turned
            for e in RING:
                src, dst = ys.at[half, k, e, :, lanes], yr.at[half, k, e, :, lanes]
                send(src, dst, ys_sem.at[0], yr_sem.at[half, k, p], (along_y[e], x))
            yr[half, k, 0, :, lanes] = turned[0]

    def stage_y(half):
        near = lax.rem(x + 1 + half, 2)
        total = 0.0
        for k in range(NK):
            place = place_v[pl.ds(k * 128, 128), :]
            for p, lanes in enumerate(parts_of(half, k)):
                wait_for(yr.at[half, k, pl.ds(1, NY - 1), :, lanes], yr_sem.at[half, k, p])
                rows = yr[half, k, :, :, lanes].reshape(128, lanes.size)
                feats = [
                    nt(eye[:128, :128], rows[:, n : n + 128]).astype(BF16)
                    for n in range(0, lanes.size, 128)
                ]
                part = jnp.dot(
                    jnp.concatenate(feats, axis=0), place, preferred_element_type=F32
                )
                if k < NK - 1:
                    total = total + part
                    continue
                result = total[lanes.start : lanes.start + lanes.size] + part
                t_v[half, lanes] = result.astype(BF16)
                pltpu.make_async_copy(
                    t_v.at[half, lanes], out_ref.at[near, lanes], t_sem.at[half]
                ).start()

    chunks = [(half, k) for half in range(2) for k in range(NK)]
    network(0, 0, 1)
    pl.semaphore_wait(barrier, len(peers))
    send_x(0, 0)
    network(0, 1, 2)
    send_x(0, 1)
    send_x(0, 2)
    stage_x(0, 0)
    network(1, 0, 1)
    send_x(1, 0)
    network(1, 1, 2)
    def placed_from(q):
        source = (q * 21846) >> 16
        d, e = (z - (source >> 4)) & 7, (y - (source >> 1)) & 7
        return (q - source * NK) * 128 + e * 16 + d * 2 + ((source & 1) ^ c)

    place_v[...] = selector(BLOCK, BLOCK, placed_from)
    for t in range(1, len(chunks) + 1):
        if t < len(chunks):
            stage_x(*chunks[t])
        if t <= 2:
            send_x(1, t)
        stage_z(*chunks[t - 1])
    for half in range(2):
        stage_y(half)

    wait_for(sx.at[pl.ds(0, 3)], sx_sem.at[0])
    wait_for(sx.at[3, :, 1], sx_sem.at[0])
    wait_for(zs.at[:, :, pl.ds(1, NZ - 1)], zs_sem.at[0])
    wait_for(ys.at[:, :, pl.ds(1, NY - 1)], ys_sem.at[0])
    for half in range(2):
        wait_for(t_v.at[half], t_sem.at[half])


def spread(t_ref, out_ref, t_v, o_v, t_sem, o_sem):
    pieces = [(n, pl.ds(b * 128, 128)) for n in range(2) for b in range(NK)]
    loads = [
        pltpu.make_async_copy(t_ref.at[n, :, lanes], t_v.at[m], t_sem.at[m])
        for m, (n, lanes) in enumerate(pieces)
    ]
    for load in loads:
        load.start()
    stores = []
    for m, (n, _) in enumerate(pieces):
        loads[m].wait()
        values = t_v[m].astype(F32)
        flag = values[OUT : OUT + 1]
        for far, weight in enumerate((flag, 1.0 - flag)):
            slot = m + 6 * far
            o_v[slot] = (values[:OUT] * weight).astype(BF16)
            store = pltpu.make_async_copy(
                o_v.at[slot], out_ref.at[:, pl.ds(slot * 128, 128)], o_sem.at[slot]
            )
            store.start()
            stores.append(store)
    for store in stores:
        store.wait()


def shards(
    features, daylit_list, daylit_count, in_weight, in_bias, mid_weight, mid_bias, out_weight, out_bias
):
    hbm = pl.BlockSpec(memory_space=pltpu.HBM)
    dma = pltpu.SemaphoreType.DMA
    halves = pl.pallas_call(
        kernel,
        out_shape=jax.ShapeDtypeStruct((2, LANES, BLOCK), BF16),
        in_specs=[pl.BlockSpec(memory_space=pltpu.SMEM)] + [hbm] * 8,
        out_specs=hbm,
        scratch_shapes=[
            pltpu.VMEM((COLS,), jnp.int32),
            pltpu.VMEM((4, FEAT, BLOCK), BF16),
            pltpu.VMEM((FEAT, HID), BF16),
            pltpu.VMEM((HID,), F32),
            pltpu.VMEM((2, HID, HID), BF16),
            pltpu.VMEM((2, HID), F32),
            pltpu.VMEM((LANES, HID), BF16),
            pltpu.VMEM((OUT,), F32),
            pltpu.VMEM((16, 128), F32),
            pltpu.VMEM((HID, FEAT), BF16),
            pltpu.VMEM((BLOCK, BLOCK), BF16),
            pltpu.VMEM((BLOCK, BLOCK), BF16),
            pltpu.VMEM((NX, NK, NC, ROWS, LANES), BF16),
            pltpu.VMEM((2, NK, 4, ROWS, LANES), BF16),
            pltpu.VMEM((2, NK, NZ, 16, LANES), BF16),
            pltpu.VMEM((2, NK, NZ, 16, LANES), BF16),
            pltpu.VMEM((2, NK, NY, 16, LANES), BF16),
            pltpu.VMEM((2, NK, NY, 16, LANES), BF16),
            pltpu.VMEM((2, LANES, BLOCK), BF16),
            dma((11,)),
            dma((1,)),
            dma((2, NK)),
            dma((1,)),
            dma((2, NK, 2)),
            dma((1,)),
            dma((2, NK, 2)),
            dma((2,)),
        ],
        compiler_params=pltpu.CompilerParams(
            collective_id=0, has_side_effects=True, vmem_limit_bytes=VMEM
        ),
    )(
        daylit_count,
        daylit_list,
        features,
        in_weight,
        in_bias,
        mid_weight,
        mid_bias,
        out_weight,
        out_bias,
    )
    return pl.pallas_call(
        spread,
        out_shape=jax.ShapeDtypeStruct((OUT, COLS), BF16),
        in_specs=[hbm],
        out_specs=hbm,
        scratch_shapes=[
            pltpu.VMEM((6, LANES, 128), BF16),
            pltpu.VMEM((12, OUT, 128), BF16),
            dma((6,)),
            dma((12,)),
        ],
        compiler_params=pltpu.CompilerParams(vmem_limit_bytes=VMEM),
    )(halves)


def solution(mesh):
    in_specs = (
        P(None, ("blk", "pair")),
        P(("blk", "pair")),
        P(("blk", "pair")),
        P(),
        P(),
        P(),
        P(),
        P(),
        P(),
    )
    out_specs = P(None, ("blk", "pair"))
    return jax.shard_map(shards, mesh=mesh, in_specs=in_specs, out_specs=out_specs, check_vma=False)
```

```python
import jax
import jax.numpy as jnp
from jax import lax
from jax.experimental import pallas as pl
from jax.experimental.pallas import tpu as pltpu
from jax.sharding import PartitionSpec as P

FEAT, HID, OUT = 557, 512, 368
LANES = 384
NX, NZ, NY, NC, NK = 4, 8, 8, 2, 3
BLOCK = NZ * NY * NC * NK
ROWS = NZ * NY
COLS = NX * BLOCK
OFFSETS = (1, 3, 2, 0)
RING = (4, 3, 5, 2, 6, 1, 7)
VMEM = 62 * 1024 * 1024
LOADED = (5, 6, 9, 10)
ROUNDS = ((0, 1), (1, 2), (3, 1), (4, 1), (5, 1))
BF16, F32 = jnp.bfloat16, jnp.float32
MESH = pl.DeviceIdType.MESH


def nt(a, b):
    return lax.dot_general(a, b, (((1,), (1,)), ((), ())), preferred_element_type=F32)


def leaky(t):
    return jnp.maximum(t, 0.15 * t)


def selector(rows, cols, row_of_column):
    r = lax.broadcasted_iota(jnp.int32, (rows, cols), 0)
    wanted = row_of_column(lax.broadcasted_iota(jnp.int32, (1, cols), 1))
    return jnp.where(r == wanted, 1.0, 0.0).astype(BF16)


def column(row):
    return jnp.transpose(jnp.broadcast_to(row, (128, row.shape[1])))


def kernel(
    count_ref, list_ref, feat_ref, w0_ref, b0_ref, wm_ref, bm_ref, wo_ref, bo_ref, out_ref,
    list_v, f_v, w0_v, b0_v, wm_v, bm_v, wo_v, bo_v, day_v, w0t_v, pick_v, place_v, sx, rx, zs, zr, ys, yr, t_v,
    load_sem, sx_sem, rx_sem, zs_sem, zr_sem, ys_sem, yr_sem, t_sem,
):
    x = lax.axis_index("pair")
    blk = lax.axis_index("blk")
    z, y, c = blk // (NY * NC), (blk // NC) % NY, blk % NC

    def blk_of(zz, yy, cc):
        return (zz * NY + yy) * NC + cc

    sectors = [lax.rem(x + off, NX) for off in OFFSETS]

    def features_of(i):
        return (
            feat_ref.at[:, pl.ds(pl.multiple_of(sectors[i] * BLOCK, 128), BLOCK)],
            f_v.at[i],
        )

    loads = [
        pltpu.make_async_copy(src, dst, load_sem.at[n])
        for n, (src, dst) in enumerate(
            (
                (list_ref, list_v),
                (b0_ref, b0_v),
                (bm_ref, bm_v),
                (bo_ref, bo_v),
                (w0_ref, w0_v),
                features_of(0),
                features_of(1),
                (wm_ref, wm_v),
                (wo_ref, wo_v.at[pl.ds(0, OUT)]),
                features_of(2),
                features_of(3),
            )
        )
    ]
    for n in (4, 5, 6, 0, 1, 2, 3, 7, 8, 9, 10):
        loads[n].start()

    barrier = pltpu.get_barrier_semaphore()
    other = blk_of(z, y, 1 - c)
    cores = (blk, other)
    along_z = [blk_of(lax.rem(z + d, NZ), y, c) for d in range(NZ)]
    along_y = [blk_of(z, lax.rem(y + d, NY), c) for d in range(NY)]
    peers = [(other, a) for a in sectors]
    peers += [(blk, a) for a in sectors[:3]]
    peers += [(along_z[d], x) for d in RING]
    peers += [(along_y[d], x) for d in RING]
    def picked_from(q):
        zz, yy = ((q >> 3) + z) & 7, (q + y) & 7
        return (zz * NY + yy) * (NC * NK) + (((q >> 6) & 1) ^ c) * NK + (q >> 7)

    pick_v[...] = selector(BLOCK, BLOCK, picked_from)
    wo_v[pl.ds(OUT, LANES - OUT), :] = jnp.zeros((LANES - OUT, HID), BF16)

    eye = selector(256, 256, lambda r: r)
    turn = selector(128, 128, lambda q: (q & 7) * 16 + (q >> 3))

    for load in loads[:7]:
        load.wait()
    for peer in peers:
        pl.semaphore_signal(barrier, inc=1, device_id=peer, device_id_type=MESH)

    entries = list_v[...].reshape(1, COLS)
    usable = lax.broadcasted_iota(jnp.int32, (1, COLS), 1) < count_ref[0]
    high = jnp.where(usable, entries >> 7, -1)
    high = jnp.broadcast_to(high, (16, COLS)) == lax.broadcasted_iota(jnp.int32, (16, COLS), 0)
    low = jnp.broadcast_to(entries & 127, (128, COLS)) == lax.broadcasted_iota(
        jnp.int32, (128, COLS), 0
    )
    day_v[...] = nt(
        jnp.where(high, 1.0, 0.0).astype(BF16), jnp.where(low, 1.0, 0.0).astype(BF16)
    )
    biases = [column(b0_v[...].reshape(1, HID))]
    biases += [column(bm_v[pl.ds(n, 1), :]) for n in range(2)]
    bias_out = jnp.concatenate([bo_v[...].reshape(1, OUT), jnp.zeros((1, LANES - OUT), F32)], axis=1)
    biases.append(column(bias_out))
    first_half = jnp.where(x < NX // 2, 1.0, 0.0)

    for lo in range(0, HID, 256):
        w0t_v[pl.ds(lo, 256), :] = nt(eye, w0_v[:, pl.ds(lo, 256)]).astype(BF16)

    def network(half, first, count):
        picked, days = [], []
        lanes = pl.ds(first * 128, count * 128)
        for i in (2 * half, 2 * half + 1):
            if first == 0 and i >= 2:
                loads[LOADED[i]].wait()
            part = jnp.dot(f_v[i], pick_v[:, lanes], preferred_element_type=F32)
            picked.append(part.astype(BF16))
            day = jnp.concatenate(
                [day_v[pl.ds(sectors[i] * NK + t, 1), :] for t in range(NK)], axis=1
            )
            day = jnp.broadcast_to(jnp.where(day > 0.5, 1.0, 0.0), (16, BLOCK)).astype(BF16)
            days.append(jnp.dot(day, pick_v[:, lanes], preferred_element_type=F32)[:1])
        h, day = jnp.concatenate(picked, axis=1), jnp.concatenate(days, axis=1)
        tiled = [jnp.concatenate([b] * (2 * count), axis=1) for b in biases]
        h = jnp.dot(w0t_v[...], h, preferred_element_type=F32)
        h = leaky(h + tiled[0]).astype(BF16)
        if half == 0 and first == 0:
            loads[7].wait()
        for layer in range(2):
            h = jnp.dot(wm_v[layer], h, preferred_element_type=F32)
            h = leaky(h + tiled[1 + layer]).astype(BF16)
        if half == 0 and first == 0:
            loads[8].wait()
        v = jnp.dot(wo_v[...], h, preferred_element_type=F32) + tiled[3]
        feat = lax.broadcasted_iota(jnp.int32, v.shape, 0)
        v = (jnp.where(feat == OUT, first_half, v) * day).astype(BF16)
        for n in range(2 * count):
            rows = nt(eye[:128, :128], v[:, n * 128 : (n + 1) * 128]).astype(BF16)
            sx[2 * half + n // count, first + n % count] = rows.reshape(NC, ROWS, LANES)

    def send(src, dst, send_sem, recv_sem, device):
        pltpu.make_async_remote_copy(
            src_ref=src,
            dst_ref=dst,
            send_sem=send_sem,
            recv_sem=recv_sem,
            device_id=device,
            device_id_type=MESH,
        ).start()

    def send_x(half, k):
        for i in (2 * half, 2 * half + 1):
            for r in range(NC) if i < 3 else (1,):
                dst = rx.at[half, k, 2 * (i % 2) + r]
                device = (cores[r], sectors[i])
                send(sx.at[i, k, r], dst, sx_sem.at[0], rx_sem.at[half, k], device)

    def wait_for(view, sem):
        pltpu.make_async_copy(view, view, sem).wait()

    def merge(n):
        half, k = n // NK, n % NK
        slots = (0, 1, 2, 3) if half == 0 else (0, 1, 3)
        wait_for(rx.at[half, k, pl.ds(0, len(slots))], rx_sem.at[half, k])
        sums = []
        for r in range(NC):
            near = sx[3, k, 0] if half == 1 and r == 0 else rx[half, k, 2 + r]
            total = rx[half, k, r].astype(F32) + near.astype(F32)
            sums.append(total.reshape(NZ, NY, LANES))
        merged = jnp.concatenate(sums, axis=1).astype(BF16)
        zs[n] = merged
        zr[n, 0] = merged[0]

    def stage_x(first, count):
        chunks = pl.ds(first, count)
        for n in range(first, first + count):
            merge(n)
        for d in RING:
            src, dst = zs.at[chunks, d], zr.at[chunks, d]
            send(src, dst, zs_sem.at[0], zr_sem.at[first], (along_z[d], x))

    def stage_z(first, count):
        chunks = pl.ds(first, count)
        wait_for(zr.at[chunks, pl.ds(1, NZ - 1)], zr_sem.at[first])
        for n in range(first, first + count):
            rows = zr[n].reshape(128, LANES)
            turned = jnp.dot(turn, rows, preferred_element_type=F32)
            turned = turned.astype(BF16).reshape(NY, 16, LANES)
            ys[n] = turned
            yr[n, 0] = turned[0]
        for e in RING:
            src, dst = ys.at[chunks, e], yr.at[chunks, e]
            send(src, dst, ys_sem.at[0], yr_sem.at[first], (along_y[e], x))

    def stage_y(half):
        near = lax.rem(x + 1 + half, 2)
        total = 0.0
        for k in range(NK):
            n = half * NK + k
            for first, count in ROUNDS:
                if first == n:
                    wait_for(yr.at[pl.ds(n, count), pl.ds(1, NY - 1)], yr_sem.at[n])
            rows = yr[n].reshape(128, LANES)
            feats = [
                nt(eye[:128, :128], rows[:, lo : lo + 128]).astype(BF16)
                for lo in range(0, LANES, 128)
            ]
            total = total + jnp.dot(
                jnp.concatenate(feats, axis=0),
                place_v[pl.ds(k * 128, 128), :],
                preferred_element_type=F32,
            )
        t_v[half] = total.astype(BF16)
        pltpu.make_async_copy(t_v.at[half], out_ref.at[near], t_sem.at[half]).start()

    network(0, 0, 1)
    pl.semaphore_wait(barrier, len(peers))
    send_x(0, 0)
    network(0, 1, 2)
    send_x(0, 1)
    send_x(0, 2)
    network(1, 0, 1)
    send_x(1, 0)
    stage_x(*ROUNDS[0])
    network(1, 1, 2)
    send_x(1, 1)
    send_x(1, 2)
    def placed_from(q):
        source = (q * 21846) >> 16
        d, e = (z - (source >> 4)) & 7, (y - (source >> 1)) & 7
        return (q - source * NK) * 128 + e * 16 + d * 2 + ((source & 1) ^ c)

    place_v[...] = selector(BLOCK, BLOCK, placed_from)
    for t in range(1, len(ROUNDS) + 1):
        if t < len(ROUNDS):
            stage_x(*ROUNDS[t])
        stage_z(*ROUNDS[t - 1])
    for half in range(2):
        stage_y(half)

    wait_for(sx.at[pl.ds(0, 3)], sx_sem.at[0])
    wait_for(sx.at[3, :, 1], sx_sem.at[0])
    wait_for(zs.at[:, pl.ds(1, NZ - 1)], zs_sem.at[0])
    wait_for(ys.at[:, pl.ds(1, NY - 1)], ys_sem.at[0])
    for half in range(2):
        wait_for(t_v.at[half], t_sem.at[half])


def spread(t_ref, out_ref, t_v, o_v, t_sem, o_sem):
    pieces = [(n, pl.ds(b * 128, 128)) for n in range(2) for b in range(NK)]
    loads = [
        pltpu.make_async_copy(t_ref.at[n, :, lanes], t_v.at[m], t_sem.at[m])
        for m, (n, lanes) in enumerate(pieces)
    ]
    for load in loads:
        load.start()
    stores = []
    for m, (n, _) in enumerate(pieces):
        loads[m].wait()
        values = t_v[m].astype(F32)
        flag = values[OUT : OUT + 1]
        for far, weight in enumerate((flag, 1.0 - flag)):
            slot = m + 6 * far
            o_v[slot] = (values[:OUT] * weight).astype(BF16)
            store = pltpu.make_async_copy(
                o_v.at[slot], out_ref.at[:, pl.ds(slot * 128, 128)], o_sem.at[slot]
            )
            store.start()
            stores.append(store)
    for store in stores:
        store.wait()


def shards(
    features, daylit_list, daylit_count, in_weight, in_bias, mid_weight, mid_bias, out_weight, out_bias
):
    hbm = pl.BlockSpec(memory_space=pltpu.HBM)
    dma = pltpu.SemaphoreType.DMA
    halves = pl.pallas_call(
        kernel,
        out_shape=jax.ShapeDtypeStruct((2, LANES, BLOCK), BF16),
        in_specs=[pl.BlockSpec(memory_space=pltpu.SMEM)] + [hbm] * 8,
        out_specs=hbm,
        scratch_shapes=[
            pltpu.VMEM((COLS,), jnp.int32),
            pltpu.VMEM((4, FEAT, BLOCK), BF16),
            pltpu.VMEM((FEAT, HID), BF16),
            pltpu.VMEM((HID,), F32),
            pltpu.VMEM((2, HID, HID), BF16),
            pltpu.VMEM((2, HID), F32),
            pltpu.VMEM((LANES, HID), BF16),
            pltpu.VMEM((OUT,), F32),
            pltpu.VMEM((16, 128), F32),
            pltpu.VMEM((HID, FEAT), BF16),
            pltpu.VMEM((BLOCK, BLOCK), BF16),
            pltpu.VMEM((BLOCK, BLOCK), BF16),
            pltpu.VMEM((NX, NK, NC, ROWS, LANES), BF16),
            pltpu.VMEM((2, NK, 4, ROWS, LANES), BF16),
            pltpu.VMEM((2 * NK, NZ, 16, LANES), BF16),
            pltpu.VMEM((2 * NK, NZ, 16, LANES), BF16),
            pltpu.VMEM((2 * NK, NY, 16, LANES), BF16),
            pltpu.VMEM((2 * NK, NY, 16, LANES), BF16),
            pltpu.VMEM((2, LANES, BLOCK), BF16),
            dma((11,)),
            dma((1,)),
            dma((2, NK)),
            dma((1,)),
            dma((2 * NK,)),
            dma((1,)),
            dma((2 * NK,)),
            dma((2,)),
        ],
        compiler_params=pltpu.CompilerParams(
            collective_id=0, has_side_effects=True, vmem_limit_bytes=VMEM
        ),
    )(
        daylit_count,
        daylit_list,
        features,
        in_weight,
        in_bias,
        mid_weight,
        mid_bias,
        out_weight,
        out_bias,
    )
    return pl.pallas_call(
        spread,
        out_shape=jax.ShapeDtypeStruct((OUT, COLS), BF16),
        in_specs=[hbm],
        out_specs=hbm,
        scratch_shapes=[
            pltpu.VMEM((6, LANES, 128), BF16),
            pltpu.VMEM((12, OUT, 128), BF16),
            dma((6,)),
            dma((12,)),
        ],
        compiler_params=pltpu.CompilerParams(vmem_limit_bytes=VMEM),
    )(halves)


def solution(mesh):
    in_specs = (
        P(None, ("blk", "pair")),
        P(("blk", "pair")),
        P(("blk", "pair")),
        P(),
        P(),
        P(),
        P(),
        P(),
        P(),
    )
    out_specs = P(None, ("blk", "pair"))
    return jax.shard_map(shards, mesh=mesh, in_specs=in_specs, out_specs=out_specs, check_vma=False)
```

```python
import jax
import jax.numpy as jnp
from jax import lax
from jax.experimental import pallas as pl
from jax.experimental.pallas import tpu as pltpu
from jax.sharding import PartitionSpec as P

FEAT, HID, OUT = 557, 512, 368
LANES = 384
NX, NZ, NY, NC, NK = 4, 8, 8, 2, 3
BLOCK = NZ * NY * NC * NK
ROWS = NZ * NY
COLS = NX * BLOCK
OFFSETS = (1, 3, 2, 0)
RING = (4, 3, 5, 2, 6, 1, 7)
VMEM = 62 * 1024 * 1024
LOADED = (5, 6, 9, 10)
BF16, F32 = jnp.bfloat16, jnp.float32
MESH = pl.DeviceIdType.MESH


def nt(a, b):
    return lax.dot_general(a, b, (((1,), (1,)), ((), ())), preferred_element_type=F32)


def leaky(t):
    return jnp.maximum(t, 0.15 * t)


def selector(rows, cols, row_of_column):
    r = lax.broadcasted_iota(jnp.int32, (rows, cols), 0)
    wanted = row_of_column(lax.broadcasted_iota(jnp.int32, (1, cols), 1))
    return jnp.where(r == wanted, 1.0, 0.0).astype(BF16)


def column(row):
    return jnp.transpose(jnp.broadcast_to(row, (128, row.shape[1])))


def kernel(
    count_ref, list_ref, feat_ref, w0_ref, b0_ref, wm_ref, bm_ref, wo_ref, bo_ref, out_ref,
    list_v, f_v, w0_v, b0_v, wm_v, bm_v, wo_v, bo_v, day_v, w0t_v, pick_v, place_v, sx, rx, zs, zr, ys, yr, t_v,
    load_sem, sx_sem, rx_sem, zs_sem, zr_sem, ys_sem, yr_sem, t_sem,
):
    x = lax.axis_index("pair")
    blk = lax.axis_index("blk")
    z, y, c = blk // (NY * NC), (blk // NC) % NY, blk % NC

    def blk_of(zz, yy, cc):
        return (zz * NY + yy) * NC + cc

    sectors = [lax.rem(x + off, NX) for off in OFFSETS]

    def features_of(i):
        return (
            feat_ref.at[:, pl.ds(pl.multiple_of(sectors[i] * BLOCK, 128), BLOCK)],
            f_v.at[i],
        )

    loads = [
        pltpu.make_async_copy(src, dst, load_sem.at[n])
        for n, (src, dst) in enumerate(
            (
                (list_ref, list_v),
                (b0_ref, b0_v),
                (bm_ref, bm_v),
                (bo_ref, bo_v),
                (w0_ref, w0_v),
                features_of(0),
                features_of(1),
                (wm_ref, wm_v),
                (wo_ref, wo_v.at[pl.ds(0, OUT)]),
                features_of(2),
                features_of(3),
            )
        )
    ]
    for n in (4, 5, 6, 0, 1, 2, 3, 7, 8, 9, 10):
        loads[n].start()

    barrier = pltpu.get_barrier_semaphore()
    other = blk_of(z, y, 1 - c)
    cores = (blk, other)
    along_z = [blk_of(lax.rem(z + d, NZ), y, c) for d in range(NZ)]
    along_y = [blk_of(z, lax.rem(y + d, NY), c) for d in range(NY)]
    peers = [(other, a) for a in sectors]
    peers += [(blk, a) for a in sectors[:3]]
    peers += [(along_z[d], x) for d in RING]
    peers += [(along_y[d], x) for d in RING]
    def picked_from(half):
        def source(q):
            major, minor = (q >> 3) & 7, q & 7
            z_first = (((q >> 7) + half) & 1) == 0
            zz = (jnp.where(z_first, major, minor) + z) & 7
            yy = (jnp.where(z_first, minor, major) + y) & 7
            return (zz * NY + yy) * (NC * NK) + (((q >> 6) & 1) ^ c) * NK + (q >> 7)

        return source

    pick_v[0] = selector(BLOCK, BLOCK, picked_from(0))
    wo_v[pl.ds(OUT, LANES - OUT), :] = jnp.zeros((LANES - OUT, HID), BF16)

    eye = selector(256, 256, lambda r: r)
    turn = selector(128, 128, lambda q: (q & 7) * 16 + (q >> 3))

    for load in loads[:7]:
        load.wait()
    for peer in peers:
        pl.semaphore_signal(barrier, inc=1, device_id=peer, device_id_type=MESH)

    entries = list_v[...].reshape(1, COLS)
    usable = lax.broadcasted_iota(jnp.int32, (1, COLS), 1) < count_ref[0]
    high = jnp.where(usable, entries >> 7, -1)
    high = jnp.broadcast_to(high, (16, COLS)) == lax.broadcasted_iota(jnp.int32, (16, COLS), 0)
    low = jnp.broadcast_to(entries & 127, (128, COLS)) == lax.broadcasted_iota(
        jnp.int32, (128, COLS), 0
    )
    day_v[...] = nt(
        jnp.where(high, 1.0, 0.0).astype(BF16), jnp.where(low, 1.0, 0.0).astype(BF16)
    )
    biases = [column(b0_v[...].reshape(1, HID))]
    biases += [column(bm_v[pl.ds(n, 1), :]) for n in range(2)]
    bias_out = jnp.concatenate([bo_v[...].reshape(1, OUT), jnp.zeros((1, LANES - OUT), F32)], axis=1)
    biases.append(column(bias_out))
    first_half = jnp.where(x < NX // 2, 1.0, 0.0)

    for lo in range(0, HID, 256):
        w0t_v[pl.ds(lo, 256), :] = nt(eye, w0_v[:, pl.ds(lo, 256)]).astype(BF16)

    def network(half, first, count):
        picked, days = [], []
        lanes = pl.ds(first * 128, count * 128)
        for i in (2 * half, 2 * half + 1):
            if first == 0 and i >= 2:
                loads[LOADED[i]].wait()
            part = jnp.dot(f_v[i], pick_v[half, :, lanes], preferred_element_type=F32)
            picked.append(part.astype(BF16))
            day = jnp.concatenate(
                [day_v[pl.ds(sectors[i] * NK + t, 1), :] for t in range(NK)], axis=1
            )
            day = jnp.broadcast_to(jnp.where(day > 0.5, 1.0, 0.0), (16, BLOCK)).astype(BF16)
            days.append(jnp.dot(day, pick_v[half, :, lanes], preferred_element_type=F32)[:1])
        h, day = jnp.concatenate(picked, axis=1), jnp.concatenate(days, axis=1)
        tiled = [jnp.concatenate([b] * (2 * count), axis=1) for b in biases]
        h = jnp.dot(w0t_v[...], h, preferred_element_type=F32)
        h = leaky(h + tiled[0]).astype(BF16)
        if half == 0 and first == 0:
            loads[7].wait()
        for layer in range(2):
            h = jnp.dot(wm_v[layer], h, preferred_element_type=F32)
            h = leaky(h + tiled[1 + layer]).astype(BF16)
        if half == 0 and first == 0:
            loads[8].wait()
        v = jnp.dot(wo_v[...], h, preferred_element_type=F32) + tiled[3]
        feat = lax.broadcasted_iota(jnp.int32, v.shape, 0)
        v = (jnp.where(feat == OUT, first_half, v) * day).astype(BF16)
        for n in range(2 * count):
            rows = nt(eye[:128, :128], v[:, n * 128 : (n + 1) * 128]).astype(BF16)
            sx[2 * half + n // count, first + n % count] = rows.reshape(NC, ROWS, LANES)

    def send(src, dst, send_sem, recv_sem, device):
        pltpu.make_async_remote_copy(
            src_ref=src,
            dst_ref=dst,
            send_sem=send_sem,
            recv_sem=recv_sem,
            device_id=device,
            device_id_type=MESH,
        ).start()

    def send_x(half, k):
        for i in (2 * half, 2 * half + 1):
            for r in range(NC) if i < 3 else (1,):
                dst = rx.at[half, k, 2 * (i % 2) + r]
                device = (cores[r], sectors[i])
                send(sx.at[i, k, r], dst, sx_sem.at[0], rx_sem.at[half, k], device)

    def wait_for(view, sem):
        pltpu.make_async_copy(view, view, sem).wait()

    def axes_of(half, k):
        return (along_z, along_y) if (half + k) % 2 == 0 else (along_y, along_z)

    def stage_x(half, k):
        slots = (0, 1, 2, 3) if half == 0 else (0, 1, 3)
        wait_for(rx.at[half, k, pl.ds(0, len(slots))], rx_sem.at[half, k])
        sums = []
        for r in range(NC):
            near = sx[3, k, 0] if half == 1 and r == 0 else rx[half, k, 2 + r]
            total = rx[half, k, r].astype(F32) + near.astype(F32)
            sums.append(total.reshape(NZ, NY, LANES))
        merged = jnp.concatenate(sums, axis=1).astype(BF16)
        zs[half, k] = merged
        for d in RING:
            dst = zr.at[half, k, d]
            send(zs.at[half, k, d], dst, zs_sem.at[0], zr_sem.at[half, k], (axes_of(half, k)[0][d], x))
        zr[half, k, 0] = merged[0]

    def stage_z(half, k):
        wait_for(zr.at[half, k, pl.ds(1, NZ - 1)], zr_sem.at[half, k])
        rows = zr[half, k].reshape(128, LANES)
        turned = jnp.dot(turn, rows, preferred_element_type=F32)
        turned = turned.astype(BF16).reshape(NY, 16, LANES)
        ys[half, k] = turned
        for e in RING:
            dst = yr.at[half, k, e]
            send(ys.at[half, k, e], dst, ys_sem.at[0], yr_sem.at[half, k], (axes_of(half, k)[1][e], x))
        yr[half, k, 0] = turned[0]

    def stage_y(half):
        near = lax.rem(x + 1 + half, 2)
        total = 0.0
        for k in range(NK):
            wait_for(yr.at[half, k, pl.ds(1, NY - 1)], yr_sem.at[half, k])
            rows = yr[half, k].reshape(128, LANES)
            feats = [
                nt(eye[:128, :128], rows[:, n : n + 128]).astype(BF16)
                for n in range(0, LANES, 128)
            ]
            total = total + jnp.dot(
                jnp.concatenate(feats, axis=0),
                place_v[half, pl.ds(k * 128, 128), :],
                preferred_element_type=F32,
            )
        t_v[half] = total.astype(BF16)
        pltpu.make_async_copy(t_v.at[half], out_ref.at[near], t_sem.at[half]).start()

    chunks = [(half, k) for half in range(2) for k in range(NK)]
    network(0, 0, 1)
    pl.semaphore_wait(barrier, len(peers))
    send_x(0, 0)
    network(0, 1, 2)
    send_x(0, 1)
    pick_v[1] = selector(BLOCK, BLOCK, picked_from(1))
    network(1, 0, 1)
    send_x(0, 2)
    stage_x(0, 0)
    send_x(1, 0)
    network(1, 1, 2)
    def placed_from(half):
        def row(q):
            source = (q * 21846) >> 16
            k = q - source * NK
            d, e = (z - (source >> 4)) & 7, (y - (source >> 1)) & 7
            z_first = ((k + half) & 1) == 0
            major, minor = jnp.where(z_first, e, d), jnp.where(z_first, d, e)
            return k * 128 + major * 16 + minor * 2 + ((source & 1) ^ c)

        return row

    for half in range(2):
        place_v[half] = selector(BLOCK, BLOCK, placed_from(half))
    for t in range(1, len(chunks) + 1):
        if t < len(chunks):
            stage_x(*chunks[t])
        if t <= 2:
            send_x(1, t)
        stage_z(*chunks[t - 1])
    for half in range(2):
        stage_y(half)

    wait_for(sx.at[pl.ds(0, 3)], sx_sem.at[0])
    wait_for(sx.at[3, :, 1], sx_sem.at[0])
    wait_for(zs.at[:, :, pl.ds(1, NZ - 1)], zs_sem.at[0])
    wait_for(ys.at[:, :, pl.ds(1, NY - 1)], ys_sem.at[0])
    for half in range(2):
        wait_for(t_v.at[half], t_sem.at[half])


def spread(t_ref, out_ref, t_v, o_v, t_sem, o_sem):
    pieces = [(n, pl.ds(b * 128, 128)) for n in range(2) for b in range(NK)]
    loads = [
        pltpu.make_async_copy(t_ref.at[n, :, lanes], t_v.at[m], t_sem.at[m])
        for m, (n, lanes) in enumerate(pieces)
    ]
    for load in loads:
        load.start()
    stores = []
    for m, (n, _) in enumerate(pieces):
        loads[m].wait()
        values = t_v[m].astype(F32)
        flag = values[OUT : OUT + 1]
        for far, weight in enumerate((flag, 1.0 - flag)):
            slot = m + 6 * far
            o_v[slot] = (values[:OUT] * weight).astype(BF16)
            store = pltpu.make_async_copy(
                o_v.at[slot], out_ref.at[:, pl.ds(slot * 128, 128)], o_sem.at[slot]
            )
            store.start()
            stores.append(store)
    for store in stores:
        store.wait()


def shards(
    features, daylit_list, daylit_count, in_weight, in_bias, mid_weight, mid_bias, out_weight, out_bias
):
    hbm = pl.BlockSpec(memory_space=pltpu.HBM)
    dma = pltpu.SemaphoreType.DMA
    halves = pl.pallas_call(
        kernel,
        out_shape=jax.ShapeDtypeStruct((2, LANES, BLOCK), BF16),
        in_specs=[pl.BlockSpec(memory_space=pltpu.SMEM)] + [hbm] * 8,
        out_specs=hbm,
        scratch_shapes=[
            pltpu.VMEM((COLS,), jnp.int32),
            pltpu.VMEM((4, FEAT, BLOCK), BF16),
            pltpu.VMEM((FEAT, HID), BF16),
            pltpu.VMEM((HID,), F32),
            pltpu.VMEM((2, HID, HID), BF16),
            pltpu.VMEM((2, HID), F32),
            pltpu.VMEM((LANES, HID), BF16),
            pltpu.VMEM((OUT,), F32),
            pltpu.VMEM((16, 128), F32),
            pltpu.VMEM((HID, FEAT), BF16),
            pltpu.VMEM((2, BLOCK, BLOCK), BF16),
            pltpu.VMEM((2, BLOCK, BLOCK), BF16),
            pltpu.VMEM((NX, NK, NC, ROWS, LANES), BF16),
            pltpu.VMEM((2, NK, 4, ROWS, LANES), BF16),
            pltpu.VMEM((2, NK, NZ, 16, LANES), BF16),
            pltpu.VMEM((2, NK, NZ, 16, LANES), BF16),
            pltpu.VMEM((2, NK, NY, 16, LANES), BF16),
            pltpu.VMEM((2, NK, NY, 16, LANES), BF16),
            pltpu.VMEM((2, LANES, BLOCK), BF16),
            dma((11,)),
            dma((1,)),
            dma((2, NK)),
            dma((1,)),
            dma((2, NK)),
            dma((1,)),
            dma((2, NK)),
            dma((2,)),
        ],
        compiler_params=pltpu.CompilerParams(
            collective_id=0, has_side_effects=True, vmem_limit_bytes=VMEM
        ),
    )(
        daylit_count,
        daylit_list,
        features,
        in_weight,
        in_bias,
        mid_weight,
        mid_bias,
        out_weight,
        out_bias,
    )
    return pl.pallas_call(
        spread,
        out_shape=jax.ShapeDtypeStruct((OUT, COLS), BF16),
        in_specs=[hbm],
        out_specs=hbm,
        scratch_shapes=[
            pltpu.VMEM((6, LANES, 128), BF16),
            pltpu.VMEM((12, OUT, 128), BF16),
            dma((6,)),
            dma((12,)),
        ],
        compiler_params=pltpu.CompilerParams(vmem_limit_bytes=VMEM),
    )(halves)


def solution(mesh):
    in_specs = (
        P(None, ("blk", "pair")),
        P(("blk", "pair")),
        P(("blk", "pair")),
        P(),
        P(),
        P(),
        P(),
        P(),
        P(),
    )
    out_specs = P(None, ("blk", "pair"))
    return jax.shard_map(shards, mesh=mesh, in_specs=in_specs, out_specs=out_specs, check_vma=False)
```

```python
import jax
import jax.numpy as jnp
from jax import lax
from jax.experimental import pallas as pl
from jax.experimental.pallas import tpu as pltpu
from jax.sharding import PartitionSpec as P

FEAT, HID, OUT = 557, 512, 368
LANES = 384
NX, NZ, NY, NC, NK = 4, 8, 8, 2, 3
BLOCK = NZ * NY * NC * NK
ROWS = NZ * NY
COLS = NX * BLOCK
OFFSETS = (1, 3, 2, 0)
RING = (4, 3, 5, 2, 6, 1, 7)
VMEM = 62 * 1024 * 1024
LOADED = (5, 6, 9, 10)
BF16, F32 = jnp.bfloat16, jnp.float32
MESH = pl.DeviceIdType.MESH


def nt(a, b):
    return lax.dot_general(a, b, (((1,), (1,)), ((), ())), preferred_element_type=F32)


def leaky(t):
    return jnp.maximum(t, 0.15 * t)


def selector(rows, cols, row_of_column):
    r = lax.broadcasted_iota(jnp.int32, (rows, cols), 0)
    wanted = row_of_column(lax.broadcasted_iota(jnp.int32, (1, cols), 1))
    return jnp.where(r == wanted, 1.0, 0.0).astype(BF16)


def column(row):
    return jnp.transpose(jnp.broadcast_to(row, (128, row.shape[1])))


def kernel(
    count_ref, list_ref, feat_ref, w0_ref, b0_ref, wm_ref, bm_ref, wo_ref, bo_ref, out_ref,
    list_v, f_v, w0_v, b0_v, wm_v, bm_v, wo_v, bo_v, day_v, w0t_v, pick_v, place_v, sx, rx, zs, zr, ys, yr, t_v,
    load_sem, sx_sem, rx_sem, zs_sem, zr_sem, ys_sem, yr_sem, t_sem,
):
    x = lax.axis_index("pair")
    blk = lax.axis_index("blk")
    z, y, c = blk // (NY * NC), (blk // NC) % NY, blk % NC

    def blk_of(zz, yy, cc):
        return (zz * NY + yy) * NC + cc

    sectors = [lax.rem(x + off, NX) for off in OFFSETS]

    def features_of(i):
        return (
            feat_ref.at[:, pl.ds(pl.multiple_of(sectors[i] * BLOCK, 128), BLOCK)],
            f_v.at[i],
        )

    loads = [
        pltpu.make_async_copy(src, dst, load_sem.at[n])
        for n, (src, dst) in enumerate(
            (
                (list_ref, list_v),
                (b0_ref, b0_v),
                (bm_ref, bm_v),
                (bo_ref, bo_v),
                (w0_ref, w0_v),
                features_of(0),
                features_of(1),
                (wm_ref, wm_v),
                (wo_ref, wo_v.at[pl.ds(0, OUT)]),
                features_of(2),
                features_of(3),
            )
        )
    ]
    for n in (4, 5, 6, 0, 1, 2, 3, 7, 8, 9, 10):
        loads[n].start()

    barrier = pltpu.get_barrier_semaphore()
    other = blk_of(z, y, 1 - c)
    core_0, core_1 = blk_of(z, y, 0), blk_of(z, y, 1)
    along_z = [blk_of(lax.rem(z + d, NZ), y, c) for d in range(NZ)]
    along_y = [blk_of(z, lax.rem(y + d, NY), c) for d in range(NY)]
    peers = [(other, a) for a in sectors]
    peers += [(blk, a) for a in sectors[:3]]
    peers += [(along_z[d], x) for d in RING]
    peers += [(along_y[d], x) for d in RING]
    def picked_from(q):
        zz, yy = ((q >> 3) + z) & 7, (q + y) & 7
        return (zz * NY + yy) * (NC * NK) + (((q >> 6) & 1) ^ c) * NK + (q >> 7)

    pick_v[...] = selector(BLOCK, BLOCK, picked_from)
    wo_v[pl.ds(OUT, LANES - OUT), :] = jnp.zeros((LANES - OUT, HID), BF16)

    eye = selector(256, 256, lambda r: r)
    turn = selector(128, 128, lambda q: (q & 7) * 16 + (q >> 3))

    for load in loads[:7]:
        load.wait()
    for peer in peers:
        pl.semaphore_signal(barrier, inc=1, device_id=peer, device_id_type=MESH)

    entries = list_v[...].reshape(1, COLS)
    usable = lax.broadcasted_iota(jnp.int32, (1, COLS), 1) < count_ref[0]
    high = jnp.where(usable, entries >> 7, -1)
    high = jnp.broadcast_to(high, (16, COLS)) == lax.broadcasted_iota(jnp.int32, (16, COLS), 0)
    low = jnp.broadcast_to(entries & 127, (128, COLS)) == lax.broadcasted_iota(
        jnp.int32, (128, COLS), 0
    )
    day_v[...] = nt(
        jnp.where(high, 1.0, 0.0).astype(BF16), jnp.where(low, 1.0, 0.0).astype(BF16)
    )
    biases = [column(b0_v[...].reshape(1, HID))]
    biases += [column(bm_v[pl.ds(n, 1), :]) for n in range(2)]
    bias_out = jnp.concatenate([bo_v[...].reshape(1, OUT), jnp.zeros((1, LANES - OUT), F32)], axis=1)
    biases.append(column(bias_out))
    first_half = jnp.where(x < NX // 2, 1.0, 0.0)

    for lo in range(0, HID, 256):
        w0t_v[pl.ds(lo, 256), :] = nt(eye, w0_v[:, pl.ds(lo, 256)]).astype(BF16)

    def network(half, first, count):
        picked, days = [], []
        lanes = pl.ds(first * 128, count * 128)
        for i in (2 * half, 2 * half + 1):
            if first == 0 and i >= 2:
                loads[LOADED[i]].wait()
            part = jnp.dot(f_v[i], pick_v[:, lanes], preferred_element_type=F32)
            picked.append(part.astype(BF16))
            day = jnp.concatenate(
                [day_v[pl.ds(sectors[i] * NK + t, 1), :] for t in range(NK)], axis=1
            )
            day = jnp.broadcast_to(jnp.where(day > 0.5, 1.0, 0.0), (16, BLOCK)).astype(BF16)
            days.append(jnp.dot(day, pick_v[:, lanes], preferred_element_type=F32)[:1])
        h, day = jnp.concatenate(picked, axis=1), jnp.concatenate(days, axis=1)
        tiled = [jnp.concatenate([b] * (2 * count), axis=1) for b in biases]
        h = jnp.dot(w0t_v[...], h, preferred_element_type=F32)
        h = leaky(h + tiled[0]).astype(BF16)
        if half == 0 and first == 0:
            loads[7].wait()
        for layer in range(2):
            h = jnp.dot(wm_v[layer], h, preferred_element_type=F32)
            h = leaky(h + tiled[1 + layer]).astype(BF16)
        if half == 0 and first == 0:
            loads[8].wait()
        v = jnp.dot(wo_v[...], h, preferred_element_type=F32) + tiled[3]
        feat = lax.broadcasted_iota(jnp.int32, v.shape, 0)
        v = (jnp.where(feat == OUT, first_half, v) * day).astype(BF16)
        for n in range(2 * count):
            rows = nt(eye[:128, :128], v[:, n * 128 : (n + 1) * 128]).astype(BF16)
            sx[2 * half + n // count, first + n % count] = rows.reshape(NC, ROWS, LANES)

    def send(src, dst, send_sem, recv_sem, device):
        pltpu.make_async_remote_copy(
            src_ref=src,
            dst_ref=dst,
            send_sem=send_sem,
            recv_sem=recv_sem,
            device_id=device,
            device_id_type=MESH,
        ).start()

    def send_x(half, k):
        for i in (2 * half, 2 * half + 1):
            for r, core in ((c, core_0), (1 - c, core_1)) if i < 3 else ((1, other),):
                dst = rx.at[half, k, 2 * (i % 2) + r]
                device = (core, sectors[i])
                send(sx.at[i, k, r], dst, sx_sem.at[0], rx_sem.at[half, k], device)

    def wait_for(view, sem):
        pltpu.make_async_copy(view, view, sem).wait()

    def stage_x(half, k):
        slots = (0, 1, 2, 3) if half == 0 else (0, 1, 3)
        wait_for(rx.at[half, k, pl.ds(0, len(slots))], rx_sem.at[half, k])
        sums = []
        for r in range(NC):
            near = sx[3, k, 0] if half == 1 and r == 0 else rx[half, k, 2 + r]
            total = rx[half, k, r].astype(F32) + near.astype(F32)
            sums.append(total.reshape(NZ, NY, LANES))
        merged = jnp.concatenate(sums, axis=1).astype(BF16)
        zs[half, k] = merged
        for d in RING:
            dst = zr.at[half, k, d]
            send(zs.at[half, k, d], dst, zs_sem.at[0], zr_sem.at[half, k], (along_z[d], x))
        zr[half, k, 0] = merged[0]

    def stage_z(half, k):
        wait_for(zr.at[half, k, pl.ds(1, NZ - 1)], zr_sem.at[half, k])
        rows = zr[half, k].reshape(128, LANES)
        turned = jnp.dot(turn, rows, preferred_element_type=F32)
        turned = turned.astype(BF16).reshape(NY, 16, LANES)
        ys[half, k] = turned
        for e in RING:
            dst = yr.at[half, k, e]
            send(ys.at[half, k, e], dst, ys_sem.at[0], yr_sem.at[half, k], (along_y[e], x))
        yr[half, k, 0] = turned[0]

    def stage_y(half):
        near = lax.rem(x + 1 + half, 2)
        total = 0.0
        for k in range(NK):
            wait_for(yr.at[half, k, pl.ds(1, NY - 1)], yr_sem.at[half, k])
            rows = yr[half, k].reshape(128, LANES)
            feats = [
                nt(eye[:128, :128], rows[:, n : n + 128]).astype(BF16)
                for n in range(0, LANES, 128)
            ]
            total = total + jnp.dot(
                jnp.concatenate(feats, axis=0),
                place_v[pl.ds(k * 128, 128), :],
                preferred_element_type=F32,
            )
        t_v[half] = total.astype(BF16)
        pltpu.make_async_copy(t_v.at[half], out_ref.at[near], t_sem.at[half]).start()

    chunks = [(half, k) for half in range(2) for k in range(NK)]
    network(0, 0, 1)
    pl.semaphore_wait(barrier, len(peers))
    send_x(0, 0)
    network(0, 1, 2)
    send_x(0, 1)
    network(1, 0, 1)
    send_x(0, 2)
    stage_x(0, 0)
    send_x(1, 0)
    network(1, 1, 2)
    def placed_from(q):
        source = (q * 21846) >> 16
        d, e = (z - (source >> 4)) & 7, (y - (source >> 1)) & 7
        return (q - source * NK) * 128 + e * 16 + d * 2 + ((source & 1) ^ c)

    place_v[...] = selector(BLOCK, BLOCK, placed_from)
    for t in range(1, len(chunks) + 1):
        if t < len(chunks):
            stage_x(*chunks[t])
        if t <= 2:
            send_x(1, t)
        stage_z(*chunks[t - 1])
    for half in range(2):
        stage_y(half)

    wait_for(sx.at[pl.ds(0, 3)], sx_sem.at[0])
    wait_for(sx.at[3, :, 1], sx_sem.at[0])
    wait_for(zs.at[:, :, pl.ds(1, NZ - 1)], zs_sem.at[0])
    wait_for(ys.at[:, :, pl.ds(1, NY - 1)], ys_sem.at[0])
    for half in range(2):
        wait_for(t_v.at[half], t_sem.at[half])


def spread(t_ref, out_ref, t_v, o_v, t_sem, o_sem):
    pieces = [(n, pl.ds(b * 128, 128)) for n in range(2) for b in range(NK)]
    loads = [
        pltpu.make_async_copy(t_ref.at[n, :, lanes], t_v.at[m], t_sem.at[m])
        for m, (n, lanes) in enumerate(pieces)
    ]
    for load in loads:
        load.start()
    stores = []
    for m, (n, _) in enumerate(pieces):
        loads[m].wait()
        values = t_v[m].astype(F32)
        flag = values[OUT : OUT + 1]
        for far, weight in enumerate((flag, 1.0 - flag)):
            slot = m + 6 * far
            o_v[slot] = (values[:OUT] * weight).astype(BF16)
            store = pltpu.make_async_copy(
                o_v.at[slot], out_ref.at[:, pl.ds(slot * 128, 128)], o_sem.at[slot]
            )
            store.start()
            stores.append(store)
    for store in stores:
        store.wait()


def shards(
    features, daylit_list, daylit_count, in_weight, in_bias, mid_weight, mid_bias, out_weight, out_bias
):
    hbm = pl.BlockSpec(memory_space=pltpu.HBM)
    dma = pltpu.SemaphoreType.DMA
    halves = pl.pallas_call(
        kernel,
        out_shape=jax.ShapeDtypeStruct((2, LANES, BLOCK), BF16),
        in_specs=[pl.BlockSpec(memory_space=pltpu.SMEM)] + [hbm] * 8,
        out_specs=hbm,
        scratch_shapes=[
            pltpu.VMEM((COLS,), jnp.int32),
            pltpu.VMEM((4, FEAT, BLOCK), BF16),
            pltpu.VMEM((FEAT, HID), BF16),
            pltpu.VMEM((HID,), F32),
            pltpu.VMEM((2, HID, HID), BF16),
            pltpu.VMEM((2, HID), F32),
            pltpu.VMEM((LANES, HID), BF16),
            pltpu.VMEM((OUT,), F32),
            pltpu.VMEM((16, 128), F32),
            pltpu.VMEM((HID, FEAT), BF16),
            pltpu.VMEM((BLOCK, BLOCK), BF16),
            pltpu.VMEM((BLOCK, BLOCK), BF16),
            pltpu.VMEM((NX, NK, NC, ROWS, LANES), BF16),
            pltpu.VMEM((2, NK, 4, ROWS, LANES), BF16),
            pltpu.VMEM((2, NK, NZ, 16, LANES), BF16),
            pltpu.VMEM((2, NK, NZ, 16, LANES), BF16),
            pltpu.VMEM((2, NK, NY, 16, LANES), BF16),
            pltpu.VMEM((2, NK, NY, 16, LANES), BF16),
            pltpu.VMEM((2, LANES, BLOCK), BF16),
            dma((11,)),
            dma((1,)),
            dma((2, NK)),
            dma((1,)),
            dma((2, NK)),
            dma((1,)),
            dma((2, NK)),
            dma((2,)),
        ],
        compiler_params=pltpu.CompilerParams(
            collective_id=0, has_side_effects=True, vmem_limit_bytes=VMEM
        ),
    )(
        daylit_count,
        daylit_list,
        features,
        in_weight,
        in_bias,
        mid_weight,
        mid_bias,
        out_weight,
        out_bias,
    )
    return pl.pallas_call(
        spread,
        out_shape=jax.ShapeDtypeStruct((OUT, COLS), BF16),
        in_specs=[hbm],
        out_specs=hbm,
        scratch_shapes=[
            pltpu.VMEM((6, LANES, 128), BF16),
            pltpu.VMEM((12, OUT, 128), BF16),
            dma((6,)),
            dma((12,)),
        ],
        compiler_params=pltpu.CompilerParams(vmem_limit_bytes=VMEM),
    )(halves)


def solution(mesh):
    in_specs = (
        P(None, ("blk", "pair")),
        P(("blk", "pair")),
        P(("blk", "pair")),
        P(),
        P(),
        P(),
        P(),
        P(),
        P(),
    )
    out_specs = P(None, ("blk", "pair"))
    return jax.shard_map(shards, mesh=mesh, in_specs=in_specs, out_specs=out_specs, check_vma=False)
```

```python
import jax
import jax.numpy as jnp
from jax import lax
from jax.experimental import pallas as pl
from jax.experimental.pallas import tpu as pltpu
from jax.sharding import PartitionSpec as P

FEAT, HID, OUT = 557, 512, 368
LANES = 384
NX, NZ, NY, NC, NK = 4, 8, 8, 2, 3
BLOCK = NZ * NY * NC * NK
ROWS = NZ * NY
COLS = NX * BLOCK
OFFSETS = (1, 3, 2, 0)
RING = (4, 3, 5, 2, 6, 1, 7)
VMEM = 62 * 1024 * 1024
LOADED = (5, 6, 9, 10)
BF16, F32 = jnp.bfloat16, jnp.float32
MESH = pl.DeviceIdType.MESH


def nt(a, b):
    return lax.dot_general(a, b, (((1,), (1,)), ((), ())), preferred_element_type=F32)


def leaky(t):
    return jnp.maximum(t, 0.15 * t)


def selector(rows, cols, row_of_column):
    r = lax.broadcasted_iota(jnp.int32, (rows, cols), 0)
    wanted = row_of_column(lax.broadcasted_iota(jnp.int32, (1, cols), 1))
    return jnp.where(r == wanted, 1.0, 0.0).astype(BF16)


def column(row):
    return jnp.transpose(jnp.broadcast_to(row, (128, row.shape[1])))


def kernel(
    count_ref, list_ref, feat_ref, w0_ref, b0_ref, wm_ref, bm_ref, wo_ref, bo_ref, out_ref,
    list_v, f_v, w0_v, b0_v, wm_v, bm_v, wo_v, bo_v, day_v, w0t_v, pick_v, place_v, sx, rx, zs, zr, ys, yr, t_v,
    load_sem, sx_sem, rx_sem, zs_sem, zr_sem, ys_sem, yr_sem, t_sem,
):
    x = lax.axis_index("pair")
    blk = lax.axis_index("blk")
    z, y, c = blk // (NY * NC), (blk // NC) % NY, blk % NC

    def blk_of(zz, yy, cc):
        return (zz * NY + yy) * NC + cc

    sectors = [lax.rem(x + off, NX) for off in OFFSETS]

    def features_of(i):
        return (
            feat_ref.at[:, pl.ds(pl.multiple_of(sectors[i] * BLOCK, 128), BLOCK)],
            f_v.at[i],
        )

    loads = [
        pltpu.make_async_copy(src, dst, load_sem.at[n])
        for n, (src, dst) in enumerate(
            (
                (list_ref, list_v),
                (b0_ref, b0_v),
                (bm_ref, bm_v),
                (bo_ref, bo_v),
                (w0_ref, w0_v),
                features_of(0),
                features_of(1),
                (wm_ref, wm_v),
                (wo_ref, wo_v.at[pl.ds(0, OUT)]),
                features_of(2),
                features_of(3),
            )
        )
    ]
    for n in (4, 5, 6, 0, 1, 2, 3, 7, 8, 9, 10):
        loads[n].start()

    barrier = pltpu.get_barrier_semaphore()
    other = blk_of(z, y, 1 - c)
    cores = (blk, other)
    along_z = [blk_of(lax.rem(z + d, NZ), y, c) for d in range(NZ)]
    along_y = [blk_of(z, lax.rem(y + d, NY), c) for d in range(NY)]
    first_axis = [along_z[d] * (1 - c) + along_y[d] * c for d in range(NZ)]
    second_axis = [along_y[d] * (1 - c) + along_z[d] * c for d in range(NZ)]
    peers = [(other, a) for a in sectors]
    peers += [(blk, a) for a in sectors[:3]]
    peers += [(along_z[d], x) for d in RING]
    peers += [(along_y[d], x) for d in RING]
    def picked_from(q):
        core = ((q >> 6) & 1) ^ c
        major, minor = (q >> 3) & 7, q & 7
        zz = (major * (1 - core) + minor * core + z) & 7
        yy = (minor * (1 - core) + major * core + y) & 7
        return (zz * NY + yy) * (NC * NK) + core * NK + (q >> 7)

    pick_v[...] = selector(BLOCK, BLOCK, picked_from)
    wo_v[pl.ds(OUT, LANES - OUT), :] = jnp.zeros((LANES - OUT, HID), BF16)

    eye = selector(256, 256, lambda r: r)
    turn = selector(128, 128, lambda q: (q & 7) * 16 + (q >> 3))

    for load in loads[:7]:
        load.wait()
    for peer in peers:
        pl.semaphore_signal(barrier, inc=1, device_id=peer, device_id_type=MESH)

    entries = list_v[...].reshape(1, COLS)
    usable = lax.broadcasted_iota(jnp.int32, (1, COLS), 1) < count_ref[0]
    high = jnp.where(usable, entries >> 7, -1)
    high = jnp.broadcast_to(high, (16, COLS)) == lax.broadcasted_iota(jnp.int32, (16, COLS), 0)
    low = jnp.broadcast_to(entries & 127, (128, COLS)) == lax.broadcasted_iota(
        jnp.int32, (128, COLS), 0
    )
    day_v[...] = nt(
        jnp.where(high, 1.0, 0.0).astype(BF16), jnp.where(low, 1.0, 0.0).astype(BF16)
    )
    biases = [column(b0_v[...].reshape(1, HID))]
    biases += [column(bm_v[pl.ds(n, 1), :]) for n in range(2)]
    bias_out = jnp.concatenate([bo_v[...].reshape(1, OUT), jnp.zeros((1, LANES - OUT), F32)], axis=1)
    biases.append(column(bias_out))
    first_half = jnp.where(x < NX // 2, 1.0, 0.0)

    for lo in range(0, HID, 256):
        w0t_v[pl.ds(lo, 256), :] = nt(eye, w0_v[:, pl.ds(lo, 256)]).astype(BF16)

    def network(half, first, count):
        picked, days = [], []
        lanes = pl.ds(first * 128, count * 128)
        for i in (2 * half, 2 * half + 1):
            if first == 0 and i >= 2:
                loads[LOADED[i]].wait()
            part = jnp.dot(f_v[i], pick_v[:, lanes], preferred_element_type=F32)
            picked.append(part.astype(BF16))
            day = jnp.concatenate(
                [day_v[pl.ds(sectors[i] * NK + t, 1), :] for t in range(NK)], axis=1
            )
            day = jnp.broadcast_to(jnp.where(day > 0.5, 1.0, 0.0), (16, BLOCK)).astype(BF16)
            days.append(jnp.dot(day, pick_v[:, lanes], preferred_element_type=F32)[:1])
        h, day = jnp.concatenate(picked, axis=1), jnp.concatenate(days, axis=1)
        tiled = [jnp.concatenate([b] * (2 * count), axis=1) for b in biases]
        h = jnp.dot(w0t_v[...], h, preferred_element_type=F32)
        h = leaky(h + tiled[0]).astype(BF16)
        if half == 0 and first == 0:
            loads[7].wait()
        for layer in range(2):
            h = jnp.dot(wm_v[layer], h, preferred_element_type=F32)
            h = leaky(h + tiled[1 + layer]).astype(BF16)
        if half == 0 and first == 0:
            loads[8].wait()
        v = jnp.dot(wo_v[...], h, preferred_element_type=F32) + tiled[3]
        feat = lax.broadcasted_iota(jnp.int32, v.shape, 0)
        v = (jnp.where(feat == OUT, first_half, v) * day).astype(BF16)
        for n in range(2 * count):
            rows = nt(eye[:128, :128], v[:, n * 128 : (n + 1) * 128]).astype(BF16)
            sx[2 * half + n // count, first + n % count] = rows.reshape(NC, ROWS, LANES)

    def send(src, dst, send_sem, recv_sem, device):
        pltpu.make_async_remote_copy(
            src_ref=src,
            dst_ref=dst,
            send_sem=send_sem,
            recv_sem=recv_sem,
            device_id=device,
            device_id_type=MESH,
        ).start()

    def send_x(half, k):
        for i in (2 * half, 2 * half + 1):
            for r in range(NC) if i < 3 else (1,):
                dst = rx.at[half, k, 2 * (i % 2) + r]
                device = (cores[r], sectors[i])
                send(sx.at[i, k, r], dst, sx_sem.at[0], rx_sem.at[half, k], device)

    def wait_for(view, sem):
        pltpu.make_async_copy(view, view, sem).wait()

    def stage_x(half, k):
        slots = (0, 1, 2, 3) if half == 0 else (0, 1, 3)
        wait_for(rx.at[half, k, pl.ds(0, len(slots))], rx_sem.at[half, k])
        sums = []
        for r in range(NC):
            near = sx[3, k, 0] if half == 1 and r == 0 else rx[half, k, 2 + r]
            total = rx[half, k, r].astype(F32) + near.astype(F32)
            sums.append(total.reshape(NZ, NY, LANES))
        merged = jnp.concatenate(sums, axis=1).astype(BF16)
        zs[half, k] = merged
        for d in RING:
            dst = zr.at[half, k, d]
            send(zs.at[half, k, d], dst, zs_sem.at[0], zr_sem.at[half, k], (first_axis[d], x))
        zr[half, k, 0] = merged[0]

    def stage_z(half, k):
        wait_for(zr.at[half, k, pl.ds(1, NZ - 1)], zr_sem.at[half, k])
        rows = zr[half, k].reshape(128, LANES)
        turned = jnp.dot(turn, rows, preferred_element_type=F32)
        turned = turned.astype(BF16).reshape(NY, 16, LANES)
        ys[half, k] = turned
        for e in RING:
            dst = yr.at[half, k, e]
            send(ys.at[half, k, e], dst, ys_sem.at[0], yr_sem.at[half, k], (second_axis[e], x))
        yr[half, k, 0] = turned[0]

    def stage_y(half):
        near = lax.rem(x + 1 + half, 2)
        total = 0.0
        for k in range(NK):
            wait_for(yr.at[half, k, pl.ds(1, NY - 1)], yr_sem.at[half, k])
            rows = yr[half, k].reshape(128, LANES)
            feats = [
                nt(eye[:128, :128], rows[:, n : n + 128]).astype(BF16)
                for n in range(0, LANES, 128)
            ]
            total = total + jnp.dot(
                jnp.concatenate(feats, axis=0),
                place_v[pl.ds(k * 128, 128), :],
                preferred_element_type=F32,
            )
        t_v[half] = total.astype(BF16)
        pltpu.make_async_copy(t_v.at[half], out_ref.at[near], t_sem.at[half]).start()

    chunks = [(half, k) for half in range(2) for k in range(NK)]
    network(0, 0, 1)
    pl.semaphore_wait(barrier, len(peers))
    send_x(0, 0)
    network(0, 1, 2)
    send_x(0, 1)
    network(1, 0, 1)
    send_x(0, 2)
    stage_x(0, 0)
    send_x(1, 0)
    network(1, 1, 2)
    def placed_from(q):
        source = (q * 21846) >> 16
        d, e = (z - (source >> 4)) & 7, (y - (source >> 1)) & 7
        major, minor = e * (1 - c) + d * c, d * (1 - c) + e * c
        return (q - source * NK) * 128 + major * 16 + minor * 2 + ((source & 1) ^ c)

    place_v[...] = selector(BLOCK, BLOCK, placed_from)
    for t in range(1, len(chunks) + 1):
        if t < len(chunks):
            stage_x(*chunks[t])
        if t <= 2:
            send_x(1, t)
        stage_z(*chunks[t - 1])
    for half in range(2):
        stage_y(half)

    wait_for(sx.at[pl.ds(0, 3)], sx_sem.at[0])
    wait_for(sx.at[3, :, 1], sx_sem.at[0])
    wait_for(zs.at[:, :, pl.ds(1, NZ - 1)], zs_sem.at[0])
    wait_for(ys.at[:, :, pl.ds(1, NY - 1)], ys_sem.at[0])
    for half in range(2):
        wait_for(t_v.at[half], t_sem.at[half])


def spread(t_ref, out_ref, t_v, o_v, t_sem, o_sem):
    pieces = [(n, pl.ds(b * 128, 128)) for n in range(2) for b in range(NK)]
    loads = [
        pltpu.make_async_copy(t_ref.at[n, :, lanes], t_v.at[m], t_sem.at[m])
        for m, (n, lanes) in enumerate(pieces)
    ]
    for load in loads:
        load.start()
    stores = []
    for m, (n, _) in enumerate(pieces):
        loads[m].wait()
        values = t_v[m].astype(F32)
        flag = values[OUT : OUT + 1]
        for far, weight in enumerate((flag, 1.0 - flag)):
            slot = m + 6 * far
            o_v[slot] = (values[:OUT] * weight).astype(BF16)
            store = pltpu.make_async_copy(
                o_v.at[slot], out_ref.at[:, pl.ds(slot * 128, 128)], o_sem.at[slot]
            )
            store.start()
            stores.append(store)
    for store in stores:
        store.wait()


def shards(
    features, daylit_list, daylit_count, in_weight, in_bias, mid_weight, mid_bias, out_weight, out_bias
):
    hbm = pl.BlockSpec(memory_space=pltpu.HBM)
    dma = pltpu.SemaphoreType.DMA
    halves = pl.pallas_call(
        kernel,
        out_shape=jax.ShapeDtypeStruct((2, LANES, BLOCK), BF16),
        in_specs=[pl.BlockSpec(memory_space=pltpu.SMEM)] + [hbm] * 8,
        out_specs=hbm,
        scratch_shapes=[
            pltpu.VMEM((COLS,), jnp.int32),
            pltpu.VMEM((4, FEAT, BLOCK), BF16),
            pltpu.VMEM((FEAT, HID), BF16),
            pltpu.VMEM((HID,), F32),
            pltpu.VMEM((2, HID, HID), BF16),
            pltpu.VMEM((2, HID), F32),
            pltpu.VMEM((LANES, HID), BF16),
            pltpu.VMEM((OUT,), F32),
            pltpu.VMEM((16, 128), F32),
            pltpu.VMEM((HID, FEAT), BF16),
            pltpu.VMEM((BLOCK, BLOCK), BF16),
            pltpu.VMEM((BLOCK, BLOCK), BF16),
            pltpu.VMEM((NX, NK, NC, ROWS, LANES), BF16),
            pltpu.VMEM((2, NK, 4, ROWS, LANES), BF16),
            pltpu.VMEM((2, NK, NZ, 16, LANES), BF16),
            pltpu.VMEM((2, NK, NZ, 16, LANES), BF16),
            pltpu.VMEM((2, NK, NY, 16, LANES), BF16),
            pltpu.VMEM((2, NK, NY, 16, LANES), BF16),
            pltpu.VMEM((2, LANES, BLOCK), BF16),
            dma((11,)),
            dma((1,)),
            dma((2, NK)),
            dma((1,)),
            dma((2, NK)),
            dma((1,)),
            dma((2, NK)),
            dma((2,)),
        ],
        compiler_params=pltpu.CompilerParams(
            collective_id=0, has_side_effects=True, vmem_limit_bytes=VMEM
        ),
    )(
        daylit_count,
        daylit_list,
        features,
        in_weight,
        in_bias,
        mid_weight,
        mid_bias,
        out_weight,
        out_bias,
    )
    return pl.pallas_call(
        spread,
        out_shape=jax.ShapeDtypeStruct((OUT, COLS), BF16),
        in_specs=[hbm],
        out_specs=hbm,
        scratch_shapes=[
            pltpu.VMEM((6, LANES, 128), BF16),
            pltpu.VMEM((12, OUT, 128), BF16),
            dma((6,)),
            dma((12,)),
        ],
        compiler_params=pltpu.CompilerParams(vmem_limit_bytes=VMEM),
    )(halves)


def solution(mesh):
    in_specs = (
        P(None, ("blk", "pair")),
        P(("blk", "pair")),
        P(("blk", "pair")),
        P(),
        P(),
        P(),
        P(),
        P(),
        P(),
    )
    out_specs = P(None, ("blk", "pair"))
    return jax.shard_map(shards, mesh=mesh, in_specs=in_specs, out_specs=out_specs, check_vma=False)
```

```python
import jax
import jax.numpy as jnp
from jax import lax
from jax.experimental import pallas as pl
from jax.experimental.pallas import tpu as pltpu
from jax.sharding import PartitionSpec as P

FEAT, HID, OUT = 557, 512, 368
LANES = 384
NX, NZ, NY, NC, NK = 4, 8, 8, 2, 3
BLOCK = NZ * NY * NC * NK
ROWS = NZ * NY
COLS = NX * BLOCK
OFFSETS = (1, 3, 2, 0)
RING = (4, 3, 5, 2, 6, 1, 7)
VMEM = 62 * 1024 * 1024
LOADED = (5, 6, 9, 10)
BF16, F32 = jnp.bfloat16, jnp.float32
MESH = pl.DeviceIdType.MESH


def nt(a, b):
    return lax.dot_general(a, b, (((1,), (1,)), ((), ())), preferred_element_type=F32)


def leaky(t):
    return jnp.maximum(t, 0.15 * t)


def selector(rows, cols, row_of_column):
    r = lax.broadcasted_iota(jnp.int32, (rows, cols), 0)
    wanted = row_of_column(lax.broadcasted_iota(jnp.int32, (1, cols), 1))
    return jnp.where(r == wanted, 1.0, 0.0).astype(BF16)


def column(row):
    return jnp.transpose(jnp.broadcast_to(row, (128, row.shape[1])))


def kernel(
    count_ref, list_ref, feat_ref, w0_ref, b0_ref, wm_ref, bm_ref, wo_ref, bo_ref, out_ref,
    list_v, f_v, w0_v, b0_v, wm_v, bm_v, wo_v, bo_v, day_v, w0t_v, pick_v, place_v, sx, rx, zs, zr, ys, yr, t_v,
    load_sem, sx_sem, rx_sem, zs_sem, zr_sem, ys_sem, yr_sem, t_sem,
):
    x = lax.axis_index("pair")
    blk = lax.axis_index("blk")
    z, y, c = blk // (NY * NC), (blk // NC) % NY, blk % NC

    def blk_of(zz, yy, cc):
        return (zz * NY + yy) * NC + cc

    sectors = [lax.rem(x + off, NX) for off in OFFSETS]

    def features_of(i):
        return (
            feat_ref.at[:, pl.ds(pl.multiple_of(sectors[i] * BLOCK, 128), BLOCK)],
            f_v.at[i],
        )

    loads = [
        pltpu.make_async_copy(src, dst, load_sem.at[n])
        for n, (src, dst) in enumerate(
            (
                (list_ref, list_v),
                (b0_ref, b0_v),
                (bm_ref, bm_v),
                (bo_ref, bo_v),
                (w0_ref, w0_v),
                features_of(0),
                features_of(1),
                (wm_ref, wm_v),
                (wo_ref, wo_v.at[pl.ds(0, OUT)]),
                features_of(2),
                features_of(3),
            )
        )
    ]
    for n in (4, 5, 6, 0, 1, 2, 3, 7, 8, 9, 10):
        loads[n].start()

    barrier = pltpu.get_barrier_semaphore()
    other = blk_of(z, y, 1 - c)
    cores = (blk, other)
    along_z = [blk_of(lax.rem(z + d, NZ), y, c) for d in range(NZ)]
    along_y = [blk_of(z, lax.rem(y + d, NY), c) for d in range(NY)]
    first_axis = [along_z[d] * (1 - c) + along_y[d] * c for d in range(NZ)]
    second_axis = [along_y[d] * (1 - c) + along_z[d] * c for d in range(NZ)]
    peers = [(other, a) for a in sectors]
    peers += [(blk, a) for a in sectors[:3]]
    peers += [(along_z[d], x) for d in RING]
    peers += [(along_y[d], x) for d in RING]
    def picked_from(q):
        core = ((q >> 6) & 1) ^ c
        major, minor = (q >> 3) & 7, q & 7
        zz = (major * (1 - core) + minor * core + z) & 7
        yy = (minor * (1 - core) + major * core + y) & 7
        return (zz * NY + yy) * (NC * NK) + core * NK + (q >> 7)

    pick_v[...] = selector(BLOCK, BLOCK, picked_from)
    wo_v[pl.ds(OUT, LANES - OUT), :] = jnp.zeros((LANES - OUT, HID), BF16)

    eye = selector(256, 256, lambda r: r)
    turn = selector(128, 128, lambda q: (q & 7) * 16 + (q >> 3))

    for load in loads[:7]:
        load.wait()
    for peer in peers:
        pl.semaphore_signal(barrier, inc=1, device_id=peer, device_id_type=MESH)

    entries = list_v[...].reshape(1, COLS)
    usable = lax.broadcasted_iota(jnp.int32, (1, COLS), 1) < count_ref[0]
    high = jnp.where(usable, entries >> 7, -1)
    high = jnp.broadcast_to(high, (16, COLS)) == lax.broadcasted_iota(jnp.int32, (16, COLS), 0)
    low = jnp.broadcast_to(entries & 127, (128, COLS)) == lax.broadcasted_iota(
        jnp.int32, (128, COLS), 0
    )
    day_v[...] = nt(
        jnp.where(high, 1.0, 0.0).astype(BF16), jnp.where(low, 1.0, 0.0).astype(BF16)
    )
    biases = [column(b0_v[...].reshape(1, HID))]
    biases += [column(bm_v[pl.ds(n, 1), :]) for n in range(2)]
    bias_out = jnp.concatenate([bo_v[...].reshape(1, OUT), jnp.zeros((1, LANES - OUT), F32)], axis=1)
    biases.append(column(bias_out))
    first_half = jnp.where(x < NX // 2, 1.0, 0.0)

    for lo in range(0, HID, 256):
        w0t_v[pl.ds(lo, 256), :] = nt(eye, w0_v[:, pl.ds(lo, 256)]).astype(BF16)

    def network(half, first, count):
        picked, days = [], []
        lanes = pl.ds(first * 128, count * 128)
        for i in (2 * half, 2 * half + 1):
            if first == 0 and i >= 2:
                loads[LOADED[i]].wait()
            part = jnp.dot(f_v[i], pick_v[:, lanes], preferred_element_type=F32)
            picked.append(part.astype(BF16))
            day = jnp.concatenate(
                [day_v[pl.ds(sectors[i] * NK + t, 1), :] for t in range(NK)], axis=1
            )
            day = jnp.broadcast_to(jnp.where(day > 0.5, 1.0, 0.0), (16, BLOCK)).astype(BF16)
            days.append(jnp.dot(day, pick_v[:, lanes], preferred_element_type=F32)[:1])
        h, day = jnp.concatenate(picked, axis=1), jnp.concatenate(days, axis=1)
        tiled = [jnp.concatenate([b] * (2 * count), axis=1) for b in biases]
        h = jnp.dot(w0t_v[...], h, preferred_element_type=F32)
        h = leaky(h + tiled[0]).astype(BF16)
        if half == 0 and first == 0:
            loads[7].wait()
        for layer in range(2):
            h = jnp.dot(wm_v[layer], h, preferred_element_type=F32)
            h = leaky(h + tiled[1 + layer]).astype(BF16)
        if half == 0 and first == 0:
            loads[8].wait()
        v = jnp.dot(wo_v[...], h, preferred_element_type=F32) + tiled[3]
        feat = lax.broadcasted_iota(jnp.int32, v.shape, 0)
        v = (jnp.where(feat == OUT, first_half, v) * day).astype(BF16)
        for n in range(2 * count):
            rows = nt(eye[:128, :128], v[:, n * 128 : (n + 1) * 128]).astype(BF16)
            sx[2 * half + n // count, first + n % count] = rows.reshape(NC, ROWS, LANES)

    def send(src, dst, send_sem, recv_sem, device):
        pltpu.make_async_remote_copy(
            src_ref=src,
            dst_ref=dst,
            send_sem=send_sem,
            recv_sem=recv_sem,
            device_id=device,
            device_id_type=MESH,
        ).start()

    def send_x(half, k):
        for i in (2 * half, 2 * half + 1):
            for r in range(NC) if i < 3 else (1,):
                dst = rx.at[half, k, 2 * (i % 2) + r]
                device = (cores[r], sectors[i])
                send(sx.at[i, k, r], dst, sx_sem.at[0], rx_sem.at[half, k], device)

    def wait_for(view, sem):
        pltpu.make_async_copy(view, view, sem).wait()

    def stage_x(half, k):
        slots = (0, 1, 2, 3) if half == 0 else (0, 1, 3)
        wait_for(rx.at[half, k, pl.ds(0, len(slots))], rx_sem.at[half, k])
        sums = []
        for r in range(NC):
            near = sx[3, k, 0] if half == 1 and r == 0 else rx[half, k, 2 + r]
            total = rx[half, k, r].astype(F32) + near.astype(F32)
            sums.append(total.reshape(NZ, NY, LANES))
        merged = jnp.concatenate(sums, axis=1).astype(BF16)
        zs[half, k] = merged
        for d in RING:
            dst = zr.at[half, k, d]
            send(zs.at[half, k, d], dst, zs_sem.at[0], zr_sem.at[half, k], (first_axis[d], x))
        zr[half, k, 0] = merged[0]

    def stage_z(half, k):
        wait_for(zr.at[half, k, pl.ds(1, NZ - 1)], zr_sem.at[half, k])
        rows = zr[half, k].reshape(128, LANES)
        turned = jnp.dot(turn, rows, preferred_element_type=F32)
        turned = turned.astype(BF16).reshape(NY, 16, LANES)
        ys[half, k] = turned
        for e in RING:
            dst = yr.at[half, k, e]
            send(ys.at[half, k, e], dst, ys_sem.at[0], yr_sem.at[half, k], (second_axis[e], x))
        yr[half, k, 0] = turned[0]

    def stage_y(half):
        near = lax.rem(x + 1 + half, 2)
        total = 0.0
        for k in range(NK):
            wait_for(yr.at[half, k, pl.ds(1, NY - 1)], yr_sem.at[half, k])
            rows = yr[half, k].reshape(128, LANES)
            feats = [
                nt(eye[:128, :128], rows[:, n : n + 128]).astype(BF16)
                for n in range(0, LANES, 128)
            ]
            total = total + jnp.dot(
                jnp.concatenate(feats, axis=0),
                place_v[pl.ds(k * 128, 128), :],
                preferred_element_type=F32,
            )
        t_v[half] = total.astype(BF16)
        pltpu.make_async_copy(t_v.at[half], out_ref.at[near], t_sem.at[half]).start()

    chunks = [(half, k) for half in range(2) for k in range(NK)]
    network(0, 0, 1)
    pl.semaphore_wait(barrier, len(peers))
    send_x(0, 0)
    network(0, 1, 2)
    send_x(0, 1)
    send_x(0, 2)
    network(1, 0, 1)
    send_x(1, 0)
    stage_x(0, 0)
    network(1, 1, 2)
    send_x(1, 1)
    send_x(1, 2)
    def placed_from(q):
        source = (q * 21846) >> 16
        d, e = (z - (source >> 4)) & 7, (y - (source >> 1)) & 7
        major, minor = e * (1 - c) + d * c, d * (1 - c) + e * c
        return (q - source * NK) * 128 + major * 16 + minor * 2 + ((source & 1) ^ c)

    place_v[...] = selector(BLOCK, BLOCK, placed_from)
    for t in range(1, len(chunks) + 1):
        if t < len(chunks):
            stage_x(*chunks[t])
        stage_z(*chunks[t - 1])
    for half in range(2):
        stage_y(half)

    wait_for(sx.at[pl.ds(0, 3)], sx_sem.at[0])
    wait_for(sx.at[3, :, 1], sx_sem.at[0])
    wait_for(zs.at[:, :, pl.ds(1, NZ - 1)], zs_sem.at[0])
    wait_for(ys.at[:, :, pl.ds(1, NY - 1)], ys_sem.at[0])
    for half in range(2):
        wait_for(t_v.at[half], t_sem.at[half])


def spread(t_ref, out_ref, t_v, o_v, t_sem, o_sem):
    pieces = [(n, pl.ds(b * 128, 128)) for n in range(2) for b in range(NK)]
    loads = [
        pltpu.make_async_copy(t_ref.at[n, :, lanes], t_v.at[m], t_sem.at[m])
        for m, (n, lanes) in enumerate(pieces)
    ]
    for load in loads:
        load.start()
    stores = []
    for m, (n, _) in enumerate(pieces):
        loads[m].wait()
        values = t_v[m].astype(F32)
        flag = values[OUT : OUT + 1]
        for far, weight in enumerate((flag, 1.0 - flag)):
            slot = m + 6 * far
            o_v[slot] = (values[:OUT] * weight).astype(BF16)
            store = pltpu.make_async_copy(
                o_v.at[slot], out_ref.at[:, pl.ds(slot * 128, 128)], o_sem.at[slot]
            )
            store.start()
            stores.append(store)
    for store in stores:
        store.wait()


def shards(
    features, daylit_list, daylit_count, in_weight, in_bias, mid_weight, mid_bias, out_weight, out_bias
):
    hbm = pl.BlockSpec(memory_space=pltpu.HBM)
    dma = pltpu.SemaphoreType.DMA
    halves = pl.pallas_call(
        kernel,
        out_shape=jax.ShapeDtypeStruct((2, LANES, BLOCK), BF16),
        in_specs=[pl.BlockSpec(memory_space=pltpu.SMEM)] + [hbm] * 8,
        out_specs=hbm,
        scratch_shapes=[
            pltpu.VMEM((COLS,), jnp.int32),
            pltpu.VMEM((4, FEAT, BLOCK), BF16),
            pltpu.VMEM((FEAT, HID), BF16),
            pltpu.VMEM((HID,), F32),
            pltpu.VMEM((2, HID, HID), BF16),
            pltpu.VMEM((2, HID), F32),
            pltpu.VMEM((LANES, HID), BF16),
            pltpu.VMEM((OUT,), F32),
            pltpu.VMEM((16, 128), F32),
            pltpu.VMEM((HID, FEAT), BF16),
            pltpu.VMEM((BLOCK, BLOCK), BF16),
            pltpu.VMEM((BLOCK, BLOCK), BF16),
            pltpu.VMEM((NX, NK, NC, ROWS, LANES), BF16),
            pltpu.VMEM((2, NK, 4, ROWS, LANES), BF16),
            pltpu.VMEM((2, NK, NZ, 16, LANES), BF16),
            pltpu.VMEM((2, NK, NZ, 16, LANES), BF16),
            pltpu.VMEM((2, NK, NY, 16, LANES), BF16),
            pltpu.VMEM((2, NK, NY, 16, LANES), BF16),
            pltpu.VMEM((2, LANES, BLOCK), BF16),
            dma((11,)),
            dma((1,)),
            dma((2, NK)),
            dma((1,)),
            dma((2, NK)),
            dma((1,)),
            dma((2, NK)),
            dma((2,)),
        ],
        compiler_params=pltpu.CompilerParams(
            collective_id=0, has_side_effects=True, vmem_limit_bytes=VMEM
        ),
    )(
        daylit_count,
        daylit_list,
        features,
        in_weight,
        in_bias,
        mid_weight,
        mid_bias,
        out_weight,
        out_bias,
    )
    return pl.pallas_call(
        spread,
        out_shape=jax.ShapeDtypeStruct((OUT, COLS), BF16),
        in_specs=[hbm],
        out_specs=hbm,
        scratch_shapes=[
            pltpu.VMEM((6, LANES, 128), BF16),
            pltpu.VMEM((12, OUT, 128), BF16),
            dma((6,)),
            dma((12,)),
        ],
        compiler_params=pltpu.CompilerParams(vmem_limit_bytes=VMEM),
    )(halves)


def solution(mesh):
    in_specs = (
        P(None, ("blk", "pair")),
        P(("blk", "pair")),
        P(("blk", "pair")),
        P(),
        P(),
        P(),
        P(),
        P(),
        P(),
    )
    out_specs = P(None, ("blk", "pair"))
    return jax.shard_map(shards, mesh=mesh, in_specs=in_specs, out_specs=out_specs, check_vma=False)
```
